32 devices in a mesh: dp: 16 (over z, y, x), mp: 2 (over core).
Axes of the slice: x: 2, y: 2, z: 4, core: 2. Of those that a mesh axis runs over, the one named last changes fastest.
Arguments:
- tokens: bfloat16 [32768, 512], P('dp'), may hold values from -6 to 6
- seq_starts: int32 [16, 16], P('dp'), may hold values from 0 to 2048, as said below
- seq_lengths: int32 [16, 16], P('dp'), may hold values from 0 to 2048, as said below
- attend_weight: bfloat16 [3, 512, 512], P(None, None, 'mp'), may hold values from -0.25 to 0.25
- attend_bias: float32 [2, 512], P(None, 'mp'), may hold values from -3 to 3
- output_weight: bfloat16 [512, 512], P('mp'), may hold values from -1 to 1
- output_bias: float32 [512], replicated, may hold values from -3 to 3
- first_gain: float32 [512], replicated, may hold values from 0.5 to 1.5
- first_shift: float32 [512], replicated, may hold values from -3 to 3
- expand_weight: bfloat16 [512, 2048], P(None, 'mp'), may hold values from -0.25 to 0.25
- expand_bias: float32 [2048], P('mp'), may hold values from -3 to 3
- reduce_weight: bfloat16 [2048, 512], P('mp'), may hold values from -0.25 to 0.25
- reduce_bias: float32 [512], replicated, may hold values from -3 to 3
- second_gain: float32 [512], replicated, may hold values from 0.5 to 1.5
- second_shift: float32 [512], replicated, may hold values from -3 to 3
- cotangent: bfloat16 [32768, 512], P('dp'), may hold values from -6 to 6
Outputs:
- layer_out: bfloat16 [32768, 512], P('dp')
- grad_tokens: bfloat16 [32768, 512], P('dp')
- grad_attend: float32 [3, 512, 512], P(None, None, 'mp')
- grad_attbias: float32 [2, 512], P(None, 'mp')
- grad_output: float32 [512, 512], P('mp')
- grad_outbias: float32 [512], replicated
- grad_firstgain: float32 [512], replicated
- grad_firstshift: float32 [512], replicated
- grad_expand: float32 [512, 2048], P(None, 'mp')
- grad_expbias: float32 [2048], P('mp')
- grad_reduce: float32 [2048, 512], P('mp')
- grad_redbias: float32 [512], replicated
- grad_secondgain: float32 [512], replicated
- grad_secondshift: float32 [512], replicated
The draws below stay inside these ranges and needn't reach their ends.
Inputs may be any that keep to these rules, and one draw needn't show every extreme that they name: `seq_starts`: in each device row, used slots come first, sequences stand in order, each ends at or before the next one's start and within 2048; an unused slot has length 0 and start 2048; some device holds a single sequence of 2048 tokens. `seq_lengths`: A used slot has 21 or more tokens, the first 20 being memory tokens; an unused slot has 0; every device holds at least one sequence.
All inputs are finite; a program needn't handle non-finite values.
Results may differ from the reference program's by a relative error of at most 0.014.
The reference program's roundings to bfloat16 on the way count: a program that leaves them out, or rounds other values in their place, can miss the bound.
Values sent between devices are 32-bit elements; how exact they have to be, the bound alone decides.
No kernel may reach another device: no remote copies, remote signals or barrier semaphores. Data moves between devices by JAX's collectives and lax.ppermute only.
A program may use at most 128 MiB of HBM per device.

```python
import jax
import jax.numpy as jnp
from jax import lax

D = 512
HEADS = 8
HD = 64
FF = 2048
MEM = 20
TOK_DEV = 2048
SEQ_DEV = 16
TOKENS = 32768
N_DP = 16


def packing(key):
    key_long, key_pick, key_size, key_space = jax.random.split(key, 4)
    long_flag = jax.random.randint(key_long, (N_DP,), 0, 8) == 0
    chosen = jax.random.randint(key_pick, (), 0, N_DP)
    long_flag = long_flag | (jnp.arange(N_DP) == chosen)
    short_most = max(MEM + 1, TOK_DEV // 4)
    sizes_drawn = jax.random.randint(key_size, (N_DP, SEQ_DEV), MEM + 1, short_most + 1)
    spaces = jax.random.randint(key_space, (N_DP, SEQ_DEV), 0, 4)
    ends = jnp.cumsum(sizes_drawn + spaces, axis=1) - spaces
    starts = ends - sizes_drawn
    fits = ends <= TOK_DEV
    lengths = jnp.where(fits, sizes_drawn, 0)
    starts = jnp.where(fits, starts, TOK_DEV)
    first_slot = (jnp.arange(SEQ_DEV) == 0)[None, :]
    lengths = jnp.where(long_flag[:, None], jnp.where(first_slot, TOK_DEV, 0), lengths)
    starts = jnp.where(long_flag[:, None], jnp.where(first_slot, 0, TOK_DEV), starts)
    return (starts.astype(jnp.int32), lengths.astype(jnp.int32))


def draw_seq_starts(key, part):
    starts, lengths = packing(key)
    return starts


def draw_seq_lengths(key, part):
    starts, lengths = packing(key)
    return lengths


def block_scale(own_key, shape, cuts, low, high):
    loudness, own = 1.0, jax.random.fold_in(own_key, 6)
    for axis_at, parts in cuts:
        draws = jnp.exp(jax.random.uniform(jax.random.fold_in(own, axis_at), (parts,), jnp.float32, low / len(cuts), high / len(cuts)))
        loudness = loudness * jnp.repeat(draws, shape[axis_at] // parts).reshape([-1 if axis == axis_at else 1 for axis in range(len(shape))])
    return loudness


def bell_draw(rng, shape, scale, limit, shards=(), kind=jnp.bfloat16):
    loudness = block_scale(rng, shape, shards, -0.22, 0.18) if shards else 1.0
    entries = jax.random.normal(rng, shape, jnp.float32) * scale * loudness
    return jnp.minimum(jnp.maximum(entries, -limit), limit).astype(kind)


def setup_inputs(seed: int = 0) -> dict:
    arg_keys = jax.random.split(jax.random.key(seed), 17)
    tokens = bell_draw(arg_keys[0], (TOKENS, D), 1.0, 6.0, ((0, 16),))
    seq_starts = draw_seq_starts(jax.random.fold_in(arg_keys[16], 71), 0)
    seq_lengths = draw_seq_lengths(jax.random.fold_in(arg_keys[16], 71), 0)
    attend_weight = bell_draw(arg_keys[3], (3, D, D), D ** -0.5, 0.25, ((2, 2),))
    attend_bias = bell_draw(arg_keys[4], (2, D), 0.5, 3.0, ((1, 2),), jnp.float32)
    output_weight = bell_draw(arg_keys[5], (D, D), (D // 16) ** -0.5, 1.0, ((0, 2),))
    output_bias = bell_draw(arg_keys[6], (D,), 0.3, 3.0, (), jnp.float32)
    first_gain = jnp.clip(1.0 + 0.1 * jax.random.normal(arg_keys[7], (D,), jnp.float32), 0.5, 1.5)
    first_shift = bell_draw(arg_keys[8], (D,), 0.3, 3.0, (), jnp.float32)
    expand_weight = bell_draw(arg_keys[9], (D, FF), D ** -0.5, 0.25, ((1, 2),))
    expand_bias = bell_draw(arg_keys[10], (FF,), 0.5, 3.0, ((0, 2),), jnp.float32)
    reduce_weight = bell_draw(arg_keys[11], (FF, D), (FF // 4) ** -0.5, 0.25, ((0, 2),))
    reduce_bias = bell_draw(arg_keys[12], (D,), 0.3, 3.0, (), jnp.float32)
    second_gain = jnp.clip(1.0 + 0.1 * jax.random.normal(arg_keys[13], (D,), jnp.float32), 0.5, 1.5)
    second_shift = bell_draw(arg_keys[14], (D,), 0.3, 3.0, (), jnp.float32)
    cotangent = bell_draw(arg_keys[15], (TOKENS, D), 1.0, 6.0, ((0, 16),))
    return {"tokens": tokens, "seq_starts": seq_starts, "seq_lengths": seq_lengths, "attend_weight": attend_weight, "attend_bias": attend_bias, "output_weight": output_weight, "output_bias": output_bias, "first_gain": first_gain, "first_shift": first_shift, "expand_weight": expand_weight, "expand_bias": expand_bias, "reduce_weight": reduce_weight, "reduce_bias": reduce_bias, "second_gain": second_gain, "second_shift": second_shift, "cotangent": cotangent}


EPS = 1e-05
NEG = -1e+30
HIGHEST = lax.Precision.HIGHEST

@jax.custom_vjp
def low(v):
    return lax.optimization_barrier(v.astype(jnp.bfloat16)).astype(jnp.float32)

@jax.custom_vjp
def low_back(v):
    return v

def low_keep(v):
    return (low(v), None)

def low_pass(kept, grad):
    return (grad,)

def back_keep(v):
    return (v, None)

def back_low(kept, grad):
    return (low(grad),)
low.defvjp(low_keep, low_pass)
low_back.defvjp(back_keep, back_low)

def segment_ids(starts, lengths, count):
    places = jnp.arange(count, dtype=jnp.int32)[:, None]
    inside = (places >= starts[None, :]) & (places < (starts + lengths)[None, :])
    labels = jnp.arange(1, starts.shape[0] + 1, dtype=jnp.int32)[None, :]
    return lax.optimization_barrier(jnp.sum(jnp.where(inside, labels, 0), axis=1)).astype(jnp.int32)

def layer_norm(values, gain, shift):
    center = values - lax.optimization_barrier(jnp.mean(values, axis=-1, keepdims=True))
    spread = lax.optimization_barrier(jnp.mean(center * center, axis=-1, keepdims=True))
    return center * lax.rsqrt(spread + EPS) * gain + shift

def attend_rows(query_rows, key_rows, value_rows, segment_rows, segment_keys):
    scores = jnp.einsum('qhd,khd->hqk', query_rows, key_rows, precision=HIGHEST) * HD ** (-0.5)
    scores = low_back(scores)
    allowed = (segment_rows[:, None] == segment_keys[None, :])[None]
    scores = jnp.where(allowed, scores, NEG)
    peak = lax.optimization_barrier(jnp.max(scores, axis=-1, keepdims=True))
    total = lax.optimization_barrier(jnp.sum(jnp.exp(scores - peak), axis=-1, keepdims=True))
    probs = low(jnp.exp(scores - (peak + jnp.log(total))))
    return jnp.einsum('hqk,khd->qhd', probs, value_rows, precision=HIGHEST)

def device_layer(rows, segment, params):
    attend_weight, attend_bias, output_weight, output_bias, first_gain, first_shift, expand_weight, expand_bias, reduce_weight, reduce_bias, second_gain, second_shift = params
    count = rows.shape[0]
    block_rows = min(512, count)
    blocks = count // block_rows
    bias_full = jnp.stack([attend_bias[0], jnp.zeros_like(attend_bias[0]), attend_bias[1]])
    mixed = jnp.einsum('td,cde->cte', rows, attend_weight, precision=HIGHEST) + bias_full[:, None, :]
    mixed = low(low_back(mixed))
    query_all = mixed[0].reshape(count, HEADS, HD)
    key_all = mixed[1].reshape(count, HEADS, HD)
    value_all = mixed[2].reshape(count, HEADS, HD)
    checked = jax.checkpoint(attend_rows)
    attended = lax.map(lambda pair: checked(pair[0], key_all, value_all, pair[1], segment), (query_all.reshape(blocks, block_rows, HEADS, HD), segment.reshape(blocks, block_rows)))
    attended = low(low_back(attended.reshape(count, D)))
    branch = low_back(jnp.dot(attended, output_weight, precision=HIGHEST) + output_bias)
    normed = layer_norm(rows + branch, first_gain, first_shift)
    hidden = low_back(jnp.dot(low(normed), expand_weight, precision=HIGHEST) + expand_bias)
    active = low(jax.nn.gelu(hidden, approximate=False))
    result = low_back(jnp.dot(active, reduce_weight, precision=HIGHEST) + reduce_bias)
    final = layer_norm(normed + result, second_gain, second_shift)
    return final * (segment > 0).astype(jnp.float32)[:, None]

def reference(tokens, seq_starts, seq_lengths, attend_weight, attend_bias, output_weight, output_bias, first_gain, first_shift, expand_weight, expand_bias, reduce_weight, reduce_bias, second_gain, second_shift, cotangent):
    segments = jax.vmap(lambda starts, lengths: segment_ids(starts, lengths, TOK_DEV))(seq_starts, seq_lengths)
    params = tuple((item.astype(jnp.float32) for item in (attend_weight, attend_bias, output_weight, output_bias, first_gain, first_shift, expand_weight, expand_bias, reduce_weight, reduce_bias, second_gain, second_shift)))
    rows_all = tokens.astype(jnp.float32).reshape(N_DP, TOK_DEV, D)

    def forward(rows_all, params):

        def advance(carry, item):
            return (carry, device_layer(item[0], item[1], params))
        unused, outputs = lax.scan(advance, jnp.zeros((), jnp.float32), (rows_all, segments))
        return outputs
    outputs, pullback = jax.vjp(forward, rows_all, params)
    grad_rows, grads = pullback(cotangent.astype(jnp.float32).reshape(N_DP, TOK_DEV, D))
    return (outputs.reshape(TOKENS, D).astype(jnp.bfloat16), grad_rows.reshape(TOKENS, D).astype(jnp.bfloat16), grads[0], grads[1], grads[2], grads[3], grads[4], grads[5], grads[6], grads[7], grads[8], grads[9], grads[10], grads[11])
```

```python
import functools
import math

import jax
import jax.numpy as jnp
from jax import lax
from jax.experimental import pallas as pl
from jax.experimental.pallas import tpu as pltpu
from jax.sharding import PartitionSpec as P

HD = 64
EPS = 1e-05
FAR = 1e30
f32 = jnp.float32
bf16 = jnp.bfloat16
QB = 256
LIMIT = 60 * 2**20


def dot(a, b, ca=1, cb=0):
    return lax.dot_general(a, b, (((ca,), (cb,)), ((), ())), preferred_element_type=f32)


def vmem():
    return pl.BlockSpec(memory_space=pltpu.VMEM)


def shape(dims, kind=f32):
    return jax.ShapeDtypeStruct(dims, kind)


def call(body, outs, **extra):
    return pl.pallas_call(
        body,
        out_shape=outs,
        compiler_params=pltpu.CompilerParams(vmem_limit_bytes=LIMIT),
        **extra,
    )


def widen_kernel(*refs):
    count = len(refs) // 2
    for src, dst in zip(refs[:count], refs[count:]):
        dst[...] = src[...].astype(f32)


def widen(*arrays):
    return call(widen_kernel, [shape(a.shape) for a in arrays])(*arrays)


def split3(v):
    high = v.astype(bf16)
    rest = v - high.astype(f32)
    mid = rest.astype(bf16)
    low = (rest - mid.astype(f32)).astype(bf16)
    return high, mid, low


def query_rows(start_col, end_col, base, count):
    slots = start_col.shape[0]
    place = lax.broadcasted_iota(jnp.int32, (slots, count), 1) + base
    inside = jnp.where((place >= start_col) & (place < end_col), 1.0, 0.0)
    alone = 1.0 - jnp.sum(inside, axis=0, keepdims=True)
    return jnp.concatenate([inside, alone], axis=0) * -FAR


def key_columns(start_row, end_row, base, count, slots):
    place = lax.broadcasted_iota(jnp.int32, (count, 128), 0) + base
    lane = lax.broadcasted_iota(jnp.int32, (count, 128), 1)
    inside = jnp.where((place >= start_row) & (place < end_row), 1.0, 0.0)
    used = jnp.sum(inside, axis=1, keepdims=True)
    ones = (lane > slots) & (lane < slots + 4)
    return jnp.where(
        lane < slots, 1.0 - inside, jnp.where(lane == slots, used, jnp.where(ones, 1.0, 0.0))
    )


def forward_kernel(
    me, tok_other, tok_own, weight, bias_col, start_col, end_col, start_row, end_row,
    att_other, att_own, log_out, qt_out, kaug_out, tokens, qhl, vt, segq,
):
    half = tok_other.shape[0]
    count = 2 * half
    heads = weight.shape[2] // HD
    width = heads * HD
    slots = start_col.shape[0]
    tokens[0:half] = tok_other[...]
    tokens[half:count] = tok_own[...]
    bases = ((1 - me[0]) * half, me[0] * half)
    for part in range(2):
        segq[0 : slots + 1, part * half : (part + 1) * half] = query_rows(
            start_col[...], end_col[...], bases[part], half
        ).astype(bf16)
    segq[slots + 1 :, :] = jnp.zeros((128 - slots - 1, count), bf16)

    step = 512

    def project(i, carry):
        at = pl.multiple_of(i * step, step)
        rows = tokens[pl.ds(at, step), :]
        query = (dot(weight[0], rows, 0, 1) + bias_col[0]).astype(bf16)
        qt_out[:, pl.ds(at, step)] = query
        scaled = query.astype(f32) * (math.log2(math.e) / math.sqrt(HD))
        high = scaled.astype(bf16)
        low = (scaled - high.astype(f32)).astype(bf16)
        value = (dot(weight[2], rows, 0, 1) + bias_col[1]).astype(bf16)
        key = dot(rows, weight[1]).astype(bf16).astype(f32)
        base = jnp.where(at < half, bases[0], bases[1] - half) + at
        common = key_columns(start_row[...], end_row[...], base, step, slots).astype(bf16)
        lane = lax.broadcasted_iota(jnp.int32, (step, 128), 1)
        for h in range(heads):
            qhl[h * 128 : h * 128 + HD, pl.ds(at, step)] = high[h * HD : (h + 1) * HD]
            qhl[h * 128 + HD : (h + 1) * 128, pl.ds(at, step)] = low[h * HD : (h + 1) * HD]
            vt[h * 80 : h * 80 + HD, pl.ds(at, step)] = value[h * HD : (h + 1) * HD]
            vt[h * 80 + HD : (h + 1) * 80, pl.ds(at, step)] = jnp.ones((16, step), bf16)
            if h % 2 == 0:
                pair = key[:, h * HD : h * HD + 128]
                turned = pltpu.roll(pair, HD, 1)
                twice = (jnp.where(lane < HD, pair, turned), jnp.where(lane < HD, turned, pair))
            kaug_out[h, pl.ds(at, step), 0:128] = twice[h % 2].astype(bf16)
            kaug_out[h, pl.ds(at, step), 128:256] = common
        return carry

    lax.fori_loop(0, count // step, project, 0)

    def block(at, out, place):
        seg = segq[:, pl.ds(at, QB)]
        for h in range(heads):
            query = jnp.concatenate([qhl[h * 128 : (h + 1) * 128, pl.ds(at, QB)], seg], axis=0)
            scores = dot(kaug_out[h], query)
            peak = jnp.max(scores, axis=0, keepdims=True)
            probs = jnp.exp2(scores - peak).astype(bf16)
            summed = dot(vt[h * 80 : (h + 1) * 80, :], probs)
            total = summed[HD : HD + 1]
            out[h * HD : (h + 1) * HD, pl.ds(place, QB)] = summed[:HD] / total
            log_out[h : h + 1, pl.ds(at, QB)] = peak + jnp.log2(total)

    for part, out in enumerate((att_other, att_own)):

        def body(i, carry, part=part, out=out):
            place = pl.multiple_of(i * QB, QB)
            block(place + part * half, out, place)
            return carry

        lax.fori_loop(0, half // QB, body, 0)


def attend_forward(me, tokens, weight, bias_col, start_col, end_col, start_row, end_row):
    count, width = tokens.shape[0], weight.shape[2]
    half, heads, depth = count // 2, width // HD, tokens.shape[1]
    whole = lambda a: pl.BlockSpec(a.shape, lambda i, me, n=a.ndim: (0,) * n)
    outs = [
        shape((width, half)),
        shape((width, half)),
        shape((8, count)),
        shape((width, count), bf16),
        shape((heads, count, 256), bf16),
    ]
    return call(
        forward_kernel,
        outs,
        grid_spec=pltpu.PrefetchScalarGridSpec(
            num_scalar_prefetch=1,
            grid=(1,),
            in_specs=[
                pl.BlockSpec((half, depth), lambda i, me: (1 - me[0], 0)),
                pl.BlockSpec((half, depth), lambda i, me: (me[0], 0)),
                *[whole(a) for a in (weight, bias_col, start_col, end_col, start_row, end_row)],
            ],
            out_specs=[whole(o) for o in outs],
            scratch_shapes=[
                pltpu.VMEM((count, depth), bf16),
                pltpu.VMEM((heads * 128, count), bf16),
                pltpu.VMEM((heads * 80, count), bf16),
                pltpu.VMEM((128, count), bf16),
            ],
        ),
    )(me, tokens, tokens, weight, bias_col, start_col, end_col, start_row, end_row)


def norm(v):
    center = v - jnp.mean(v, axis=-1, keepdims=True)
    rstd = lax.rsqrt(jnp.mean(center * center, axis=-1, keepdims=True) + EPS)
    return center * rstd, rstd


def norm_back(grad, n, rstd):
    first = jnp.mean(grad, axis=-1, keepdims=True)
    second = jnp.mean(grad * n, axis=-1, keepdims=True)
    return rstd * (grad - first - n * second)


def normal_parts(h):
    size = jnp.abs(h)
    t = 1.0 / (1.0 + (0.3275911 * math.sqrt(0.5)) * size)
    bell = jnp.exp2(h * h * (-0.5 * math.log2(math.e)))
    poly = t * (
        0.127414796 + t * (-0.142248368 + t * (0.7107068705 + t * (-0.7265760135 + t * 0.5307027145)))
    )
    tail = poly * bell
    below = jnp.where(h < 0, tail, 1.0 - tail)
    return below, bell * (1.0 / math.sqrt(2.0 * math.pi))


def middle_kernel(
    me, att_own, att_rcv, wo_own, wo_rcv, we_own, we_rcv, wr_own, wr_rcv, eb_own, eb_rcv,
    tok, cot, rows, start_row, end_row,
    layer_out, resid_out, ga_own, ga_other, act_out, gh_out, nl_out, gr_out, gb_out, att_out, small, eb_out,
    wo, we, wr,
):
    i = pl.program_id(0)
    units = we_own.shape[1]
    width = wo_own.shape[0]
    count = tok.shape[0]

    @pl.when(i == 0)
    def _():
        wo[0:width] = wo_own[...]
        wo[width:] = wo_rcv[...].astype(bf16)
        we[:, 0:units] = we_own[...]
        we[:, units:] = we_rcv[...].astype(bf16)
        wr[0:units] = wr_own[...]
        wr[units:] = wr_rcv[...].astype(bf16)
        small[...] = jnp.zeros_like(small)
        eb_out[...] = jnp.zeros_like(eb_out)

    output_bias, gain1, shift1, reduce_bias, gain2, shift2 = (rows[j : j + 1] for j in range(6))
    base = (me[0] * pl.num_programs(0) + i) * count
    place = lax.broadcasted_iota(jnp.int32, (count, 128), 0) + base
    inside = jnp.where((place >= start_row[...]) & (place < end_row[...]), 1.0, 0.0)
    valid = jnp.sum(inside, axis=1, keepdims=True)

    att = jnp.concatenate([att_own[...], att_rcv[...]], axis=0).astype(bf16)
    att_out[...] = att
    resid_one = tok[...].astype(f32) + (dot(att, wo[...], 0, 0) + output_bias)
    n1, rstd1 = norm(resid_one)
    normed = n1 * gain1 + shift1
    normed_low = normed.astype(bf16)
    nl_out[...] = normed_low
    bias = jnp.concatenate([eb_own[...], eb_rcv[...]], axis=1)
    hidden = dot(normed_low, we[...]) + bias
    below, density = normal_parts(hidden)
    active = (hidden * below).astype(bf16)
    slope = below + hidden * density
    act_out[...] = active
    resid_two = normed + (dot(active, wr[...]) + reduce_bias)
    n2, rstd2 = norm(resid_two)
    layer_out[...] = ((n2 * gain2 + shift2) * valid).astype(bf16).astype(f32)
    grad = cot[...].astype(f32) * valid
    column = lambda v: jnp.sum(v, axis=0, keepdims=True)
    small[0:1] += column(grad * n2)
    small[1:2] += column(grad)
    grad_two = norm_back(grad * gain2, n2, rstd2)
    grad_result = grad_two.astype(bf16)
    gr_out[...] = grad_result
    small[2:3] += column(grad_result.astype(f32))
    grad_hidden = (dot(grad_result, wr[...], 1, 1) * slope).astype(bf16)
    gh_out[...] = grad_hidden
    eb_out[0:1] += column(grad_hidden.astype(f32))
    grad_normed = grad_two + dot(grad_hidden, we[...], 1, 1)
    small[3:4] += column(grad_normed * n1)
    small[4:5] += column(grad_normed)
    grad_one = norm_back(grad_normed * gain1, n1, rstd1)
    resid_out[...] = grad_one
    grad_branch = grad_one.astype(bf16)
    gb_out[...] = grad_branch
    small[5:6] += column(grad_branch.astype(f32))
    grad_att = dot(wo[...], grad_branch, 1, 1).astype(bf16).astype(f32)
    ga_own[...] = grad_att[0:width]
    ga_other[...] = grad_att[width:]


def middle(me, att_own, att_rcv, wo_own, wo_rcv, we_own, we_rcv, wr_own, wr_rcv, eb_own, eb_rcv, tokens, cotangent, rows, start_row, end_row):
    half, depth = tokens.shape[0] // 2, tokens.shape[1]
    width, units = wo_own.shape[0], we_own.shape[1]
    blk = 256
    steps = half // blk
    whole = lambda a: pl.BlockSpec(a.shape, lambda i, me, n=a.ndim: (0,) * n)
    by_row = lambda n: pl.BlockSpec((blk, n), lambda i, me: (i, 0))
    by_col = lambda n: pl.BlockSpec((n, blk), lambda i, me: (0, i))
    mine = pl.BlockSpec((blk, depth), lambda i, me: (me[0] * steps + i, 0))
    outs = [
        (shape((half, depth)), by_row(depth)),
        (shape((half, depth)), by_row(depth)),
        (shape((width, half)), by_col(width)),
        (shape((width, half)), by_col(width)),
        (shape((half, 2 * units), bf16), by_row(2 * units)),
        (shape((half, 2 * units), bf16), by_row(2 * units)),
        (shape((half, depth), bf16), by_row(depth)),
        (shape((half, depth), bf16), by_row(depth)),
        (shape((half, depth), bf16), by_row(depth)),
        (shape((2 * width, half), bf16), by_col(2 * width)),
        (shape((8, depth)), None),
        (shape((8, 2 * units)), None),
    ]
    args = (wo_own, wo_rcv, we_own, we_rcv, wr_own, wr_rcv, eb_own, eb_rcv)
    return call(
        middle_kernel,
        [o for o, _ in outs],
        grid_spec=pltpu.PrefetchScalarGridSpec(
            num_scalar_prefetch=1,
            grid=(steps,),
            in_specs=[
                by_col(width),
                by_col(width),
                *[whole(a) for a in args],
                mine,
                mine,
                *[whole(a) for a in (rows, start_row, end_row)],
            ],
            out_specs=[s or whole(o) for o, s in outs],
            scratch_shapes=[
                pltpu.VMEM((2 * width, depth), bf16),
                pltpu.VMEM((depth, 2 * units), bf16),
                pltpu.VMEM((2 * units, depth), bf16),
            ],
        ),
    )(me, att_own, att_rcv, *args, tokens, cotangent, rows, start_row, end_row)


def reduce_grad_kernel(act, gr, out):
    out[...] = dot(act[...], gr[...], 0, 0)


def expand_grad_kernel(nl, gh, out):
    out[...] = dot(nl[...], gh[...], 0, 0)


def reduce_grad(active, grad_result, which):
    half, units, depth = active.shape[0], active.shape[1] // 2, grad_result.shape[1]
    steps = 4
    blk = units // steps
    return call(
        reduce_grad_kernel,
        shape((units, depth)),
        grid=(steps,),
        in_specs=[
            pl.BlockSpec((half, blk), lambda i: (0, which * steps + i)),
            pl.BlockSpec((half, depth), lambda i: (0, 0)),
        ],
        out_specs=pl.BlockSpec((blk, depth), lambda i: (i, 0)),
    )(active, grad_result)


def expand_grad(normed_low, grad_hidden, which):
    half, units, depth = grad_hidden.shape[0], grad_hidden.shape[1] // 2, normed_low.shape[1]
    steps = 4
    blk = units // steps
    return call(
        expand_grad_kernel,
        shape((depth, units)),
        grid=(steps,),
        in_specs=[
            pl.BlockSpec((half, depth), lambda i: (0, 0)),
            pl.BlockSpec((half, blk), lambda i: (0, which * steps + i)),
        ],
        out_specs=pl.BlockSpec((depth, blk), lambda i: (0, i)),
    )(normed_low, grad_hidden)


def output_grad_kernel(att, gb, own, other):
    width = own.shape[0]
    both = dot(att[...], gb[...])
    own[...] = both[:width]
    other[...] = both[width:]


def output_grad(att, grad_branch):
    width, depth = att.shape[0] // 2, grad_branch.shape[1]
    return call(output_grad_kernel, [shape((width, depth)), shape((width, depth))])(att, grad_branch)


def backward_kernel(
    me, tok_other, tok_own, weight, bias_row, start_col, end_col, qt, kaug, logs, att_other, att_own,
    ga_other, ga_own, dq, dk, dv, kt, vaug, segq, dkt, dvt,
):
    head = pl.program_id(0)
    half = tok_other.shape[0]
    count = 2 * half
    heads = weight.shape[2] // HD
    slots = start_col.shape[0]
    scale = HD**-0.5

    @pl.when(head == 0)
    def _():
        bases = ((1 - me[0]) * half, me[0] * half)
        for part, tok in enumerate((tok_other, tok_own)):
            segq[0 : slots + 1, part * half : (part + 1) * half] = query_rows(
                start_col[...], end_col[...], bases[part], half
            ).astype(bf16)
            kt[:, part * half : (part + 1) * half] = dot(weight[1], tok[...], 0, 1).astype(bf16)
            value = (dot(tok[...], weight[2]) + bias_row[...]).astype(bf16).astype(f32)
            lane = lax.broadcasted_iota(jnp.int32, (half, 128), 1)
            ones = jnp.where(lane < HD + 3, 1.0, 0.0)
            for h in range(heads):
                pair = value[:, h // 2 * 128 : h // 2 * 128 + 128]
                if h % 2:
                    pair = pltpu.roll(pair, HD, 1)
                vaug[h, part * half : (part + 1) * half, :] = jnp.where(
                    lane < HD, pair, ones
                ).astype(bf16)

    dkt[...] = jnp.zeros_like(dkt)
    dvt[...] = jnp.zeros_like(dvt)
    zeros_q = jnp.zeros((128 - slots - 4, QB), bf16)
    zeros_v = jnp.zeros((128 - HD - 3, QB), bf16)

    for part, (att, ga) in enumerate(((att_other, ga_other), (att_own, ga_own))):

        def body(i, carry, part=part, att=att, ga=ga):
            place = pl.multiple_of(i * QB, QB)
            at = place + part * half
            grad = ga[:, pl.ds(place, QB)]
            inner = -jnp.sum(grad * att[:, pl.ds(place, QB)], axis=0, keepdims=True)
            grad_low = grad.astype(bf16)
            upper = jnp.concatenate([grad_low, *split3(inner), zeros_v], axis=0)
            query = qt[:, pl.ds(at, QB)]
            scaled = query.astype(f32) * (math.log2(math.e) / math.sqrt(HD))
            high = scaled.astype(bf16)
            low = (scaled - high.astype(f32)).astype(bf16)
            logs_q = logs[pl.ds(head, 1), pl.ds(at, QB)]
            seg = segq[0 : slots + 1, pl.ds(at, QB)]
            left = jnp.concatenate([high, low, seg, *split3(-logs_q), zeros_q], axis=0)
            probs = jnp.exp2(dot(kaug[0], left))
            grad_probs = dot(vaug[head], upper)
            grad_scores = (probs * grad_probs).astype(bf16)
            dvt[...] += dot(grad_low, probs.astype(bf16), 1, 1)
            dkt[...] += dot(query, grad_scores, 1, 1)
            dq[:, pl.ds(at, QB)] = (
                dot(kt[pl.ds(pl.multiple_of(head * HD, HD), HD), :], grad_scores) * scale
            ).astype(bf16)
            return carry

        lax.fori_loop(0, half // QB, body, 0)
    dk[...] = (dkt[...] * scale).astype(bf16)
    dv[...] = dvt[...].astype(bf16)


def attend_backward(me, tokens, weight, bias_row, start_col, end_col, qt, kaug, logs, att_other, att_own, ga_other, ga_own):
    count, width = tokens.shape[0], weight.shape[2]
    half, heads, depth = count // 2, width // HD, tokens.shape[1]
    slots = start_col.shape[0]
    whole = lambda a: pl.BlockSpec(a.shape, lambda i, me, n=a.ndim: (0,) * n)
    by_head = lambda n: pl.BlockSpec((HD, n), lambda i, me: (i, 0))
    outs = [shape((width, count), bf16)] * 3
    return call(
        backward_kernel,
        outs,
        grid_spec=pltpu.PrefetchScalarGridSpec(
            num_scalar_prefetch=1,
            grid=(heads,),
            in_specs=[
                pl.BlockSpec((half, depth), lambda i, me: (1 - me[0], 0)),
                pl.BlockSpec((half, depth), lambda i, me: (me[0], 0)),
                *[whole(a) for a in (weight, bias_row, start_col, end_col)],
                by_head(count),
                pl.BlockSpec((1, count, 256), lambda i, me: (i, 0, 0)),
                whole(logs),
                *[by_head(half)] * 4,
            ],
            out_specs=[by_head(count)] * 3,
            scratch_shapes=[
                pltpu.VMEM((width, count), bf16),
                pltpu.VMEM((heads, count, 128), bf16),
                pltpu.VMEM((slots + 1, count), bf16),
                pltpu.VMEM((HD, count), f32),
                pltpu.VMEM((HD, count), f32),
            ],
        ),
    )(me, tokens, tokens, weight, bias_row, start_col, end_col, qt, kaug, logs, att_other, att_own, ga_other, ga_own)


def project_back_kernel(me, tok_other, tok_own, weight, dq, dk, dv, grad, bias, rows_other, rows_own):
    half = tok_other.shape[0]
    for c, part in enumerate((dq, dk, dv)):
        turned = dot(part[:, 0:half], tok_other[...]) + dot(part[:, half:], tok_own[...])
        grad[c] = turned.T
        if c != 1:
            bias[:, c // 2 : c // 2 + 1] = jnp.sum(part[...].astype(f32), axis=1, keepdims=True)
    for at, out in ((0, rows_other), (half, rows_own)):
        out[...] = sum(
            dot(part[:, at : at + half], weight[c], 0, 1) for c, part in enumerate((dq, dk, dv))
        )


def project_back(me, tokens, weight, dq, dk, dv):
    half, depth, width = tokens.shape[0] // 2, tokens.shape[1], weight.shape[2]
    whole = lambda a: pl.BlockSpec(a.shape, lambda i, me, n=a.ndim: (0,) * n)
    outs = [shape((3, depth, width)), shape((width, 2)), shape((half, depth)), shape((half, depth))]
    return call(
        project_back_kernel,
        outs,
        grid_spec=pltpu.PrefetchScalarGridSpec(
            num_scalar_prefetch=1,
            grid=(1,),
            in_specs=[
                pl.BlockSpec((half, depth), lambda i, me: (1 - me[0], 0)),
                pl.BlockSpec((half, depth), lambda i, me: (me[0], 0)),
                *[whole(a) for a in (weight, dq, dk, dv)],
            ],
            out_specs=[whole(o) for o in outs],
        ),
    )(me, tokens, tokens, weight, dq, dk, dv)


def add_rows_kernel(a, b, c, out):
    out[...] = (a[...] + b[...] + c[...]).astype(bf16).astype(f32)


def add_rows(a, b, c):
    rows, depth = a.shape
    blk = pl.BlockSpec((rows // 4, depth), lambda i: (i, 0))
    return call(add_rows_kernel, shape(a.shape), grid=(4,), in_specs=[blk] * 3, out_specs=blk)(a, b, c)


def join_kernel(me, own, other, out):
    mine = pl.program_id(0) == me[0]

    @pl.when(mine)
    def _():
        out[...] = own[...].astype(bf16)

    @pl.when(jnp.logical_not(mine))
    def _():
        out[...] = other[...].astype(bf16)


def join(me, own, other):
    half, depth = own.shape
    whole = pl.BlockSpec((half, depth), lambda i, me: (0, 0))
    return call(
        join_kernel,
        shape((2 * half, depth), bf16),
        grid_spec=pltpu.PrefetchScalarGridSpec(
            num_scalar_prefetch=1,
            grid=(2,),
            in_specs=[whole, whole],
            out_specs=pl.BlockSpec((half, depth), lambda i, me: (i, 0)),
        ),
    )(me, own, other)


def swap(v):
    return lax.ppermute(v, "mp", [(0, 1), (1, 0)])


def local(
    tokens, seq_starts, seq_lengths, attend_weight, attend_bias, output_weight, output_bias, first_gain, first_shift,
    expand_weight, expand_bias, reduce_weight, reduce_bias, second_gain, second_shift, cotangent,
):
    slots = seq_starts.shape[1]
    me = lax.axis_index("mp").astype(jnp.int32)[None]
    ends = seq_starts + seq_lengths
    start_col, end_col = seq_starts.reshape(slots, 1), ends.reshape(slots, 1)
    start_row = jnp.pad(seq_starts, ((0, 0), (0, 128 - slots)))
    end_row = jnp.pad(ends, ((0, 0), (0, 128 - slots)))
    bias_col = attend_bias[:, :, None]
    eb_own = expand_bias[None, :]
    wide = widen(output_weight, expand_weight, reduce_weight)
    wo_rcv, we_rcv, wr_rcv = (swap(w) for w in wide)
    eb_rcv = swap(eb_own)

    att_other, att_own, logs, qt, kaug = attend_forward(
        me, tokens, attend_weight, bias_col, start_col, end_col, start_row, end_row
    )
    att_rcv = swap(att_other)
    rows = jnp.stack(
        [output_bias, first_gain, first_shift, reduce_bias, second_gain, second_shift, first_gain, first_gain]
    )
    (layer_own, resid, ga_own, ga_other, active, gh, nl, gr, gb, att, small, eb_grad) = middle(
        me, att_own, att_rcv, output_weight, wo_rcv, expand_weight, we_rcv, reduce_weight, wr_rcv,
        eb_own, eb_rcv, tokens, cotangent, rows, start_row, end_row,
    )
    ga_rcv = swap(ga_other)
    layer_rcv = swap(layer_own)
    grad_reduce = reduce_grad(active, gr, 0) + swap(reduce_grad(active, gr, 1))
    grad_expand = expand_grad(nl, gh, 0) + swap(expand_grad(nl, gh, 1))
    out_own, out_other = output_grad(att, gb)
    grad_output = out_own + swap(out_other)
    units = expand_weight.shape[1]
    eb_sum = eb_grad[0, :units] + swap(eb_grad[0, units:])

    dq, dk, dv = attend_backward(
        me, tokens, attend_weight, attend_bias[1:2], start_col, end_col, qt, kaug, logs,
        att_other, att_own, ga_rcv, ga_own,
    )
    grad_attend, bias_grad, rows_other, rows_own = project_back(me, tokens, attend_weight, dq, dk, dv)
    mine = add_rows(rows_own, swap(rows_other), resid)
    grad_tokens = join(me, mine, swap(mine))
    layer_out = join(me, layer_own, layer_rcv)

    small = lax.psum(small, ("dp", "mp"))
    grad_attbias, grad_expbias = lax.psum((bias_grad.T, eb_sum), "dp")
    grad_attend, grad_output, grad_expand, grad_reduce = lax.psum(
        (grad_attend, grad_output, grad_expand, grad_reduce), "dp"
    )
    return (
        layer_out,
        grad_tokens,
        grad_attend,
        grad_attbias,
        grad_output,
        small[5],
        small[3],
        small[4],
        grad_expand,
        grad_expbias,
        grad_reduce,
        small[2],
        small[0],
        small[1],
    )


def solution(mesh):
    return jax.shard_map(
        local,
        mesh=mesh,
        in_specs=(
            P("dp", None),
            P("dp", None),
            P("dp", None),
            P(None, None, "mp"),
            P(None, "mp"),
            P("mp", None),
            P(),
            P(),
            P(),
            P(None, "mp"),
            P("mp"),
            P("mp", None),
            P(),
            P(),
            P(),
            P("dp", None),
        ),
        out_specs=(
            P("dp", None),
            P("dp", None),
            P(None, None, "mp"),
            P(None, "mp"),
            P("mp", None),
            P(),
            P(),
            P(),
            P(None, "mp"),
            P("mp"),
            P("mp", None),
            P(),
            P(),
            P(),
        ),
        check_vma=False,
    )
```

```python
import functools
import math

import jax
import jax.numpy as jnp
from jax import lax
from jax.experimental import pallas as pl
from jax.experimental.pallas import tpu as pltpu
from jax.sharding import PartitionSpec as P

HD = 64
EPS = 1e-05
FAR = 1e30
f32 = jnp.float32
bf16 = jnp.bfloat16
QB = 512
QF = 256
PIECES = 16
LIMIT = 60 * 2**20


def dot(a, b, ca=1, cb=0):
    return lax.dot_general(a, b, (((ca,), (cb,)), ((), ())), preferred_element_type=f32)


def cost(flops, size):
    return pl.CostEstimate(flops=int(flops), bytes_accessed=int(size), transcendentals=0)


def shape(dims, kind=f32):
    return jax.ShapeDtypeStruct(dims, kind)


def whole(a):
    return pl.BlockSpec(a.shape, lambda *_: (0,) * len(a.shape))


def call(body, outs, scalars=(), arrays=(), in_specs=None, out_specs=None, grid=(1,), scratch=(), estimate=None, after=()):
    n, m = len(scalars) + len(arrays), len(after)
    outs = list(outs)

    def kernel(*refs):
        body(*refs[:n], *refs[n + m :])

    return pl.pallas_call(
        kernel,
        out_shape=outs,
        grid_spec=pltpu.PrefetchScalarGridSpec(
            num_scalar_prefetch=len(scalars),
            grid=grid,
            in_specs=[*(in_specs or [whole(a) for a in arrays]), *[pl.BlockSpec(memory_space=pl.ANY)] * m],
            out_specs=out_specs or [whole(o) for o in outs],
            scratch_shapes=list(scratch),
        ),
        compiler_params=pltpu.CompilerParams(vmem_limit_bytes=LIMIT),
        cost_estimate=estimate,
    )(*scalars, *arrays, *after)


def widen_kernel(*refs):
    count = len(refs) // 2
    for src, dst in zip(refs[:count], refs[count:]):
        dst[...] = src[...].astype(f32)


def widen(*arrays):
    return call(widen_kernel, [shape(a.shape) for a in arrays], arrays=arrays)


def turned_row(row):
    return jnp.broadcast_to(row, (8, row.shape[1])).T[:, 0:1]


def split3(v):
    high = v.astype(bf16)
    rest = v - high.astype(f32)
    mid = rest.astype(bf16)
    low = rest - mid.astype(f32)
    return high.astype(f32), mid.astype(f32), low


def tile_of(*given):
    row = lax.broadcasted_iota(jnp.int32, (16, given[0].shape[1]), 0)
    out = jnp.zeros(row.shape, f32)
    for j, v in enumerate(given):
        out = jnp.where(row == j, v, out)
    return out.astype(bf16)


def place_in(spans, shape_, base, axis):
    place = lax.broadcasted_iota(jnp.int32, shape_, axis) + base
    return jnp.where((place >= spans[0]) & (place < spans[1]), 1.0, 0.0)


def query_rows(spans, slots, base, count):
    cols = spans.astype(f32).T.astype(jnp.int32)
    inside = place_in((cols[:slots, 0:1], cols[:slots, 1:2]), (slots, count), base, 1)
    alone = 1.0 - jnp.sum(inside, axis=0, keepdims=True)
    return jnp.concatenate([(inside * -FAR).astype(bf16), tile_of(alone * -FAR)], axis=0)


def key_columns(spans, slots, base, count):
    inside = place_in((spans[0:1], spans[1:2]), (count, 128), base, 0)
    used = jnp.sum(inside, axis=1, keepdims=True)
    lane = lax.broadcasted_iota(jnp.int32, (count, 128), 1)
    ones = (lane > slots) & (lane < slots + 4)
    return jnp.where(
        lane < slots, 1.0 - inside, jnp.where(lane == slots, used, jnp.where(ones, 1.0, 0.0))
    )


def scaled_query(query):
    scaled = query.astype(f32) * (math.log2(math.e) / math.sqrt(HD))
    high = scaled.astype(bf16)
    return high, (scaled - high.astype(f32)).astype(bf16)


def forward_kernel(
    slots, me, tok_other, tok_own, weight, bias, spans,
    att_other, att_own, log_out, qt_out, kaug_out, seg_out, tokens, qhl, vt, segq, sbuf, mbuf,
):
    half = tok_other.shape[0]
    count = 2 * half
    heads = weight.shape[2] // HD
    tokens[0:half] = tok_other[...]
    tokens[half:count] = tok_own[...]
    bases = ((1 - me[0]) * half, me[0] * half)
    for part in range(2):
        at = slice(part * half, (part + 1) * half)
        segq[0 : slots + 16, at] = query_rows(spans[...], slots, bases[part], half)
    segq[slots + 16 :, :] = jnp.zeros((128 - slots - 16, count), bf16)
    seg_out[...] = segq[0 : slots + 16, :]
    bias_q, bias_v = turned_row(bias[0:1]), turned_row(bias[1:2])

    step = 512

    def project(i, carry):
        at = pl.multiple_of(i * step, step)
        rows = tokens[pl.ds(at, step), :]
        query = (dot(weight[0], rows, 0, 1) + bias_q).astype(bf16)
        qt_out[:, pl.ds(at, step)] = query
        high, low = scaled_query(query)
        value = (dot(weight[2], rows, 0, 1) + bias_v).astype(bf16)
        key = dot(rows, weight[1]).astype(bf16).astype(f32)
        base = jnp.where(at < half, bases[0], bases[1] - half) + at
        common = key_columns(spans[...], slots, base, step).astype(bf16)
        lane = lax.broadcasted_iota(jnp.int32, (step, 128), 1)
        for h in range(heads):
            qhl[h * 128 : h * 128 + HD, pl.ds(at, step)] = high[h * HD : (h + 1) * HD]
            qhl[h * 128 + HD : (h + 1) * 128, pl.ds(at, step)] = low[h * HD : (h + 1) * HD]
            vt[h * 80 : h * 80 + HD, pl.ds(at, step)] = value[h * HD : (h + 1) * HD]
            vt[h * 80 + HD : (h + 1) * 80, pl.ds(at, step)] = jnp.ones((16, step), bf16)
            if h % 2 == 0:
                pair = key[:, h * HD : h * HD + 128]
                turned = pltpu.roll(pair, HD, 1)
                twice = (jnp.where(lane < HD, pair, turned), jnp.where(lane < HD, turned, pair))
            kaug_out[h, pl.ds(at, step), 0:128] = twice[h % 2].astype(bf16)
            kaug_out[h, pl.ds(at, step), 128:256] = common
        return carry

    lax.fori_loop(0, count // step, project, 0)

    def score(h, at, slot):
        query = jnp.concatenate([qhl[h * 128 : (h + 1) * 128, pl.ds(at, QF)], segq[:, pl.ds(at, QF)]], axis=0)
        scores = dot(kaug_out[h], query)
        sbuf[slot] = scores
        mbuf[slot] = jnp.max(scores.reshape(count // 8, 8, QF), axis=0)

    def attend(h, at, out, place, slot):
        peak = jnp.max(mbuf[slot], axis=0, keepdims=True)
        probs = jnp.exp2(sbuf[slot] - peak).astype(bf16)
        summed = dot(vt[h * 80 : (h + 1) * 80, :], probs)
        total = summed[HD : HD + 1]
        out[h * HD : (h + 1) * HD, pl.ds(place, QF)] = summed[:HD] / total
        log_out[h : h + 1, pl.ds(at, QF)] = peak + jnp.log2(total)

    score(0, 0, 0)
    for part, out in enumerate((att_other, att_own)):

        def body(i, carry, part=part, out=out):
            place = pl.multiple_of(i * QF, QF)
            at = place + part * half
            for h in range(heads):
                if h + 1 < heads:
                    score(h + 1, at, (h + 1) % 2)
                else:
                    score(0, pl.multiple_of(jnp.minimum(at + QF, count - QF), QF), 0)
                attend(h, at, out, place, h % 2)
            return carry

        lax.fori_loop(0, half // QF, body, 0)


def halves_of(tokens):
    half, depth = tokens.shape[0] // 2, tokens.shape[1]
    return [
        pl.BlockSpec((half, depth), lambda i, me: (1 - me[0], 0)),
        pl.BlockSpec((half, depth), lambda i, me: (me[0], 0)),
    ]


def attend_forward(me, tokens, weight, bias, spans, slots):
    count, width = tokens.shape[0], weight.shape[2]
    half, heads, depth = count // 2, width // HD, tokens.shape[1]
    outs = [
        shape((width, half)),
        shape((width, half)),
        shape((8, count)),
        shape((width, count), bf16),
        shape((heads, count, 256), bf16),
        shape((slots + 16, count), bf16),
    ]
    rest = (weight, bias, spans)
    return call(
        functools.partial(forward_kernel, slots),
        outs,
        scalars=(me,),
        arrays=(tokens, tokens, *rest),
        in_specs=[*halves_of(tokens), *[whole(a) for a in rest]],
        scratch=[
            pltpu.VMEM((count, depth), bf16),
            pltpu.VMEM((heads * 128, count), bf16),
            pltpu.VMEM((heads * 80, count), bf16),
            pltpu.VMEM((128, count), bf16),
            pltpu.VMEM((2, count, QF), f32),
            pltpu.VMEM((2, 8, QF), f32),
        ],
        estimate=cost(20e9, 12e6),
    )


def norm(v):
    center = v - jnp.mean(v, axis=-1, keepdims=True)
    rstd = lax.rsqrt(jnp.mean(center * center, axis=-1, keepdims=True) + EPS)
    return center * rstd, rstd


def norm_back(grad, n, rstd):
    first = jnp.mean(grad, axis=-1, keepdims=True)
    second = jnp.mean(grad * n, axis=-1, keepdims=True)
    return rstd * (grad - first - n * second)


def normal_parts(h):
    size = jnp.abs(h)
    t = 1.0 / (1.0 + (0.3275911 * math.sqrt(0.5)) * size)
    bell = jnp.exp2(h * h * (-0.5 * math.log2(math.e)))
    poly = t * (
        0.127414796 + t * (-0.142248368 + t * (0.7107068705 + t * (-0.7265760135 + t * 0.5307027145)))
    )
    tail = poly * bell
    below = jnp.where(h < 0, tail, 1.0 - tail)
    return below, bell * (1.0 / math.sqrt(2.0 * math.pi))


def gather(ref, order, first, pieces):
    deep = ref.shape[0] // PIECES
    return jnp.concatenate(
        [ref[pl.ds(pl.multiple_of(order[first + r] * deep, deep), deep), :] for r in range(pieces)], axis=0
    )


def grad_lanes(grt, nlt, gbt, act, gh, att):
    return jnp.concatenate([dot(grt, act), dot(nlt, gh), dot(gbt, att, 1, 1)], axis=1)


def middle_kernel(
    order, me, att_own, att_rcv, wo_own, wo_rcv, we_own, we_rcv, wr_own, wr_rcv, eb_own, eb_rcv,
    tok, cot, rows, spans,
    layer_out, resid_out, ga_own, ga_other, act_out, gh_out, nlt_out, grt_out, gbt_out, att_out, small,
    keep_out, send_out, wo, we, wr, act_s, gh_s, nlt_s, grt_s, gbt_s, att_s,
):
    i = pl.program_id(0)
    steps = pl.num_programs(0) - 2
    units = we_own.shape[1]
    width = wo_own.shape[0]
    count, depth = tok.shape

    @pl.when(i == 0)
    def _():
        wo[0:width] = wo_own[...]
        wo[width:] = wo_rcv[...].astype(bf16)
        we[:, 0:units] = we_own[...]
        we[:, units:] = we_rcv[...].astype(bf16)
        wr[0:units] = wr_own[...]
        wr[units:] = wr_rcv[...].astype(bf16)
        small[...] = jnp.zeros_like(small)

    @pl.when(i < steps)
    def _():
        output_bias, gain1, shift1, reduce_bias, gain2, shift2 = (rows[j : j + 1] for j in range(6))
        base = (me[0] * steps + i) * count
        inside = place_in((spans[0:1], spans[1:2]), (count, 128), base, 0)
        valid = jnp.sum(inside, axis=1, keepdims=True)
        here = pl.ds(pl.multiple_of(i * count, count), count)

        att = jnp.concatenate([att_own[...], att_rcv[...]], axis=0).astype(bf16)
        att_out[...] = att[:width]
        att_s[:, here] = att[width:]
        resid_one = tok[...].astype(f32) + (dot(att, wo[...], 0, 0) + output_bias)
        n1, rstd1 = norm(resid_one)
        normed = n1 * gain1 + shift1
        normed_low = normed.astype(bf16)
        turned = normed_low.T
        nlt_out[...] = turned
        nlt_s[:, here] = turned
        bias = jnp.concatenate([eb_own[...], eb_rcv[...]], axis=1)
        hidden = dot(normed_low, we[...]) + bias
        below, density = normal_parts(hidden)
        active = (hidden * below).astype(bf16)
        slope = below + hidden * density
        act_out[...] = active[:, :units]
        act_s[here, :] = active[:, units:]
        resid_two = normed + (dot(active, wr[...]) + reduce_bias)
        n2, rstd2 = norm(resid_two)
        layer_out[...] = ((n2 * gain2 + shift2) * valid).astype(bf16).astype(f32)
        grad = cot[...].astype(f32) * valid
        column = lambda v: jnp.sum(v, axis=0, keepdims=True)
        small[0:1, :depth] += column(grad * n2)
        small[1:2, :depth] += column(grad)
        grad_two = norm_back(grad * gain2, n2, rstd2)
        grad_result = grad_two.astype(bf16)
        turned = grad_result.T
        grt_out[...] = turned
        grt_s[:, here] = turned
        small[2:3, :depth] += column(grad_result.astype(f32))
        grad_hidden = (dot(grad_result, wr[...], 1, 1) * slope).astype(bf16)
        gh_out[...] = grad_hidden[:, :units]
        gh_s[here, :] = grad_hidden[:, units:]
        small[6:7] += column(grad_hidden.astype(f32))
        grad_normed = grad_two + dot(grad_hidden, we[...], 1, 1)
        small[3:4, :depth] += column(grad_normed * n1)
        small[4:5, :depth] += column(grad_normed)
        grad_one = norm_back(grad_normed * gain1, n1, rstd1)
        resid_out[...] = grad_one
        grad_branch = grad_one.astype(bf16)
        turned = grad_branch.T
        gbt_out[...] = turned
        gbt_s[:, here] = turned
        small[5:6, :depth] += column(grad_branch.astype(f32))
        grad_att = dot(wo[...], grad_branch, 1, 1).astype(bf16).astype(f32)
        ga_own[...] = grad_att[0:width]
        ga_other[...] = grad_att[width:]

    for first, out in ((0, keep_out), (PIECES // 2, send_out)):

        @pl.when(i == steps + first // (PIECES // 2))
        def _(first=first, out=out):
            parts = [gather(ref, order, first, PIECES // 2) for ref in (grt_s, nlt_s, gbt_s)]
            wide = out.shape[1] // 2
            for j in range(2):
                u = slice(j * units // 2, (j + 1) * units // 2)
                e = slice(j * width // 2, (j + 1) * width // 2)
                out[:, j * wide : (j + 1) * wide] = grad_lanes(*parts, act_s[:, u], gh_s[:, u], att_s[e, :])


def middle(order, me, att_own, att_rcv, weights, tokens, cotangent, rows, spans):
    half, depth = tokens.shape[0] // 2, tokens.shape[1]
    width, units = weights[0].shape[0], weights[2].shape[1]
    blk = 256
    steps = half // blk
    at = lambda i: jnp.minimum(i, steps - 1)
    by_row = lambda n: pl.BlockSpec((blk, n), lambda i, *_: (at(i), 0))
    by_col = lambda n: pl.BlockSpec((n, blk), lambda i, *_: (0, at(i)))
    mine = pl.BlockSpec((blk, depth), lambda i, order, me: (me[0] * steps + at(i), 0))
    lanes = 2 * units + width
    outs = [
        (shape((half, depth)), by_row(depth)),
        (shape((half, depth)), by_row(depth)),
        (shape((width, half)), by_col(width)),
        (shape((width, half)), by_col(width)),
        (shape((half, units), bf16), by_row(units)),
        (shape((half, units), bf16), by_row(units)),
        (shape((depth, half), bf16), by_col(depth)),
        (shape((depth, half), bf16), by_col(depth)),
        (shape((depth, half), bf16), by_col(depth)),
        (shape((width, half), bf16), by_col(width)),
        (shape((8, 2 * units)), None),
        (shape((depth // 2, lanes)), None),
        (shape((depth // 2, lanes)), None),
    ]
    return call(
        middle_kernel,
        [o for o, _ in outs],
        scalars=(order, me),
        arrays=(att_own, att_rcv, *weights, tokens, cotangent, rows, spans),
        in_specs=[
            by_col(width),
            by_col(width),
            *[whole(a) for a in weights],
            mine,
            mine,
            whole(rows),
            whole(spans),
        ],
        out_specs=[s or whole(o) for o, s in outs],
        grid=(steps + 2,),
        scratch=[
            pltpu.VMEM((2 * width, depth), bf16),
            pltpu.VMEM((depth, 2 * units), bf16),
            pltpu.VMEM((2 * units, depth), bf16),
            pltpu.VMEM((half, units), bf16),
            pltpu.VMEM((half, units), bf16),
            pltpu.VMEM((depth, half), bf16),
            pltpu.VMEM((depth, half), bf16),
            pltpu.VMEM((depth, half), bf16),
            pltpu.VMEM((width, half), bf16),
        ],
        estimate=cost(20e9, 40e6),
    )


def own_grads_kernel(first, order, grt, nlt, gbt, act, gh, att, got, out):
    parts = [gather(ref, order, first, PIECES // 2) for ref in (grt, nlt, gbt)]
    out[...] = grad_lanes(*parts, act[...], gh[...], att[...]) + got[...]


def own_grads(first, order, grt, nlt, gbt, act, gh, att, got):
    half, units, width = act.shape[0], act.shape[1], att.shape[0]
    rows, lanes = got.shape
    part = pl.BlockSpec((half, units // 2), lambda i, order: (0, i))
    block = pl.BlockSpec((rows, lanes // 2), lambda i, order: (0, i))
    return call(
        functools.partial(own_grads_kernel, first),
        [shape(got.shape)],
        scalars=(order,),
        arrays=(grt, nlt, gbt, act, gh, att, got),
        in_specs=[
            *[whole(a) for a in (grt, nlt, gbt)],
            part,
            part,
            pl.BlockSpec((width // 2, half), lambda i, order: (i, 0)),
            block,
        ],
        out_specs=[block],
        grid=(2,),
        estimate=cost(3e9, 10e6),
    )[0]


def place_grads_kernel(order, low, high, reduce, expand, out, red, outt):
    deep = expand.shape[0] // PIECES
    units, width = red.shape[1] // 2, outt.shape[1] // 2
    for r in range(PIECES):
        src = (low, high)[r // (PIECES // 2)]
        of = slice(r % (PIECES // 2) * deep, r % (PIECES // 2) * deep + deep)
        at = pl.ds(pl.multiple_of(order[r] * deep, deep), deep)
        for j in range(2):
            lane = j * (src.shape[1] // 2)
            for dst, wide in ((red, units), (expand, units), (outt, width)):
                dst[at, j * wide : (j + 1) * wide] = src[of, lane : lane + wide]
                lane += wide
    reduce[...] = red[...].T
    out[...] = outt[...].T


def place_grads(order, low, high, units, width):
    depth = 2 * low.shape[0]
    return call(
        place_grads_kernel,
        [shape((units, depth)), shape((depth, units)), shape((width, depth))],
        scalars=(order,),
        arrays=(low, high),
        scratch=[pltpu.VMEM((depth, units), f32), pltpu.VMEM((depth, width), f32)],
        estimate=cost(0, 10e6),
    )


def prepare_kernel(me, tok_other, tok_own, weight, bias, kt, vaug, tokt):
    half = tok_other.shape[0]
    heads = weight.shape[2] // HD
    lane = lax.broadcasted_iota(jnp.int32, (half, 128), 1)
    ones = jnp.where(lane < HD + 3, 1.0, 0.0)
    for part, tok in enumerate((tok_other, tok_own)):
        at = slice(part * half, (part + 1) * half)
        tokt[:, at] = tok[...].T
        kt[:, at] = dot(weight[1], tok[...], 0, 1).astype(bf16)
        value = (dot(tok[...], weight[2]) + bias[1:2]).astype(bf16).astype(f32)
        for h in range(heads):
            pair = value[:, h // 2 * 128 : h // 2 * 128 + 128]
            if h % 2:
                pair = pltpu.roll(pair, HD, 1)
            vaug[h, at, :] = jnp.where(lane < HD, pair, ones).astype(bf16)


def prepare(me, tokens, weight, bias, after):
    count, depth = tokens.shape
    width = weight.shape[2]
    return call(
        prepare_kernel,
        [shape((width, count), bf16), shape((width // HD, count, 128), bf16), shape((depth, count), bf16)],
        scalars=(me,),
        arrays=(tokens, tokens, weight, bias),
        in_specs=[*halves_of(tokens), whole(weight), whole(bias)],
        estimate=cost(4e9, 8e6),
        after=after,
    )


def backward_kernel(
    head, qt, kt, kaug, vaug, seg, logs, att_other, att_own, ga_other, ga_own, dq, dk, dv, dkt, dvt
):
    half = att_other.shape[1]
    slots = seg.shape[0] - 16
    scale = HD**-0.5
    dkt[...] = jnp.zeros_like(dkt)
    dvt[...] = jnp.zeros_like(dvt)
    zeros_q = jnp.zeros((256 - 2 * HD - slots - 16, QB), bf16)
    zeros_v = jnp.zeros((128 - HD - 16, QB), bf16)

    for part, (att, ga) in enumerate(((att_other, ga_other), (att_own, ga_own))):

        def body(i, carry, part=part, att=att, ga=ga):
            place = pl.multiple_of(i * QB, QB)
            at = place + part * half
            grad = ga[:, pl.ds(place, QB)]
            inner = -jnp.sum(grad * att[:, pl.ds(place, QB)], axis=0, keepdims=True)
            grad_low = grad.astype(bf16)
            upper = jnp.concatenate([grad_low, tile_of(*split3(inner)), zeros_v], axis=0)
            query = qt[:, pl.ds(at, QB)]
            logs_q = logs[head : head + 1, pl.ds(at, QB)]
            alone = seg[slots : slots + 1, pl.ds(at, QB)].astype(f32)
            tile = tile_of(alone, *split3(-logs_q))
            left = jnp.concatenate([*scaled_query(query), seg[0:slots, pl.ds(at, QB)], tile, zeros_q], axis=0)
            probs = jnp.exp2(dot(kaug[0], left))
            grad_probs = dot(vaug[0], upper)
            grad_scores = (probs * grad_probs).astype(bf16)
            dvt[...] += dot(grad_low, probs.astype(bf16), 1, 1)
            dkt[...] += dot(query, grad_scores, 1, 1)
            dq[:, pl.ds(at, QB)] = (dot(kt[...], grad_scores) * scale).astype(bf16)
            return carry

        lax.fori_loop(0, half // QB, body, 0)
    dk[...] = (dkt[...] * scale).astype(bf16)
    dv[...] = dvt[...].astype(bf16)


def attend_backward(head, qt, kt, kaug, vaug, seg, logs, att_other, att_own, ga_other, ga_own, after):
    count = qt.shape[1]
    by_head = lambda n: pl.BlockSpec((HD, n), lambda i: (head, 0))
    return call(
        functools.partial(backward_kernel, head),
        [shape((HD, count), bf16)] * 3,
        arrays=(qt, kt, kaug, vaug, seg, logs, att_other, att_own, ga_other, ga_own),
        in_specs=[
            by_head(count),
            by_head(count),
            pl.BlockSpec((1, count, 256), lambda i: (head, 0, 0)),
            pl.BlockSpec((1, count, 128), lambda i: (head, 0, 0)),
            whole(seg),
            whole(logs),
            *[by_head(count // 2)] * 4,
        ],
        scratch=[pltpu.VMEM((HD, count), f32), pltpu.VMEM((HD, count), f32)],
        estimate=cost(13e9, 6e6),
        after=after,
    )


def project_grad_kernel(order, tokt, small, small_rcv, *refs):
    *parts, keep, send, full = refs
    rows, lanes = keep.shape
    units, depth = small.shape[1] // 2, tokt.shape[0]
    width = lanes // 3
    for j, part in enumerate(parts):
        full[j * HD : (j + 1) * HD] = part[...]
    for first, out in ((0, keep), (PIECES // 2, send)):
        out[: rows - 16] = dot(gather(tokt, order, first, PIECES // 2), full[...], 1, 1)
        out[rows - 16 :] = jnp.zeros((16, lanes), f32)
        out[rows - 16 : rows - 10, :depth] = small[0:6, :depth] + small_rcv[0:6, :depth]
        hidden = small[6:7, :units] + small_rcv[6:7, units:]
        for j in range(units // depth):
            out[rows - 10 + j : rows - 9 + j, :depth] = hidden[:, j * depth : (j + 1) * depth]
        column = dot(jnp.ones((8, full.shape[1]), bf16), full[...], 1, 1)
        out[rows - 8 : rows - 7, 0:width] = column[0:1, 0:width]
        out[rows - 8 : rows - 7, width : 2 * width] = column[0:1, 2 * width :]


def project_grad(order, tokt, small, small_rcv, parts):
    depth, count = tokt.shape
    lanes = len(parts) * HD
    return call(
        project_grad_kernel,
        [shape((depth // 2 + 16, lanes))] * 2,
        scalars=(order,),
        arrays=(tokt, small, small_rcv, *parts),
        scratch=[pltpu.VMEM((lanes, count), bf16)],
        estimate=cost(4e9, 8e6),
    )


def project_rows_kernel(weight, *refs):
    *parts, other, own, full = refs
    half = other.shape[1]
    width = weight.shape[2]
    for j, part in enumerate(parts):
        full[j * HD : (j + 1) * HD] = part[...]
    for at, out in ((0, other), (half, own)):
        out[...] = sum(
            dot(weight[c], full[c * width : (c + 1) * width, at : at + half]) for c in range(weight.shape[0])
        )


def project_rows(weight, parts, after):
    depth, count = weight.shape[1], parts[0].shape[1]
    return call(
        project_rows_kernel,
        [shape((depth, count // 2))] * 2,
        arrays=(weight, *parts),
        scratch=[pltpu.VMEM((len(parts) * HD, count), bf16)],
        estimate=cost(4e9, 8e6),
        after=after,
    )


def place_attend_kernel(order, low, high, small, out, bias, hidden, *vectors):
    deep = out.shape[1] // PIECES
    width = out.shape[2]
    depth = out.shape[1]
    for r in range(PIECES):
        src = (low, high)[r // (PIECES // 2)]
        of = slice(r % (PIECES // 2) * deep, r % (PIECES // 2) * deep + deep)
        at = pl.ds(pl.multiple_of(order[r] * deep, deep), deep)
        for c in range(3):
            out[c, at, :] = src[of, c * width : (c + 1) * width]
    bias[0:1] = small[8:9, 0:width]
    bias[1:2] = small[8:9, width : 2 * width]
    for j in range(hidden.shape[1] // depth):
        hidden[:, j * depth : (j + 1) * depth] = small[6 + j : 7 + j, :depth]
    for j, vector in enumerate(vectors):
        vector[...] = small[j : j + 1, :depth]


def place_attend(order, low, high, small, depth, width, units):
    return call(
        place_attend_kernel,
        [shape((3, depth, width)), shape((2, width)), shape((1, units)), *[shape((1, depth))] * 6],
        scalars=(order,),
        arrays=(low, high, small),
        estimate=cost(0, 6e6),
    )


def add_rows_kernel(a, b, c, out):
    out[...] = ((a[...] + b[...]).T + c[...]).astype(bf16).astype(f32)


def add_rows(a, b, c):
    rows, depth = c.shape
    turned = pl.BlockSpec((depth, rows // 4), lambda i: (0, i))
    blk = pl.BlockSpec((rows // 4, depth), lambda i: (i, 0))
    return call(
        add_rows_kernel,
        [shape(c.shape)],
        arrays=(a, b, c),
        grid=(4,),
        in_specs=[turned, turned, blk],
        out_specs=[blk],
        estimate=cost(0, 8e6),
    )[0]


def join_kernel(me, own, other, out):
    mine = pl.program_id(0) == me[0]

    @pl.when(mine)
    def _():
        out[...] = own[...].astype(bf16)

    @pl.when(jnp.logical_not(mine))
    def _():
        out[...] = other[...].astype(bf16)


def join(me, own, other, after=()):
    half, depth = own.shape
    block = pl.BlockSpec((half, depth), lambda i, me: (0, 0))
    return call(
        join_kernel,
        [shape((2 * half, depth), bf16)],
        scalars=(me,),
        arrays=(own, other),
        grid=(2,),
        in_specs=[block, block],
        out_specs=[pl.BlockSpec((half, depth), lambda i, me: (i, 0))],
        estimate=cost(0, 6e6),
        after=after,
    )[0]


def swap(v):
    return lax.ppermute(v, "mp", [(0, 1), (1, 0)])


BITS = ((1, 2), (2, 1), (4, 4), (8, 8))


def masks(core):
    return [sum(BITS[3 - b][core] for b in range(4) if r >> b & 1) for r in range(PIECES)]


def piece_order(which):
    table = jnp.array([masks(0), masks(1)], jnp.int32)
    core = lax.axis_index("mp")
    return lax.axis_index("dp").astype(jnp.int32) ^ table[1 - core if which else core]


def across(v, position):
    pairs = [
        (2 * d + core, 2 * (d ^ masks(core)[position]) + core) for d in range(PIECES) for core in range(2)
    ]
    return lax.ppermute(v, ("dp", "mp"), pairs)


def halve_first(keep, send, extra=0):
    got = across(send, 8)
    half = (keep.shape[0] - extra) // 2
    lead = keep[half:] + got[half:]
    return lead, keep[:half] + got[:half]


def halve_second(lead, rest, extra=0):
    got = across(lead, 4)
    half = rest.shape[0]
    mine = rest + got[:half]
    return mine, lead[half:] + got[half:]


def halve_last(mine, more, extra=0):
    size = mine.shape[0] // 4
    got = []
    for p in (3, 2, 1):
        part = mine[p * size : (p + 1) * size]
        got.append(across(jnp.concatenate([part, more]) if extra else part, p))
    piece = mine[:size] + got[0][:size] + got[1][:size] + got[2][:size]
    return piece, more + got[0][size:] + got[1][size:] + got[2][size:]


def double_first(piece):
    got = [across(piece, p) for p in (3, 2, 1)]
    return jnp.concatenate([piece, got[2], got[1], got[0]])


def double_second(four):
    return jnp.concatenate([four, across(four, 4)])


def local(
    tokens, seq_starts, seq_lengths, attend_weight, attend_bias, output_weight, output_bias, first_gain, first_shift,
    expand_weight, expand_bias, reduce_weight, reduce_bias, second_gain, second_shift, cotangent,
):
    slots = seq_starts.shape[1]
    units, width, depth = expand_weight.shape[1], output_weight.shape[0], tokens.shape[1]
    by_pieces = lax.axis_size("dp") == PIECES
    me = lax.axis_index("mp").astype(jnp.int32)[None]
    plain = jnp.arange(PIECES, dtype=jnp.int32)
    order, order_other = (piece_order(0), piece_order(1)) if by_pieces else (plain, plain)
    spans = jnp.concatenate([seq_starts, seq_starts + seq_lengths])
    spans = jnp.pad(spans, ((0, 6), (0, 128 - slots)))
    eb_own = expand_bias[None, :]
    wide = widen(output_weight, expand_weight, reduce_weight)
    wo_rcv, we_rcv, wr_rcv = (swap(w) for w in wide)
    eb_rcv = swap(eb_own)
    rows = jnp.stack(
        [output_bias, first_gain, first_shift, reduce_bias, second_gain, second_shift, first_gain, first_gain]
    )

    att_other, att_own, logs, qt, kaug, seg = attend_forward(me, tokens, attend_weight, attend_bias, spans, slots)
    att_rcv = swap(att_other)
    weights = (output_weight, wo_rcv, expand_weight, we_rcv, reduce_weight, wr_rcv, eb_own, eb_rcv)
    (layer_own, resid, ga_own, ga_other, act, gh, nlt, grt, gbt, att, small, keep, send) = middle(
        order_other, me, att_own, att_rcv, weights, tokens, cotangent, rows, spans
    )
    send_rcv, keep_rcv, ga_rcv = swap(send), swap(keep), swap(ga_other)
    small_rcv, layer_rcv = swap(small), swap(layer_own)
    kt, vaug, tokt = prepare(me, tokens, attend_weight, attend_bias, (small,))
    send = own_grads(PIECES // 2, order, grt, nlt, gbt, act, gh, att, send_rcv)
    keep = own_grads(0, order, grt, nlt, gbt, act, gh, att, keep_rcv)

    def backward(h, after):
        return attend_backward(h, qt, kt, kaug, vaug, seg, logs, att_other, att_own, ga_rcv, ga_own, after)

    heads = [backward(0, (keep,)), backward(1, (keep,))]
    if by_pieces:
        lead, rest = halve_first(keep, send)
        heads.append(backward(2, (lead,)))
        mine, more = halve_second(lead, rest)
        heads.append(backward(3, (mine,)))
        piece, _ = halve_last(mine, more)
    else:
        heads += [backward(2, ()), backward(3, ())]
    parts = [head[c] for c in range(3) for head in heads]
    keep_a, send_a = project_grad(order, tokt, small, small_rcv, parts)
    rows_other, rows_own = project_rows(attend_weight, parts, (keep_a,))
    rows_rcv = swap(rows_other)
    mine_rows = add_rows(rows_own, rows_rcv, resid)
    rows_back = swap(mine_rows)

    if by_pieces:
        four = double_first(piece)
        lead_a, rest_a = halve_first(keep_a, send_a, 16)
        mine_a, more_a = halve_second(lead_a, rest_a, 16)
        piece_a, totals = halve_last(mine_a, more_a, 16)
        low = double_second(four)
        four_a = double_first(piece_a)
        high = across(low, 8)
        low_a = double_second(four_a)
        high_a = across(low_a, 8)
    else:
        low, high, low_a, high_a = lax.psum((keep, send, keep_a, send_a), "dp")
        totals = low_a[-16:]
    grad_tokens = join(me, mine_rows, rows_back)
    layer_out = join(me, layer_own, layer_rcv)
    grad_reduce, grad_expand, grad_output = place_grads(order, low, high, units, width)
    grad_attend, grad_bias, grad_hidden, *vectors = place_attend(order, low_a, high_a, totals, depth, width, units)
    vectors = [v.reshape(depth) for v in vectors]
    return (
        layer_out,
        grad_tokens,
        grad_attend,
        grad_bias,
        grad_output,
        vectors[5],
        vectors[3],
        vectors[4],
        grad_expand,
        grad_hidden.reshape(units),
        grad_reduce,
        vectors[2],
        vectors[0],
        vectors[1],
    )


def solution(mesh):
    return jax.shard_map(
        local,
        mesh=mesh,
        in_specs=(
            P("dp", None),
            P("dp", None),
            P("dp", None),
            P(None, None, "mp"),
            P(None, "mp"),
            P("mp", None),
            P(),
            P(),
            P(),
            P(None, "mp"),
            P("mp"),
            P("mp", None),
            P(),
            P(),
            P(),
            P("dp", None),
        ),
        out_specs=(
            P("dp", None),
            P("dp", None),
            P(None, None, "mp"),
            P(None, "mp"),
            P("mp", None),
            P(),
            P(),
            P(),
            P(None, "mp"),
            P("mp"),
            P("mp", None),
            P(),
            P(),
            P(),
        ),
        check_vma=False,
    )
```

```python
import functools
import math

import jax
import jax.numpy as jnp
from jax import lax
from jax.experimental import pallas as pl
from jax.experimental.pallas import tpu as pltpu
from jax.sharding import PartitionSpec as P

HD = 64
EPS = 1e-05
FAR = 1e30
f32 = jnp.float32
bf16 = jnp.bfloat16
QB = 512
QF = 256
PIECES = 16


def dot(a, b, ca=1, cb=0):
    return lax.dot_general(a, b, (((ca,), (cb,)), ((), ())), preferred_element_type=f32)


def cost(flops, size):
    return pl.CostEstimate(flops=int(flops), bytes_accessed=int(size), transcendentals=0)


def shape(dims, kind=f32):
    return jax.ShapeDtypeStruct(dims, kind)


def whole(a):
    return pl.BlockSpec(a.shape, lambda *_: (0,) * len(a.shape), pipeline_mode=pl.Buffered(1))


def call(body, outs, scalars=(), arrays=(), in_specs=None, out_specs=None, grid=(1,), scratch=(), estimate=None, after=(), limit=10, mark=False):
    n, m, k = len(scalars) + len(arrays), len(after), len(outs)
    outs = list(outs)
    out_specs = list(out_specs or [whole(o) for o in outs])
    if mark:
        outs.append(shape((8, 128)))
        out_specs.append(whole(outs[-1]))

    def kernel(*refs):
        body(*refs[:n], *refs[n + m : n + m + k], *refs[n + m + k + mark :])
        if mark:
            refs[n + m + k][...] = jnp.zeros((8, 128), f32)

    return pl.pallas_call(
        kernel,
        out_shape=outs,
        grid_spec=pltpu.PrefetchScalarGridSpec(
            num_scalar_prefetch=len(scalars),
            grid=grid,
            in_specs=[*(in_specs or [whole(a) for a in arrays]), *[pl.BlockSpec(memory_space=pl.ANY)] * m],
            out_specs=out_specs,
            scratch_shapes=list(scratch),
        ),
        compiler_params=pltpu.CompilerParams(vmem_limit_bytes=limit * 2**20),
        cost_estimate=estimate,
    )(*scalars, *arrays, *after)


def hbm(a):
    return pltpu.with_memory_space_constraint(a, pltpu.HBM)


def widen_kernel(output, expand, low, high, bias, out):
    i = pl.program_id(0)
    units, depth = expand.shape[1], output.shape[1]
    out[:, :units] = expand[...].astype(f32)
    out[:, units : units + depth] = low[...].astype(f32)
    out[:, units + depth : units + 2 * depth] = high[...].astype(f32)

    @pl.when(i < 2)
    def _():
        out[:, units + 2 * depth :] = output[...].astype(f32)

    @pl.when(i >= 2)
    def _():
        out[0:1, units + 2 * depth :] = bias[:, :depth]
        out[1:2, units + 2 * depth :] = bias[:, depth:]


def widen(output, expand, reduce, bias):
    depth, units = expand.shape
    blk = depth // 4
    rows = lambda n, at: pl.BlockSpec((blk, n), at)
    out = shape((depth, units + 3 * depth))
    return call(
        widen_kernel,
        [out],
        arrays=[hbm(a) for a in (output, expand, reduce, reduce, bias)],
        in_specs=[
            rows(depth, lambda i: (jnp.minimum(i, 1), 0)),
            rows(units, lambda i: (i, 0)),
            rows(depth, lambda i: (i, 0)),
            rows(depth, lambda i: (i + 4, 0)),
            whole(bias),
        ],
        out_specs=[rows(out.shape[1], lambda i: (i, 0))],
        grid=(4,),
        estimate=cost(0, 7e6),
        limit=14,
    )[0]


def turned_row(row):
    return jnp.broadcast_to(row, (8, row.shape[1])).T[:, 0:1]


def split3(v):
    high = v.astype(bf16)
    rest = v - high.astype(f32)
    mid = rest.astype(bf16)
    low = rest - mid.astype(f32)
    return high.astype(f32), mid.astype(f32), low


def tile_of(*given):
    row = lax.broadcasted_iota(jnp.int32, (16, given[0].shape[1]), 0)
    out = jnp.zeros(row.shape, f32)
    for j, v in enumerate(given):
        out = jnp.where(row == j, v, out)
    return out.astype(bf16)


def place_in(spans, shape_, base, axis):
    place = lax.broadcasted_iota(jnp.int32, shape_, axis) + base
    return jnp.where((place >= spans[0]) & (place < spans[1]), 1.0, 0.0)


def query_rows(spans, slots, base, count):
    cols = spans.astype(f32).T.astype(jnp.int32)
    inside = place_in((cols[:slots, 0:1], cols[:slots, 1:2]), (slots, count), base, 1)
    alone = 1.0 - jnp.sum(inside, axis=0, keepdims=True)
    return jnp.concatenate([(inside * -FAR).astype(bf16), tile_of(alone * -FAR)], axis=0)


def key_columns(spans, slots, base, count):
    inside = place_in((spans[0:1], spans[1:2]), (count, 128), base, 0)
    used = jnp.sum(inside, axis=1, keepdims=True)
    lane = lax.broadcasted_iota(jnp.int32, (count, 128), 1)
    ones = (lane > slots) & (lane < slots + 4)
    return jnp.where(
        lane < slots, 1.0 - inside, jnp.where(lane == slots, used, jnp.where(ones, 1.0, 0.0))
    )


def scaled_query(query):
    scaled = query.astype(f32) * (math.log2(math.e) / math.sqrt(HD))
    high = scaled.astype(bf16)
    return high, (scaled - high.astype(f32)).astype(bf16)


def forward_kernel(
    slots, me, tok_other, tok_own, weight, bias, spans,
    att_other, own_hbm, log_hbm, qt_hbm, kaug_hbm, seg_hbm, tokens, qhl, vt, segq, sbuf, mbuf,
    att_own, log_out, qt_out, kaug_out, sems,
):
    half = tok_other.shape[0]
    count = 2 * half
    heads = weight.shape[2] // HD
    tokens[0:half] = tok_other[...]
    tokens[half:count] = tok_own[...]
    bases = ((1 - me[0]) * half, me[0] * half)
    for part in range(2):
        at = slice(part * half, (part + 1) * half)
        segq[0 : slots + 16, at] = query_rows(spans[...], slots, bases[part], half)
    segq[slots + 16 :, :] = jnp.zeros((128 - slots - 16, count), bf16)
    bias_q, bias_v = turned_row(bias[0:1]), turned_row(bias[1:2])

    step = 512

    def project(i, carry):
        at = pl.multiple_of(i * step, step)
        rows = tokens[pl.ds(at, step), :]
        query = (dot(weight[0], rows, 0, 1) + bias_q).astype(bf16)
        qt_out[:, pl.ds(at, step)] = query
        high, low = scaled_query(query)
        value = (dot(weight[2], rows, 0, 1) + bias_v).astype(bf16)
        key = dot(rows, weight[1]).astype(bf16).astype(f32)
        base = jnp.where(at < half, bases[0], bases[1] - half) + at
        common = key_columns(spans[...], slots, base, step).astype(bf16)
        lane = lax.broadcasted_iota(jnp.int32, (step, 128), 1)
        for h in range(heads):
            qhl[h * 128 : h * 128 + HD, pl.ds(at, step)] = high[h * HD : (h + 1) * HD]
            qhl[h * 128 + HD : (h + 1) * 128, pl.ds(at, step)] = low[h * HD : (h + 1) * HD]
            vt[h * 80 : h * 80 + HD, pl.ds(at, step)] = value[h * HD : (h + 1) * HD]
            vt[h * 80 + HD : (h + 1) * 80, pl.ds(at, step)] = jnp.ones((16, step), bf16)
            if h % 2 == 0:
                pair = key[:, h * HD : h * HD + 128]
                turned = pltpu.roll(pair, HD, 1)
                twice = (jnp.where(lane < HD, pair, turned), jnp.where(lane < HD, turned, pair))
            kaug_out[h, pl.ds(at, step), 0:128] = twice[h % 2].astype(bf16)
            kaug_out[h, pl.ds(at, step), 128:256] = common
        return carry

    lax.fori_loop(0, count // step, project, 0)
    copies = [
        pltpu.make_async_copy(src, dst, sems.at[j])
        for j, (src, dst) in enumerate(
            ((kaug_out, kaug_hbm), (qt_out, qt_hbm), (segq.at[0 : slots + 16, :], seg_hbm), (log_out, log_hbm), (att_own, own_hbm))
        )
    ]
    for copy in copies[:3]:
        copy.start()

    def score(h, at, slot):
        query = jnp.concatenate([qhl[h * 128 : (h + 1) * 128, pl.ds(at, QF)], segq[:, pl.ds(at, QF)]], axis=0)
        scores = dot(kaug_out[h], query)
        sbuf[slot] = scores
        mbuf[slot] = jnp.max(scores.reshape(count // 8, 8, QF), axis=0)

    def attend(h, at, out, place, slot):
        peak = jnp.max(mbuf[slot], axis=0, keepdims=True)
        probs = jnp.exp2(sbuf[slot] - peak).astype(bf16)
        summed = dot(vt[h * 80 : (h + 1) * 80, :], probs)
        total = summed[HD : HD + 1]
        out[h * HD : (h + 1) * HD, pl.ds(place, QF)] = summed[:HD] / total
        log_out[h : h + 1, pl.ds(at, QF)] = peak + jnp.log2(total)

    score(0, 0, 0)
    for part, out in enumerate((att_other, att_own)):

        def body(i, carry, part=part, out=out):
            place = pl.multiple_of(i * QF, QF)
            at = place + part * half
            for h in range(heads):
                if h + 1 < heads:
                    score(h + 1, at, (h + 1) % 2)
                else:
                    score(0, pl.multiple_of(jnp.minimum(at + QF, count - QF), QF), 0)
                attend(h, at, out, place, h % 2)
            return carry

        lax.fori_loop(0, half // QF, body, 0)
    for copy in copies[3:]:
        copy.start()
    for copy in copies:
        copy.wait()


def halves_of(tokens):
    half, depth = tokens.shape[0] // 2, tokens.shape[1]
    return [
        pl.BlockSpec((half, depth), lambda i, me: (1 - me[0], 0)),
        pl.BlockSpec((half, depth), lambda i, me: (me[0], 0)),
    ]


def attend_forward(me, tokens, weight, bias, spans, slots):
    count, width = tokens.shape[0], weight.shape[2]
    half, heads, depth = count // 2, width // HD, tokens.shape[1]
    kept = [
        ((width, half), f32),
        ((8, count), f32),
        ((width, count), bf16),
        ((heads, count, 256), bf16),
        ((slots + 16, count), bf16),
    ]
    outs = [shape((width, half)), *[pltpu.HBM(*k) for k in kept]]
    rest = (hbm(weight), bias, spans)
    return call(
        functools.partial(forward_kernel, slots),
        outs,
        scalars=(me,),
        arrays=(hbm(tokens), hbm(tokens), *rest),
        in_specs=[*halves_of(tokens), *[whole(a) for a in rest]],
        out_specs=[whole(outs[0]), *[pl.BlockSpec(memory_space=pltpu.HBM)] * 5],
        scratch=[
            pltpu.VMEM((count, depth), bf16),
            pltpu.VMEM((heads * 128, count), bf16),
            pltpu.VMEM((heads * 80, count), bf16),
            pltpu.VMEM((128, count), bf16),
            pltpu.VMEM((2, count, QF), f32),
            pltpu.VMEM((2, 8, QF), f32),
            *[pltpu.VMEM(*k) for k in kept[:4]],
            pltpu.SemaphoreType.DMA((5,)),
        ],
        estimate=cost(20e9, 12e6),
        limit=28,
    )


def norm(v):
    center = v - jnp.mean(v, axis=-1, keepdims=True)
    rstd = lax.rsqrt(jnp.mean(center * center, axis=-1, keepdims=True) + EPS)
    return center * rstd, rstd


def norm_back(grad, n, rstd):
    first = jnp.mean(grad, axis=-1, keepdims=True)
    second = jnp.mean(grad * n, axis=-1, keepdims=True)
    return rstd * (grad - first - n * second)


def normal_parts(h):
    below = 0.5 + 0.5 * lax.erf(h * math.sqrt(0.5))
    bell = jnp.exp2(h * h * (-0.5 * math.log2(math.e)))
    return below, bell * (1.0 / math.sqrt(2.0 * math.pi))


def gather(ref, order, first, pieces):
    deep = ref.shape[0] // PIECES
    return jnp.concatenate(
        [ref[pl.ds(pl.multiple_of(order[first + r] * deep, deep), deep), :] for r in range(pieces)], axis=0
    )


def grad_lanes(order, first, grt, nlt, gbt, act, gh, att):
    pieces, half = PIECES // 2, gh.shape[1] // 2
    main = [gather(ref, order, first, pieces) for ref in (grt, nlt)]
    side = [gather(ref, order, PIECES + first, pieces) for ref in (nlt, gbt)]
    main = [dot(main[0], act[...]), dot(main[1], gh[:, :half])]
    side = [dot(side[0], gh[:, half:]), dot(side[1], att[...], 1, 1)]
    return jnp.concatenate(main, axis=1), jnp.concatenate(side, axis=1)


def middle_kernel(
    order, me, att_own, att_rcv, wo_own, we_own, wr_own, eb_own, wide,
    output_bias, gain1, shift1, reduce_bias, gain2, shift2, tok, cot, spans,
    layer_out, resid_out, ga_own, ga_other, act_out, gh_out, nlt_out, grt_out, gbt_out, att_out, small,
    keep_out, send_out, wo, we, wr, act_s, gh_s, nlt_s, grt_s, gbt_s, att_s,
):
    i = pl.program_id(0)
    steps = pl.num_programs(0) - 2
    units = we_own.shape[1]
    width = wo_own.shape[0]
    count, depth = tok.shape

    @pl.when(i == 0)
    def _():
        wo[0:width] = wo_own[...]
        wo[width:] = wide[:width, units + 2 * depth :].astype(bf16)
        we[:, 0:units] = we_own[...]
        we[:, units:] = wide[:, :units].astype(bf16)
        wr[0:units] = wr_own[...]
        for j in range(2):
            at = units + j * depth
            wr[at : at + depth] = wide[:, at : at + depth].astype(bf16)
        small[...] = jnp.zeros_like(small)

    @pl.when(i < steps)
    def _():
        base = (me[0] * steps + i) * count
        inside = place_in((spans[0:1], spans[1:2]), (count, 128), base, 0)
        valid = jnp.sum(inside, axis=1, keepdims=True)
        here = pl.ds(pl.multiple_of(i * count, count), count)

        att = jnp.concatenate([att_own[...], att_rcv[...]], axis=0).astype(bf16)
        att_out[...] = att[:width]
        att_s[:, here] = att[width:]
        resid_one = tok[...].astype(f32) + (dot(att, wo[...], 0, 0) + output_bias[...])
        n1, rstd1 = norm(resid_one)
        normed = n1 * gain1[...] + shift1[...]
        normed_low = normed.astype(bf16)
        turned = normed_low.T
        nlt_out[...] = turned
        nlt_s[:, here] = turned
        bias = [wide[width + j : width + j + 1, units + 2 * depth :] for j in range(2)]
        bias = jnp.concatenate([eb_own[...], *bias], axis=1)
        hidden = dot(normed_low, we[...]) + bias
        below, density = normal_parts(hidden)
        active = (hidden * below).astype(bf16)
        slope = below + hidden * density
        act_out[...] = active[:, :units]
        act_s[here, :] = active[:, units:]
        resid_two = normed + (dot(active, wr[...]) + reduce_bias[...])
        n2, rstd2 = norm(resid_two)
        layer_out[...] = ((n2 * gain2[...] + shift2[...]) * valid).astype(bf16).astype(f32)
        grad = cot[...].astype(f32) * valid
        column = lambda v: jnp.sum(v, axis=0, keepdims=True)
        small[0:1, :depth] += column(grad * n2)
        small[1:2, :depth] += column(grad)
        grad_two = norm_back(grad * gain2[...], n2, rstd2)
        grad_result = grad_two.astype(bf16)
        turned = grad_result.T
        grt_out[...] = turned
        grt_s[:, here] = turned
        small[2:3, :depth] += column(grad_result.astype(f32))
        grad_hidden = (dot(grad_result, wr[...], 1, 1) * slope).astype(bf16)
        gh_out[...] = grad_hidden[:, :units]
        gh_s[here, :] = grad_hidden[:, units:]
        small[6:7] += column(grad_hidden.astype(f32))
        grad_normed = grad_two + dot(grad_hidden, we[...], 1, 1)
        small[3:4, :depth] += column(grad_normed * n1)
        small[4:5, :depth] += column(grad_normed)
        grad_one = norm_back(grad_normed * gain1[...], n1, rstd1)
        resid_out[...] = grad_one.T
        grad_branch = grad_one.astype(bf16)
        turned = grad_branch.T
        gbt_out[...] = turned
        gbt_s[:, here] = turned
        small[5:6, :depth] += column(grad_branch.astype(f32))
        grad_att = dot(wo[...], grad_branch, 1, 1).astype(bf16).astype(f32)
        ga_own[...] = grad_att[0:width]
        ga_other[...] = grad_att[width:]

    for first, out in ((0, keep_out), (PIECES // 2, send_out)):

        @pl.when(i == steps + first // (PIECES // 2))
        def _(first=first, out=out):
            main, side = grad_lanes(order, first, grt_s, nlt_s, gbt_s, act_s, gh_s, att_s)
            out[:, : main.shape[1]] = main
            out[:, main.shape[1] :] = side


def middle(order, me, att_own, att_rcv, weights, tokens, cotangent, spans):
    half, depth = tokens.shape[0] // 2, tokens.shape[1]
    width, units = weights[0].shape[0], weights[1].shape[1]
    blk = 256
    steps = half // blk
    at = lambda i: jnp.minimum(i, steps - 1)
    by_row = lambda n: pl.BlockSpec((blk, n), lambda i, *_: (at(i), 0))
    by_col = lambda n: pl.BlockSpec((n, blk), lambda i, *_: (0, at(i)))
    mine = pl.BlockSpec((blk, depth), lambda i, order, me: (me[0] * steps + at(i), 0))
    lanes = 2 * units + width
    outs = [
        (shape((half, depth)), by_row(depth)),
        (pltpu.HBM((depth, half), f32), by_col(depth)),
        (pltpu.HBM((width, half), f32), by_col(width)),
        (shape((width, half)), by_col(width)),
        (shape((half, units), bf16), by_row(units)),
        (shape((half, units), bf16), by_row(units)),
        (shape((depth, half), bf16), by_col(depth)),
        (shape((depth, half), bf16), by_col(depth)),
        (shape((depth, half), bf16), by_col(depth)),
        (shape((width, half), bf16), by_col(width)),
        (shape((8, 2 * units)), None),
        (shape((depth // 2, lanes)), None),
        (shape((depth // 2, lanes)), None),
    ]
    return call(
        middle_kernel,
        [o for o, _ in outs],
        scalars=(order, me),
        arrays=(hbm(att_own), att_rcv, *weights, hbm(tokens), hbm(cotangent), spans),
        in_specs=[
            by_col(width),
            by_col(width),
            *[whole(a) for a in weights],
            mine,
            mine,
            whole(spans),
        ],
        out_specs=[s or whole(o) for o, s in outs],
        grid=(steps + 2,),
        scratch=[
            pltpu.VMEM((2 * width, depth), bf16),
            pltpu.VMEM((depth, 2 * units), bf16),
            pltpu.VMEM((2 * units, depth), bf16),
            pltpu.VMEM((half, units), bf16),
            pltpu.VMEM((half, units), bf16),
            pltpu.VMEM((depth, half), bf16),
            pltpu.VMEM((depth, half), bf16),
            pltpu.VMEM((depth, half), bf16),
            pltpu.VMEM((width, half), bf16),
        ],
        limit=36,
        estimate=cost(20e9, 40e6),
    )


def own_grads_kernel(first, order, grt, nlt, gbt, act, gh, att, got, main, side):
    a, b = grad_lanes(order, first, grt, nlt, gbt, act, gh, att)
    wide = main.shape[1]
    main[...] = a + got[:, :wide]
    side[...] = b + got[:, wide:]


def own_grads(first, order, grt, nlt, gbt, act, gh, att, got, after=()):
    units, width, rows = act.shape[1], att.shape[0], got.shape[0]
    *outs, mark = call(
        functools.partial(own_grads_kernel, first),
        [shape((rows, units + units // 2)), shape((rows, units // 2 + width))],
        scalars=(order,),
        arrays=(grt, nlt, gbt, act, gh, att, got),
        limit=24,
        estimate=cost(1e3, 1e3),
        after=after,
        mark=True,
    )
    return outs, (mark,)


def place_grads_kernel(order, low, high, low_side, high_side, reduce, expand, out, red, outt):
    deep = expand.shape[0] // PIECES
    units, width = red.shape[1], outt.shape[1]
    half = units // 2
    for r in range(PIECES):
        top, of = divmod(r, PIECES // 2)
        of = slice(of * deep, of * deep + deep)
        at = pl.ds(pl.multiple_of(order[r] * deep, deep), deep)
        red[at, :] = (low, high)[top][of, :units]
        expand[at, :half] = (low, high)[top][of, units:]
        at = pl.ds(pl.multiple_of(order[PIECES + r] * deep, deep), deep)
        expand[at, half:] = (low_side, high_side)[top][of, :half]
        outt[at, :] = (low_side, high_side)[top][of, half:]
    reduce[...] = red[...].T
    out[...] = outt[...].T


def place_grads(order, main, side, units, width, after):
    depth = 2 * main[0].shape[0]
    return call(
        place_grads_kernel,
        [pltpu.HBM(d, f32) for d in ((units, depth), (depth, units), (width, depth))],
        scalars=(order,),
        arrays=(*main, *side),
        scratch=[pltpu.VMEM((depth, units), f32), pltpu.VMEM((depth, width), f32)],
        estimate=cost(1e3, 1e3),
        after=after,
        limit=18,
        mark=True,
    )


def prepare_kernel(me, tok_other, tok_own, weight, bias, kt, vaug, tokt):
    half = tok_other.shape[0]
    heads = weight.shape[2] // HD
    lane = lax.broadcasted_iota(jnp.int32, (half, 128), 1)
    ones = jnp.where(lane < HD + 3, 1.0, 0.0)
    for part, tok in enumerate((tok_other, tok_own)):
        at = slice(part * half, (part + 1) * half)
        tokt[:, at] = tok[...].T
        kt[:, at] = dot(weight[1], tok[...], 0, 1).astype(bf16)
        value = (dot(tok[...], weight[2]) + bias[1:2]).astype(bf16).astype(f32)
        for h in range(heads):
            pair = value[:, h // 2 * 128 : h // 2 * 128 + 128]
            if h % 2:
                pair = pltpu.roll(pair, HD, 1)
            vaug[h, at, :] = jnp.where(lane < HD, pair, ones).astype(bf16)


def prepare(me, tokens, weight, bias, after):
    count, depth = tokens.shape
    width = weight.shape[2]
    return call(
        prepare_kernel,
        [shape((width, count), bf16), shape((width // HD, count, 128), bf16), shape((depth, count), bf16)],
        scalars=(me,),
        arrays=(tokens, tokens, weight, bias),
        in_specs=[*halves_of(tokens), whole(weight), whole(bias)],
        limit=10,
        mark=True,
        estimate=cost(1e3, 1e3),
        after=after,
    )


def backward_kernel(
    head, qt, kt, kaug, vaug, seg, logs, att_other, att_own, ga_other, ga_own, dq, dk, dv, dkt, dvt
):
    half = att_other.shape[1]
    slots = seg.shape[0] - 16
    scale = HD**-0.5
    dkt[...] = jnp.zeros_like(dkt)
    dvt[...] = jnp.zeros_like(dvt)
    zeros_q = jnp.zeros((256 - 2 * HD - slots - 16, QB), bf16)
    zeros_v = jnp.zeros((128 - HD - 16, QB), bf16)

    for part, (att, ga) in enumerate(((att_other, ga_other), (att_own, ga_own))):

        def body(i, carry, part=part, att=att, ga=ga):
            place = pl.multiple_of(i * QB, QB)
            at = place + part * half
            grad = ga[:, pl.ds(place, QB)]
            inner = -jnp.sum(grad * att[:, pl.ds(place, QB)], axis=0, keepdims=True)
            grad_low = grad.astype(bf16)
            upper = jnp.concatenate([grad_low, tile_of(*split3(inner)), zeros_v], axis=0)
            query = qt[:, pl.ds(at, QB)]
            logs_q = logs[head : head + 1, pl.ds(at, QB)]
            alone = seg[slots : slots + 1, pl.ds(at, QB)].astype(f32)
            tile = tile_of(alone, *split3(-logs_q))
            left = jnp.concatenate([*scaled_query(query), seg[0:slots, pl.ds(at, QB)], tile, zeros_q], axis=0)
            probs = jnp.exp2(dot(kaug[0], left))
            grad_probs = dot(vaug[0], upper)
            grad_scores = (probs * grad_probs).astype(bf16)
            dvt[...] += dot(grad_low, probs.astype(bf16), 1, 1)
            dkt[...] += dot(query, grad_scores, 1, 1)
            dq[:, pl.ds(at, QB)] = (dot(kt[...], grad_scores) * scale).astype(bf16)
            return carry

        lax.fori_loop(0, half // QB, body, 0)
    dk[...] = (dkt[...] * scale).astype(bf16)
    dv[...] = dvt[...].astype(bf16)


def attend_backward(head, qt, kt, kaug, vaug, seg, logs, att_other, att_own, ga_other, ga_own, after):
    count = qt.shape[1]
    by_head = lambda n: pl.BlockSpec((HD, n), lambda i: (head, 0))
    return call(
        functools.partial(backward_kernel, head),
        [shape((HD, count), bf16)] * 3,
        arrays=(qt, kt, kaug, vaug, seg, logs, att_other, att_own, ga_other, ga_own),
        in_specs=[
            by_head(count),
            by_head(count),
            pl.BlockSpec((1, count, 256), lambda i: (head, 0, 0)),
            pl.BlockSpec((1, count, 128), lambda i: (head, 0, 0)),
            whole(seg),
            whole(logs),
            *[by_head(count // 2)] * 4,
        ],
        scratch=[pltpu.VMEM((HD, count), f32), pltpu.VMEM((HD, count), f32)],
        mark=True,
        limit=18,
        estimate=cost(1e3, 1e3),
        after=after,
    )


def project_grad_kernel(order, tokt, small, *refs):
    *parts, keep, send, full = refs
    rows, lanes = keep.shape
    width = lanes // 3
    for j, part in enumerate(parts):
        full[j * HD : (j + 1) * HD] = part[...]
    column = dot(jnp.ones((8, full.shape[1]), bf16), full[...], 1, 1)
    for first, out in ((0, keep), (PIECES // 2, send)):
        out[: rows - 8] = dot(gather(tokt, order, first, PIECES // 2), full[...], 1, 1)
        out[rows - 8 :] = small[...]
        for j in range(2):
            out[rows - 4 + j : rows - 3 + j, 2 * width :] = column[0:1, 2 * j * width : (2 * j + 1) * width]


def project_grad(order, tokt, small, parts, after):
    depth, count = tokt.shape
    lanes = len(parts) * HD
    return call(
        project_grad_kernel,
        [shape((depth // 2 + 8, lanes))] * 2,
        scalars=(order,),
        arrays=(tokt, small, *parts),
        after=after,
        scratch=[pltpu.VMEM((lanes, count), bf16)],
        limit=12,
        mark=True,
        estimate=cost(1e3, 1e3),
    )


def project_rows_kernel(weight, resid, *refs):
    *parts, out, full = refs
    width, half = weight.shape[2], resid.shape[1]
    for j, part in enumerate(parts):
        full[j * HD : (j + 1) * HD] = part[...]
    total = sum(dot(weight[c], full[c * width : (c + 1) * width, :]) for c in range(weight.shape[0]))
    out[:, :half] = total[:, :half]
    out[:, half:] = total[:, half:] + resid[...]


def project_rows(weight, resid, parts, after):
    depth, count = weight.shape[1], parts[0].shape[1]
    return call(
        project_rows_kernel,
        [shape((depth, count))],
        arrays=(weight, resid, *parts),
        scratch=[pltpu.VMEM((len(parts) * HD, count), bf16)],
        limit=18,
        estimate=cost(1e3, 1e3),
        after=after,
        mark=True,
    )


def place_attend_kernel(order, low, high, small, out, bias, hidden, *vectors):
    deep = out.shape[1] // PIECES
    width = out.shape[2]
    depth = out.shape[1]
    for r in range(PIECES):
        src = (low, high)[r // (PIECES // 2)]
        of = slice(r % (PIECES // 2) * deep, r % (PIECES // 2) * deep + deep)
        at = pl.ds(pl.multiple_of(order[r] * deep, deep), deep)
        for c in range(3):
            out[c, at, :] = src[of, c * width : (c + 1) * width]
    for j in range(2):
        bias[j : j + 1] = small[4 + j : 5 + j, depth:]
    for j in range(hidden.shape[1] // width):
        hidden[:, j * width : (j + 1) * width] = small[j : j + 1, depth:]
    for j, vector in enumerate(vectors):
        vector[...] = small[j : j + 1, :depth]


def place_attend(order, low, high, small, depth, width, units, after):
    return call(
        place_attend_kernel,
        [pltpu.HBM((3, depth, width), f32), shape((2, width)), shape((1, units)), *[shape((1, depth))] * 6],
        scalars=(order,),
        arrays=(low, high, small),
        limit=8,
        after=after,
        estimate=cost(1e3, 1e3),
    )


def add_rows_kernel(me, mine, got, out):
    out[...] = (mine[...] + got[...]).T.astype(bf16)


def add_rows(me, mine, got, after):
    depth, count = mine.shape
    blk = count // 4
    last = lambda i, me: jnp.where(i // 2 == me[0], 2, 0) + i % 2
    first = lambda i, me: jnp.where(i // 2 == me[0], 0, 2) + i % 2
    turned = lambda at: pl.BlockSpec((depth, blk), lambda i, me: (0, at(i, me)))
    return call(
        add_rows_kernel,
        [pltpu.HBM((count, depth), bf16)],
        scalars=(me,),
        arrays=(mine, got),
        grid=(4,),
        in_specs=[turned(last), turned(first)],
        out_specs=[pl.BlockSpec((blk, depth), lambda i, me: (i, 0))],
        limit=12,
        after=after,
        estimate=cost(1e3, 1e3),
        mark=True,
    )


def join_kernel(me, own, other, out):
    mine = pl.program_id(0) == me[0]

    @pl.when(mine)
    def _():
        out[...] = own[...].astype(bf16)

    @pl.when(jnp.logical_not(mine))
    def _():
        out[...] = other[...].astype(bf16)


def join(me, own, other, after=()):
    half, depth = own.shape
    block = pl.BlockSpec((half, depth), lambda i, me: (0, 0))
    return call(
        join_kernel,
        [pltpu.HBM((2 * half, depth), bf16)],
        scalars=(me,),
        arrays=(own, other),
        grid=(2,),
        in_specs=[block, block],
        out_specs=[pl.BlockSpec((half, depth), lambda i, me: (i, 0))],
        estimate=cost(1e3, 1e3),
        limit=14,
        after=after,
        mark=True,
    )


def small_kernel(small, got, out):
    units, lanes = small.shape[1] // 2, out.shape[1]
    depth = lanes * 2 // 3
    wide = lanes - depth
    out[...] = jnp.zeros(out.shape, f32)
    out[0:6, :depth] = small[0:6, :depth] + got[0:6, :depth]
    hidden = small[6:7, :units] + got[6:7, units:]
    for j in range(units // wide):
        out[j : j + 1, depth:] = hidden[:, j * wide : (j + 1) * wide]


def small_rows(small, got, lanes, after):
    return call(
        small_kernel, [shape((8, lanes))], arrays=(small, got), after=after, estimate=cost(1e3, 1e3)
    )[0]


def swap(v):
    return lax.ppermute(v, "mp", [(0, 1), (1, 0)])


MAIN = ((1, 2, 4, 8), (2, 1, 8, 4))
SIDE = ((8, 4, 1, 2), (4, 8, 1, 2))
ATTEND = ((1, 2, 4, 8), (2, 1, 4, 8))


def masks(bits):
    return [sum(bits[3 - b] for b in range(4) if r >> b & 1) for r in range(PIECES)]


def piece_order(groups, which=0):
    table = jnp.array([sum((masks(group[core]) for group in groups), []) for core in (0, 1)], jnp.int32)
    core = lax.axis_index("mp")
    return lax.axis_index("dp").astype(jnp.int32) ^ table[1 - core if which else core]


def across(group, v, position):
    pairs = [
        (2 * d + core, 2 * (d ^ masks(group[core])[position]) + core)
        for d in range(PIECES)
        for core in range(2)
    ]
    return lax.ppermute(v, ("dp", "mp"), pairs)


def stage(body, outs, arrays, after, in_specs=None):
    *outs, mark = call(
        body, [shape(o) for o in outs], arrays=arrays, in_specs=in_specs, after=after, mark=True, limit=12, estimate=cost(1e3, 1e3)
    )
    return outs, (mark,)


def block_of(a, rows, at):
    return pl.BlockSpec((rows, a.shape[1]), lambda *_: (at, 0))


def sum_kernel(counts, extra, *refs):
    arrays, outs = refs[: sum(counts) + (extra and counts[0])], refs[sum(counts) + (extra and counts[0]) :]
    at = 0
    for count, out in zip(counts, outs):
        rows = arrays[at].shape[0]
        out[:rows] = sum(a[...] for a in arrays[at : at + count])
        at += count
    if extra:
        outs[0][rows:] = sum(a[...] for a in arrays[at:])


def halve(chains, after, extra=0, last=False):
    arrays, specs, outs = [], [], []
    for chain in chains:
        rows = chain[0].shape[0] - extra
        size = rows // (PIECES // 2) if last else rows >> (len(chain) - 1)
        specs += [block_of(a, size, 0 if last else 1) for a in chain]
        arrays += chain
        outs.append((size + extra, chain[0].shape[1]))
    if extra:
        specs += [block_of(a, extra, (a.shape[0] - extra) // extra) for a in chains[0]]
        arrays += chains[0]
    return stage(functools.partial(sum_kernel, [len(c) for c in chains], extra), outs, arrays, after, specs)


def quarter_kernel(many, *refs):
    arrays, (own, *parts, small) = refs[: 2 * many], refs[2 * many :]
    size = own.shape[0]
    total = lambda at: sum(a[at] for a in arrays[:many])
    own[...] = total(slice(0, size))
    sums = sum(a[...] for a in arrays[many:])
    small[...] = sums
    for j, part in enumerate(parts):
        part[:size] = total(slice((j + 1) * size, (j + 2) * size))
        part[size:] = sums


def quarters(chain, after, extra):
    rows, lanes = chain[0].shape[0] - extra, chain[0].shape[1]
    size = rows // (PIECES // 2)
    specs = [block_of(a, 4 * size, 0) for a in chain]
    specs += [block_of(a, extra, (a.shape[0] - extra) // extra) for a in chain]
    outs = [(size, lanes), *[(size + extra, lanes)] * 3, (extra, lanes)]
    return stage(functools.partial(quarter_kernel, len(chain)), outs, [*chain, *chain], after, specs)


def piece_kernel(own, a, b, c, small, out, sums):
    size = own.shape[0]
    out[...] = own[...] + a[:size] + b[:size] + c[:size]
    sums[...] = small[...] + a[size:] + b[size:] + c[size:]


def four_kernel(*refs):
    *parts, out = refs
    size = parts[0].shape[0]
    for j, part in enumerate(parts):
        out[j * size : (j + 1) * size] = part[...]


def stack_kernel(*refs):
    count = len(refs) // 3
    for low, high, out in zip(refs[:count], refs[count : 2 * count], refs[2 * count :]):
        rows = low.shape[0]
        out[:rows] = low[...]
        out[rows:] = high[...]


def stack(lows, highs, after):
    outs = [(2 * low.shape[0], low.shape[1]) for low in lows]
    return stage(stack_kernel, outs, [*lows, *highs], after)


def local(
    tokens, seq_starts, seq_lengths, attend_weight, attend_bias, output_weight, output_bias, first_gain, first_shift,
    expand_weight, expand_bias, reduce_weight, reduce_bias, second_gain, second_shift, cotangent,
):
    slots = seq_starts.shape[1]
    units, width, depth = expand_weight.shape[1], output_weight.shape[0], tokens.shape[1]
    by_pieces = lax.axis_size("dp") == PIECES
    me = lax.axis_index("mp").astype(jnp.int32)[None]
    order = order_other = order_p = jnp.arange(2 * PIECES, dtype=jnp.int32) % PIECES
    if by_pieces:
        order, order_other = piece_order((MAIN, SIDE)), piece_order((MAIN, SIDE), 1)
        order_p = piece_order((ATTEND,))
    spans = jnp.concatenate([seq_starts, seq_starts + seq_lengths])
    spans = jnp.pad(spans, ((0, 6), (0, 128 - slots)))
    eb_own = expand_bias[None, :]
    wide_rcv = swap(widen(output_weight, expand_weight, reduce_weight, eb_own))
    vectors = (output_bias, first_gain, first_shift, reduce_bias, second_gain, second_shift)
    vectors = [v[None, :] for v in vectors]

    att_other, att_own, logs, qt, kaug, seg = attend_forward(me, tokens, attend_weight, attend_bias, spans, slots)
    att_rcv = swap(att_other)
    weights = (output_weight, expand_weight, reduce_weight, eb_own, wide_rcv, *vectors)
    (layer_own, resid, ga_own, ga_other, act, gh, nlt, grt, gbt, att, small, keep, send) = middle(
        order_other, me, att_own, att_rcv, weights, tokens, cotangent, spans
    )
    send_rcv, keep_rcv, ga_rcv = swap(send), swap(keep), swap(ga_other)
    small_rcv, layer_rcv = swap(small), swap(layer_own)
    kt, vaug, tokt, mark = prepare(me, tokens, attend_weight, attend_bias, (small,))
    send, mark = own_grads(PIECES // 2, order, grt, nlt, gbt, act, gh, att, send_rcv, (mark,))
    keep, after = own_grads(0, order, grt, nlt, gbt, act, gh, att, keep_rcv, mark)

    heads = []

    def backward(after):
        *head, mark = attend_backward(
            len(heads), qt, kt, kaug, vaug, seg, logs, att_other, att_own, ga_rcv, ga_own, after
        )
        heads.append(head)
        return (mark,)

    count = width // HD
    after = backward(after)
    small = small_rows(small, small_rcv, 3 * width, after)
    layer_out, mark = join(me, layer_own, layer_rcv, (small,))
    after = (mark,)

    def project(after):
        parts = [head[c] for c in range(3) for head in heads]
        keep_p, send_p, mark = project_grad(order_p, tokt, small, parts, after)
        return keep_p, send_p, parts, (mark,)

    if by_pieces:

        def mid(pair, position):
            return [across(group, v, position) for group, v in zip((MAIN, SIDE), pair)]

        def mid_halve(after, last=False):
            return halve([list(chain) for chain in zip(*got)], after, last=last)

        att = functools.partial(across, ATTEND)
        while len(heads) < count - 2:
            after = backward(after)
        got = [keep, mid(send, 8)]
        lead, after = mid_halve(after)
        got.append(mid(lead, 4))
        after = backward(after)
        lead, after = mid_halve(after)
        got.append(mid(lead, 2))
        after = backward(after)
        lead, after = mid_halve(after)
        got.append(mid(lead, 1))
        keep_p, send_p, parts, after = project(after)
        got_p = [keep_p, att(send_p, 8)]
        rows, mark = project_rows(attend_weight, resid, parts, after)
        rows_rcv = swap(rows)
        own, after = mid_halve((mark,), last=True)
        come = mid(own, 1)
        (lead,), after = halve([got_p], after, 8)
        got_p.append(att(lead, 4))
        grad_tokens, mark = add_rows(me, rows, rows_rcv, after)
        (own_p, *parts_p, small), after = quarters(got_p, (mark,), 8)
        come_p = [att(part, j + 1) for j, part in enumerate(parts_p)]
        own, after = stack(own, come, after)
        come = mid(own, 2)
        own, after = stack(own, come, after)
        come = mid(own, 4)
        outs = [own_p.shape, small.shape]
        (own_p, totals), after = stage(piece_kernel, outs, [own_p, *come_p, small], after)
        come_p = [att(own_p, j + 1) for j in range(3)]
        low, after = stack(own, come, after)
        high = mid(low, 8)
        outs = [(4 * own_p.shape[0], own_p.shape[1])]
        (own_p,), after = stage(four_kernel, outs, [own_p, *come_p], after)
        come_p = att(own_p, 4)
        (low_p,), after = stack([own_p], [come_p], after)
        high_p = att(low_p, 8)
    else:
        while len(heads) < count:
            after = backward(after)
        keep_p, send_p, parts, after = project(after)
        rows, mark = project_rows(attend_weight, resid, parts, after)
        grad_tokens, mark = add_rows(me, rows, swap(rows), (mark,))
        low, high, low_p, high_p = lax.psum((keep, send, keep_p, send_p), "dp")
        totals, after = low_p[-8:], (mark,)
    grad_reduce, grad_expand, grad_output, mark = place_grads(order, *zip(low, high), units, width, after)
    grad_attend, grad_bias, grad_hidden, *vectors = place_attend(
        order_p, low_p, high_p, totals, depth, width, units, (mark,)
    )
    vectors = [v.reshape(depth) for v in vectors]
    return (
        layer_out,
        grad_tokens,
        grad_attend,
        grad_bias,
        grad_output,
        vectors[5],
        vectors[3],
        vectors[4],
        grad_expand,
        grad_hidden.reshape(units),
        grad_reduce,
        vectors[2],
        vectors[0],
        vectors[1],
    )


def solution(mesh):
    return jax.shard_map(
        local,
        mesh=mesh,
        in_specs=(
            P("dp", None),
            P("dp", None),
            P("dp", None),
            P(None, None, "mp"),
            P(None, "mp"),
            P("mp", None),
            P(),
            P(),
            P(),
            P(None, "mp"),
            P("mp"),
            P("mp", None),
            P(),
            P(),
            P(),
            P("dp", None),
        ),
        out_specs=(
            P("dp", None),
            P("dp", None),
            P(None, None, "mp"),
            P(None, "mp"),
            P("mp", None),
            P(),
            P(),
            P(),
            P(None, "mp"),
            P("mp"),
            P("mp", None),
            P(),
            P(),
            P(),
        ),
        check_vma=False,
    )
```

```python
import functools
import math

import jax
import jax.numpy as jnp
from jax import lax
from jax.experimental import pallas as pl
from jax.experimental.pallas import tpu as pltpu
from jax.sharding import PartitionSpec as P

HD = 64
EPS = 1e-05
FAR = 1e30
f32 = jnp.float32
bf16 = jnp.bfloat16
QB = 1024
QF = 256
PIECES = 16


def dot(a, b, ca=1, cb=0):
    return lax.dot_general(a, b, (((ca,), (cb,)), ((), ())), preferred_element_type=f32)


def cost(flops, size):
    return pl.CostEstimate(flops=int(flops), bytes_accessed=int(size), transcendentals=0)


def shape(dims, kind=f32):
    return jax.ShapeDtypeStruct(dims, kind)


def whole(a):
    return pl.BlockSpec(a.shape, lambda *_: (0,) * len(a.shape), pipeline_mode=pl.Buffered(1))


def call(body, outs, scalars=(), arrays=(), in_specs=None, out_specs=None, grid=(1,), scratch=(), estimate=None, after=(), limit=10, mark=False):
    n, m, k = len(scalars) + len(arrays), len(after), len(outs)
    outs = list(outs)
    out_specs = list(out_specs or [whole(o) for o in outs])
    if mark:
        outs.append(shape((8, 128)))
        out_specs.append(whole(outs[-1]))

    def kernel(*refs):
        body(*refs[:n], *refs[n + m : n + m + k], *refs[n + m + k + mark :])
        if mark:
            refs[n + m + k][...] = jnp.zeros((8, 128), f32)

    return pl.pallas_call(
        kernel,
        out_shape=outs,
        grid_spec=pltpu.PrefetchScalarGridSpec(
            num_scalar_prefetch=len(scalars),
            grid=grid,
            in_specs=[*(in_specs or [whole(a) for a in arrays]), *[pl.BlockSpec(memory_space=pl.ANY)] * m],
            out_specs=out_specs,
            scratch_shapes=list(scratch),
        ),
        compiler_params=pltpu.CompilerParams(vmem_limit_bytes=limit * 2**20),
        cost_estimate=estimate,
    )(*scalars, *arrays, *after)


def hbm(a):
    return pltpu.with_memory_space_constraint(a, pltpu.HBM)


def widen_kernel(output, expand, low, high, bias, out):
    i = pl.program_id(0)
    units, depth = expand.shape[1], output.shape[1]
    out[:, :units] = expand[...].astype(f32)
    out[:, units : units + depth] = low[...].astype(f32)
    out[:, units + depth : units + 2 * depth] = high[...].astype(f32)

    @pl.when(i < 2)
    def _():
        out[:, units + 2 * depth :] = output[...].astype(f32)

    @pl.when(i >= 2)
    def _():
        out[0:1, units + 2 * depth :] = bias[:, :depth]
        out[1:2, units + 2 * depth :] = bias[:, depth:]


def widen(output, expand, reduce, bias):
    depth, units = expand.shape
    blk = depth // 4
    rows = lambda n, at: pl.BlockSpec((blk, n), at)
    out = shape((depth, units + 3 * depth))
    return call(
        widen_kernel,
        [out],
        arrays=[hbm(a) for a in (output, expand, reduce, reduce, bias)],
        in_specs=[
            rows(depth, lambda i: (jnp.minimum(i, 1), 0)),
            rows(units, lambda i: (i, 0)),
            rows(depth, lambda i: (i, 0)),
            rows(depth, lambda i: (i + 4, 0)),
            whole(bias),
        ],
        out_specs=[rows(out.shape[1], lambda i: (i, 0))],
        grid=(4,),
        estimate=cost(0, 7e6),
        limit=14,
    )[0]


def turned_row(row):
    return jnp.broadcast_to(row, (8, row.shape[1])).T[:, 0:1]


def split3(v):
    high = v.astype(bf16)
    rest = v - high.astype(f32)
    mid = rest.astype(bf16)
    low = rest - mid.astype(f32)
    return high.astype(f32), mid.astype(f32), low


def tile_of(*given):
    row = lax.broadcasted_iota(jnp.int32, (16, given[0].shape[1]), 0)
    out = jnp.zeros(row.shape, f32)
    for j, v in enumerate(given):
        out = jnp.where(row == j, v, out)
    return out.astype(bf16)


def place_in(spans, shape_, base, axis):
    place = lax.broadcasted_iota(jnp.int32, shape_, axis) + base
    return jnp.where((place >= spans[0]) & (place < spans[1]), 1.0, 0.0)


def query_rows(spans, slots, base, count):
    cols = spans.astype(f32).T.astype(jnp.int32)
    inside = place_in((cols[:slots, 0:1], cols[:slots, 1:2]), (slots, count), base, 1)
    alone = 1.0 - jnp.sum(inside, axis=0, keepdims=True)
    return jnp.concatenate([(inside * -FAR).astype(bf16), tile_of(alone * -FAR)], axis=0)


def key_columns(spans, slots, base, count):
    inside = place_in((spans[0:1], spans[1:2]), (count, 128), base, 0)
    used = jnp.sum(inside, axis=1, keepdims=True)
    lane = lax.broadcasted_iota(jnp.int32, (count, 128), 1)
    ones = (lane > slots) & (lane < slots + 4)
    return jnp.where(
        lane < slots, 1.0 - inside, jnp.where(lane == slots, used, jnp.where(ones, 1.0, 0.0))
    )


def scaled_query(query):
    scaled = query.astype(f32) * (math.log2(math.e) / math.sqrt(HD))
    high = scaled.astype(bf16)
    return high, (scaled - high.astype(f32)).astype(bf16)


def forward_kernel(
    slots, me, tok_other, tok_own, weight, bias, spans,
    att_other, own_hbm, log_hbm, qt_hbm, kaug_hbm, seg_hbm, tokens, qhl, vt, segq, sbuf, mbuf,
    att_own, log_out, qt_out, kaug_out, sems,
):
    half = tok_other.shape[0]
    count = 2 * half
    heads = weight.shape[2] // HD
    tokens[0:half] = tok_other[...]
    tokens[half:count] = tok_own[...]
    bases = ((1 - me[0]) * half, me[0] * half)
    for part in range(2):
        at = slice(part * half, (part + 1) * half)
        segq[0 : slots + 16, at] = query_rows(spans[...], slots, bases[part], half)
    segq[slots + 16 :, :] = jnp.zeros((128 - slots - 16, count), bf16)
    bias_q, bias_v = turned_row(bias[0:1]), turned_row(bias[1:2])

    step = 512

    def project(i, carry):
        at = pl.multiple_of(i * step, step)
        rows = tokens[pl.ds(at, step), :]
        query = (dot(weight[0], rows, 0, 1) + bias_q).astype(bf16)
        qt_out[:, pl.ds(at, step)] = query
        high, low = scaled_query(query)
        value = (dot(weight[2], rows, 0, 1) + bias_v).astype(bf16)
        key = dot(rows, weight[1]).astype(bf16).astype(f32)
        base = jnp.where(at < half, bases[0], bases[1] - half) + at
        common = key_columns(spans[...], slots, base, step).astype(bf16)
        lane = lax.broadcasted_iota(jnp.int32, (step, 128), 1)
        for h in range(heads):
            qhl[h * 128 : h * 128 + HD, pl.ds(at, step)] = high[h * HD : (h + 1) * HD]
            qhl[h * 128 + HD : (h + 1) * 128, pl.ds(at, step)] = low[h * HD : (h + 1) * HD]
            vt[h * 80 : h * 80 + HD, pl.ds(at, step)] = value[h * HD : (h + 1) * HD]
            vt[h * 80 + HD : (h + 1) * 80, pl.ds(at, step)] = jnp.ones((16, step), bf16)
            if h % 2 == 0:
                pair = key[:, h * HD : h * HD + 128]
                turned = pltpu.roll(pair, HD, 1)
                twice = (jnp.where(lane < HD, pair, turned), jnp.where(lane < HD, turned, pair))
            kaug_out[h, pl.ds(at, step), 0:128] = twice[h % 2].astype(bf16)
            kaug_out[h, pl.ds(at, step), 128:256] = common
        return carry

    lax.fori_loop(0, count // step, project, 0)
    copies = [
        pltpu.make_async_copy(src, dst, sems.at[j])
        for j, (src, dst) in enumerate(
            ((kaug_out, kaug_hbm), (qt_out, qt_hbm), (segq.at[0 : slots + 16, :], seg_hbm), (log_out, log_hbm), (att_own, own_hbm))
        )
    ]
    for copy in copies[:3]:
        copy.start()

    def score(h, at, slot):
        query = jnp.concatenate([qhl[h * 128 : (h + 1) * 128, pl.ds(at, QF)], segq[:, pl.ds(at, QF)]], axis=0)
        scores = dot(kaug_out[h], query)
        sbuf[slot] = scores
        mbuf[slot] = jnp.max(scores.reshape(count // 8, 8, QF), axis=0)

    def attend(h, at, out, place, slot):
        peak = jnp.max(mbuf[slot], axis=0, keepdims=True)
        probs = jnp.exp2(sbuf[slot] - peak).astype(bf16)
        summed = dot(vt[h * 80 : (h + 1) * 80, :], probs)
        total = summed[HD : HD + 1]
        out[h * HD : (h + 1) * HD, pl.ds(place, QF)] = summed[:HD] / total
        log_out[h : h + 1, pl.ds(at, QF)] = peak + jnp.log2(total)

    score(0, 0, 0)
    for part, out in enumerate((att_other, att_own)):

        def body(i, carry, part=part, out=out):
            place = pl.multiple_of(i * QF, QF)
            at = place + part * half
            for h in range(heads):
                if h + 1 < heads:
                    score(h + 1, at, (h + 1) % 2)
                else:
                    score(0, pl.multiple_of(jnp.minimum(at + QF, count - QF), QF), 0)
                attend(h, at, out, place, h % 2)
            return carry

        lax.fori_loop(0, half // QF, body, 0)
    for copy in copies[3:]:
        copy.start()
    for copy in copies:
        copy.wait()


def halves_of(tokens):
    half, depth = tokens.shape[0] // 2, tokens.shape[1]
    return [
        pl.BlockSpec((half, depth), lambda i, me: (1 - me[0], 0)),
        pl.BlockSpec((half, depth), lambda i, me: (me[0], 0)),
    ]


def attend_forward(me, tokens, weight, bias, spans, slots):
    count, width = tokens.shape[0], weight.shape[2]
    half, heads, depth = count // 2, width // HD, tokens.shape[1]
    kept = [
        ((width, half), f32),
        ((8, count), f32),
        ((width, count), bf16),
        ((heads, count, 256), bf16),
        ((slots + 16, count), bf16),
    ]
    outs = [shape((width, half)), *[pltpu.HBM(*k) for k in kept]]
    rest = (hbm(weight), bias, spans)
    return call(
        functools.partial(forward_kernel, slots),
        outs,
        scalars=(me,),
        arrays=(hbm(tokens), hbm(tokens), *rest),
        in_specs=[*halves_of(tokens), *[whole(a) for a in rest]],
        out_specs=[whole(outs[0]), *[pl.BlockSpec(memory_space=pltpu.HBM)] * 5],
        scratch=[
            pltpu.VMEM((count, depth), bf16),
            pltpu.VMEM((heads * 128, count), bf16),
            pltpu.VMEM((heads * 80, count), bf16),
            pltpu.VMEM((128, count), bf16),
            pltpu.VMEM((2, count, QF), f32),
            pltpu.VMEM((2, 8, QF), f32),
            *[pltpu.VMEM(*k) for k in kept[:4]],
            pltpu.SemaphoreType.DMA((5,)),
        ],
        estimate=cost(20e9, 12e6),
        limit=28,
    )


def norm(v):
    center = v - jnp.mean(v, axis=-1, keepdims=True)
    rstd = lax.rsqrt(jnp.mean(center * center, axis=-1, keepdims=True) + EPS)
    return center * rstd, rstd


def norm_back(grad, n, rstd):
    first = jnp.mean(grad, axis=-1, keepdims=True)
    second = jnp.mean(grad * n, axis=-1, keepdims=True)
    return rstd * (grad - first - n * second)


def normal_parts(h):
    below = 0.5 + 0.5 * lax.erf(h * math.sqrt(0.5))
    bell = jnp.exp2(h * h * (-0.5 * math.log2(math.e)))
    return below, bell * (1.0 / math.sqrt(2.0 * math.pi))


def gather(ref, order, first, pieces):
    deep = ref.shape[0] // PIECES
    return jnp.concatenate(
        [ref[pl.ds(pl.multiple_of(order[first + r] * deep, deep), deep), :] for r in range(pieces)], axis=0
    )


def grad_lanes(order, first, grt, nlt, gbt, act, gh, att):
    pieces, half = PIECES // 2, gh.shape[1] // 2
    main = [gather(ref, order, first, pieces) for ref in (grt, nlt)]
    side = [gather(ref, order, PIECES + first, pieces) for ref in (nlt, gbt)]
    main = [dot(main[0], act[...]), dot(main[1], gh[:, :half])]
    side = [dot(side[0], gh[:, half:]), dot(side[1], att[...], 1, 1)]
    return jnp.concatenate(main, axis=1), jnp.concatenate(side, axis=1)


def middle_kernel(
    order, me, att_own, att_rcv, wo_own, we_own, wr_own, eb_own, wide,
    output_bias, gain1, shift1, reduce_bias, gain2, shift2, tok, cot, spans,
    layer_out, resid_out, ga_own, ga_other, act_out, gh_out, nlt_out, grt_out, gbt_out, att_out, small,
    keep_out, send_out, wo, we, wr, act_s, gh_s, nlt_s, grt_s, gbt_s, att_s,
):
    i = pl.program_id(0)
    steps = pl.num_programs(0) - 2
    units = we_own.shape[1]
    width = wo_own.shape[0]
    count, depth = tok.shape

    @pl.when(i == 0)
    def _():
        wo[...] = wide[:width, units + 2 * depth :].astype(bf16)
        we[...] = wide[:, :units].astype(bf16)
        for j in range(2):
            at = units + j * depth
            wr[j * depth : (j + 1) * depth] = wide[:, at : at + depth].astype(bf16)
        small[...] = jnp.zeros_like(small)

    @pl.when(i < steps)
    def _():
        base = (me[0] * steps + i) * count
        inside = place_in((spans[0:1], spans[1:2]), (count, 128), base, 0)
        valid = jnp.sum(inside, axis=1, keepdims=True)
        here = pl.ds(pl.multiple_of(i * count, count), count)

        att = jnp.concatenate([att_own[...], att_rcv[...]], axis=0).astype(bf16)
        att_out[...] = att[:width]
        att_s[:, here] = att[width:]
        resid_one = tok[...].astype(f32) + (dot(att[:width], wo_own[...], 0, 0) + dot(att[width:], wo[...], 0, 0) + output_bias[...])
        n1, rstd1 = norm(resid_one)
        normed = n1 * gain1[...] + shift1[...]
        normed_low = normed.astype(bf16)
        turned = normed_low.T
        nlt_out[...] = turned
        nlt_s[:, here] = turned
        bias = [wide[width + j : width + j + 1, units + 2 * depth :] for j in range(2)]
        bias = jnp.concatenate([eb_own[...], *bias], axis=1)
        hidden = jnp.concatenate([dot(normed_low, we_own[...]), dot(normed_low, we[...])], axis=1) + bias
        below, density = normal_parts(hidden)
        active = (hidden * below).astype(bf16)
        slope = below + hidden * density
        act_out[...] = active[:, :units]
        act_s[here, :] = active[:, units:]
        result = dot(active[:, :units], wr_own[...]) + dot(active[:, units:], wr[...])
        resid_two = normed + (result + reduce_bias[...])
        n2, rstd2 = norm(resid_two)
        layer_out[...] = ((n2 * gain2[...] + shift2[...]) * valid).astype(bf16).astype(f32)
        grad = cot[...].astype(f32) * valid
        column = lambda v: jnp.sum(v, axis=0, keepdims=True)
        small[0:1, :depth] += column(grad * n2)
        small[1:2, :depth] += column(grad)
        grad_two = norm_back(grad * gain2[...], n2, rstd2)
        grad_result = grad_two.astype(bf16)
        turned = grad_result.T
        grt_out[...] = turned
        grt_s[:, here] = turned
        small[2:3, :depth] += column(grad_result.astype(f32))
        grad_active = [dot(grad_result, w[...], 1, 1) for w in (wr_own, wr)]
        grad_hidden = (jnp.concatenate(grad_active, axis=1) * slope).astype(bf16)
        gh_out[...] = grad_hidden[:, :units]
        gh_s[here, :] = grad_hidden[:, units:]
        small[6:7] += column(grad_hidden.astype(f32))
        back = dot(grad_hidden[:, :units], we_own[...], 1, 1) + dot(grad_hidden[:, units:], we[...], 1, 1)
        grad_normed = grad_two + back
        small[3:4, :depth] += column(grad_normed * n1)
        small[4:5, :depth] += column(grad_normed)
        grad_one = norm_back(grad_normed * gain1[...], n1, rstd1)
        resid_out[...] = grad_one.T
        grad_branch = grad_one.astype(bf16)
        turned = grad_branch.T
        gbt_out[...] = turned
        gbt_s[:, here] = turned
        small[5:6, :depth] += column(grad_branch.astype(f32))
        ga_own[...] = dot(wo_own[...], grad_branch, 1, 1).astype(bf16).astype(f32)
        ga_other[...] = dot(wo[...], grad_branch, 1, 1).astype(bf16).astype(f32)

    for first, out in ((0, keep_out), (PIECES // 2, send_out)):

        @pl.when(i == steps + first // (PIECES // 2))
        def _(first=first, out=out):
            main, side = grad_lanes(order, first, grt_s, nlt_s, gbt_s, act_s, gh_s, att_s)
            out[:, : main.shape[1]] = main
            out[:, main.shape[1] :] = side


def middle(order, me, att_own, att_rcv, weights, tokens, cotangent, spans):
    half, depth = tokens.shape[0] // 2, tokens.shape[1]
    width, units = weights[0].shape[0], weights[1].shape[1]
    blk = 256
    steps = half // blk
    at = lambda i: jnp.minimum(i, steps - 1)
    by_row = lambda n: pl.BlockSpec((blk, n), lambda i, *_: (at(i), 0))
    by_col = lambda n: pl.BlockSpec((n, blk), lambda i, *_: (0, at(i)))
    mine = pl.BlockSpec((blk, depth), lambda i, order, me: (me[0] * steps + at(i), 0))
    lanes = 2 * units + width
    outs = [
        (shape((half, depth)), by_row(depth)),
        (pltpu.HBM((depth, half), f32), by_col(depth)),
        (pltpu.HBM((width, half), f32), by_col(width)),
        (pltpu.HBM((width, half), f32), by_col(width)),
        (shape((half, units), bf16), by_row(units)),
        (shape((half, units), bf16), by_row(units)),
        (shape((depth, half), bf16), by_col(depth)),
        (shape((depth, half), bf16), by_col(depth)),
        (shape((depth, half), bf16), by_col(depth)),
        (shape((width, half), bf16), by_col(width)),
        (shape((8, 2 * units)), None),
        (shape((depth // 2, lanes)), None),
        (shape((depth // 2, lanes)), None),
    ]
    return call(
        middle_kernel,
        [o for o, _ in outs],
        scalars=(order, me),
        arrays=(hbm(att_own), hbm(att_rcv), *weights, hbm(tokens), hbm(cotangent), spans),
        in_specs=[
            by_col(width),
            by_col(width),
            *[whole(a) for a in weights],
            mine,
            mine,
            whole(spans),
        ],
        out_specs=[s or whole(o) for o, s in outs],
        grid=(steps + 2,),
        scratch=[
            pltpu.VMEM((width, depth), bf16),
            pltpu.VMEM((depth, units), bf16),
            pltpu.VMEM((units, depth), bf16),
            pltpu.VMEM((half, units), bf16),
            pltpu.VMEM((half, units), bf16),
            pltpu.VMEM((depth, half), bf16),
            pltpu.VMEM((depth, half), bf16),
            pltpu.VMEM((depth, half), bf16),
            pltpu.VMEM((width, half), bf16),
        ],
        limit=36,
        estimate=cost(20e9, 40e6),
    )


def own_grads_kernel(first, order, grt, nlt, gbt, act, gh, att, got, main, side):
    a, b = grad_lanes(order, first, grt, nlt, gbt, act, gh, att)
    wide = main.shape[1]
    main[...] = a + got[:, :wide]
    side[...] = b + got[:, wide:]


def own_grads(first, order, grt, nlt, gbt, act, gh, att, got, after=()):
    units, width, rows = act.shape[1], att.shape[0], got.shape[0]
    *outs, mark = call(
        functools.partial(own_grads_kernel, first),
        [shape((rows, units + units // 2)), shape((rows, units // 2 + width))],
        scalars=(order,),
        arrays=(grt, nlt, gbt, act, gh, att, got),
        limit=24,
        estimate=cost(1e3, 1e3),
        after=after,
        mark=True,
    )
    return outs, (mark,)


def place_grads_kernel(order, low, high, low_side, high_side, reduce, expand, out, red, outt):
    deep = expand.shape[0] // PIECES
    units, width = red.shape[1], outt.shape[1]
    half = units // 2
    for r in range(PIECES):
        top, of = divmod(r, PIECES // 2)
        of = slice(of * deep, of * deep + deep)
        at = pl.ds(pl.multiple_of(order[r] * deep, deep), deep)
        red[at, :] = (low, high)[top][of, :units]
        expand[at, :half] = (low, high)[top][of, units:]
        at = pl.ds(pl.multiple_of(order[PIECES + r] * deep, deep), deep)
        expand[at, half:] = (low_side, high_side)[top][of, :half]
        outt[at, :] = (low_side, high_side)[top][of, half:]
    reduce[...] = red[...].T
    out[...] = outt[...].T


def place_grads(order, main, side, units, width, after):
    depth = 2 * main[0].shape[0]
    return call(
        place_grads_kernel,
        [pltpu.HBM(d, f32) for d in ((units, depth), (depth, units), (width, depth))],
        scalars=(order,),
        arrays=(*main, *side),
        scratch=[pltpu.VMEM((depth, units), f32), pltpu.VMEM((depth, width), f32)],
        estimate=cost(1e3, 1e3),
        after=after,
        limit=26,
        mark=True,
    )


def prepare_kernel(me, tok_other, tok_own, weight, bias, kt, vaug, tokt):
    half = tok_other.shape[0]
    heads = weight.shape[2] // HD
    lane = lax.broadcasted_iota(jnp.int32, (half, 128), 1)
    ones = jnp.where(lane < HD + 3, 1.0, 0.0)
    for part, tok in enumerate((tok_other, tok_own)):
        at = slice(part * half, (part + 1) * half)
        tokt[:, at] = tok[...].T
        kt[:, at] = dot(weight[1], tok[...], 0, 1).astype(bf16)
        value = (dot(tok[...], weight[2]) + bias[1:2]).astype(bf16).astype(f32)
        for h in range(heads):
            pair = value[:, h // 2 * 128 : h // 2 * 128 + 128]
            if h % 2:
                pair = pltpu.roll(pair, HD, 1)
            vaug[h, at, :] = jnp.where(lane < HD, pair, ones).astype(bf16)


def prepare(me, tokens, weight, bias, after):
    count, depth = tokens.shape
    width = weight.shape[2]
    return call(
        prepare_kernel,
        [shape((width, count), bf16), shape((width // HD, count, 128), bf16), shape((depth, count), bf16)],
        scalars=(me,),
        arrays=(tokens, tokens, weight, bias),
        in_specs=[*halves_of(tokens), whole(weight), whole(bias)],
        limit=10,
        mark=True,
        estimate=cost(1e3, 1e3),
        after=after,
    )


def backward_kernel(
    head, qt, kt, kaug, vaug, seg, logs, att_other, att_own, ga_other, ga_own, dq, dk, dv, dkt, dvt
):
    half = att_other.shape[1]
    slots = seg.shape[0] - 16
    scale = HD**-0.5
    dkt[...] = jnp.zeros_like(dkt)
    dvt[...] = jnp.zeros_like(dvt)
    zeros_q = jnp.zeros((256 - 2 * HD - slots - 16, QB), bf16)
    zeros_v = jnp.zeros((128 - HD - 16, QB), bf16)

    for part, (att, ga) in enumerate(((att_other, ga_other), (att_own, ga_own))):

        def body(i, carry, part=part, att=att, ga=ga):
            place = pl.multiple_of(i * QB, QB)
            at = place + part * half
            grad = ga[:, pl.ds(place, QB)]
            inner = -jnp.sum(grad * att[:, pl.ds(place, QB)], axis=0, keepdims=True)
            grad_low = grad.astype(bf16)
            upper = jnp.concatenate([grad_low, tile_of(*split3(inner)), zeros_v], axis=0)
            query = qt[:, pl.ds(at, QB)]
            logs_q = logs[head : head + 1, pl.ds(at, QB)]
            alone = seg[slots : slots + 1, pl.ds(at, QB)].astype(f32)
            tile = tile_of(alone, *split3(-logs_q))
            left = jnp.concatenate([*scaled_query(query), seg[0:slots, pl.ds(at, QB)], tile, zeros_q], axis=0)
            probs = jnp.exp2(dot(left.T, kaug[0], 1, 1))
            grad_probs = dot(upper.T, vaug[0], 1, 1)
            grad_scores = (probs * grad_probs).astype(bf16)
            dvt[...] += dot(grad_low, probs.astype(bf16))
            dkt[...] += dot(query, grad_scores)
            dq[:, pl.ds(at, QB)] = (dot(kt[...], grad_scores, 1, 1) * scale).astype(bf16)
            return carry

        lax.fori_loop(0, half // QB, body, 0)
    dk[...] = (dkt[...] * scale).astype(bf16)
    dv[...] = dvt[...].astype(bf16)


def attend_backward(head, qt, kt, kaug, vaug, seg, logs, att_other, att_own, ga_other, ga_own, after):
    count = qt.shape[1]
    by_head = lambda n: pl.BlockSpec((HD, n), lambda i: (head, 0))
    return call(
        functools.partial(backward_kernel, head),
        [shape((HD, count), bf16)] * 3,
        arrays=(qt, kt, kaug, vaug, seg, logs, att_other, att_own, ga_other, ga_own),
        in_specs=[
            by_head(count),
            by_head(count),
            pl.BlockSpec((1, count, 256), lambda i: (head, 0, 0)),
            pl.BlockSpec((1, count, 128), lambda i: (head, 0, 0)),
            whole(seg),
            whole(logs),
            *[by_head(count // 2)] * 4,
        ],
        scratch=[pltpu.VMEM((HD, count), f32), pltpu.VMEM((HD, count), f32)],
        mark=True,
        limit=26,
        estimate=cost(1e3, 1e3),
        after=after,
    )


def project_grad_kernel(order, tokt, small, *refs):
    *parts, keep, send, full = refs
    rows, lanes = keep.shape
    width = lanes // 3
    for j, part in enumerate(parts):
        full[j * HD : (j + 1) * HD] = part[...]
    column = dot(jnp.ones((8, full.shape[1]), bf16), full[...], 1, 1)
    for first, out in ((0, keep), (PIECES // 2, send)):
        out[: rows - 8] = dot(gather(tokt, order, first, PIECES // 2), full[...], 1, 1)
        out[rows - 8 :] = small[...]
        for j in range(2):
            out[rows - 4 + j : rows - 3 + j, 2 * width :] = column[0:1, 2 * j * width : (2 * j + 1) * width]


def project_grad(order, tokt, small, parts, after):
    depth, count = tokt.shape
    lanes = len(parts) * HD
    return call(
        project_grad_kernel,
        [shape((depth // 2 + 8, lanes))] * 2,
        scalars=(order,),
        arrays=(tokt, small, *parts),
        after=after,
        scratch=[pltpu.VMEM((lanes, count), bf16)],
        limit=12,
        mark=True,
        estimate=cost(1e3, 1e3),
    )


def project_rows_kernel(weight, resid, *refs):
    *parts, out, full = refs
    width, half = weight.shape[2], resid.shape[1]
    for j, part in enumerate(parts):
        full[j * HD : (j + 1) * HD] = part[...]
    total = sum(dot(weight[c], full[c * width : (c + 1) * width, :]) for c in range(weight.shape[0]))
    out[:, :half] = total[:, :half]
    out[:, half:] = total[:, half:] + resid[...]


def project_rows(weight, resid, parts, after):
    depth, count = weight.shape[1], parts[0].shape[1]
    return call(
        project_rows_kernel,
        [shape((depth, count))],
        arrays=(weight, resid, *parts),
        scratch=[pltpu.VMEM((len(parts) * HD, count), bf16)],
        limit=26,
        estimate=cost(1e3, 1e3),
        after=after,
        mark=True,
    )


def place_attend_kernel(order, low, high, small, out, bias, hidden, *vectors):
    deep = out.shape[1] // PIECES
    width = out.shape[2]
    depth = out.shape[1]
    for r in range(PIECES):
        src = (low, high)[r // (PIECES // 2)]
        of = slice(r % (PIECES // 2) * deep, r % (PIECES // 2) * deep + deep)
        at = pl.ds(pl.multiple_of(order[r] * deep, deep), deep)
        for c in range(3):
            out[c, at, :] = src[of, c * width : (c + 1) * width]
    for j in range(2):
        bias[j : j + 1] = small[4 + j : 5 + j, depth:]
    for j in range(hidden.shape[1] // width):
        hidden[:, j * width : (j + 1) * width] = small[j : j + 1, depth:]
    for j, vector in enumerate(vectors):
        vector[...] = small[j : j + 1, :depth]


def place_attend(order, low, high, small, depth, width, units, after):
    return call(
        place_attend_kernel,
        [pltpu.HBM((3, depth, width), f32), shape((2, width)), shape((1, units)), *[shape((1, depth))] * 6],
        scalars=(order,),
        arrays=(low, high, small),
        limit=8,
        after=after,
        estimate=cost(1e3, 1e3),
    )


def add_rows_kernel(me, mine, got, out):
    out[...] = (mine[...] + got[...]).T.astype(bf16)


def add_rows(me, mine, got, after):
    depth, count = mine.shape
    blk = count // 4
    last = lambda i, me: jnp.where(i // 2 == me[0], 2, 0) + i % 2
    first = lambda i, me: jnp.where(i // 2 == me[0], 0, 2) + i % 2
    turned = lambda at: pl.BlockSpec((depth, blk), lambda i, me: (0, at(i, me)))
    return call(
        add_rows_kernel,
        [pltpu.HBM((count, depth), bf16)],
        scalars=(me,),
        arrays=(mine, got),
        grid=(4,),
        in_specs=[turned(last), turned(first)],
        out_specs=[pl.BlockSpec((blk, depth), lambda i, me: (i, 0))],
        limit=12,
        after=after,
        estimate=cost(1e3, 1e3),
        mark=True,
    )


def join_kernel(me, own, other, out):
    mine = pl.program_id(0) == me[0]

    @pl.when(mine)
    def _():
        out[...] = own[...].astype(bf16)

    @pl.when(jnp.logical_not(mine))
    def _():
        out[...] = other[...].astype(bf16)


def join(me, own, other, after=()):
    half, depth = own.shape
    block = pl.BlockSpec((half, depth), lambda i, me: (0, 0))
    return call(
        join_kernel,
        [pltpu.HBM((2 * half, depth), bf16)],
        scalars=(me,),
        arrays=(own, other),
        grid=(2,),
        in_specs=[block, block],
        out_specs=[pl.BlockSpec((half, depth), lambda i, me: (i, 0))],
        estimate=cost(1e3, 1e3),
        limit=14,
        after=after,
        mark=True,
    )


def small_kernel(small, got, out):
    units, lanes = small.shape[1] // 2, out.shape[1]
    depth = lanes * 2 // 3
    wide = lanes - depth
    out[...] = jnp.zeros(out.shape, f32)
    out[0:6, :depth] = small[0:6, :depth] + got[0:6, :depth]
    hidden = small[6:7, :units] + got[6:7, units:]
    for j in range(units // wide):
        out[j : j + 1, depth:] = hidden[:, j * wide : (j + 1) * wide]


def small_rows(small, got, lanes, after):
    return call(
        small_kernel, [shape((8, lanes))], arrays=(small, got), after=after, estimate=cost(1e3, 1e3)
    )[0]


def swap(v):
    return lax.ppermute(v, "mp", [(0, 1), (1, 0)])


MAIN = ((1, 2, 4, 8), (2, 1, 8, 4))
SIDE = ((8, 4, 1, 2), (4, 8, 1, 2))
ATTEND = ((1, 2, 4, 8), (2, 1, 4, 8))


def masks(bits):
    return [sum(bits[3 - b] for b in range(4) if r >> b & 1) for r in range(PIECES)]


def piece_order(groups, which=0):
    table = jnp.array([sum((masks(group[core]) for group in groups), []) for core in (0, 1)], jnp.int32)
    core = lax.axis_index("mp")
    return lax.axis_index("dp").astype(jnp.int32) ^ table[1 - core if which else core]


def across(group, v, position):
    pairs = [
        (2 * d + core, 2 * (d ^ masks(group[core])[position]) + core)
        for d in range(PIECES)
        for core in range(2)
    ]
    return lax.ppermute(v, ("dp", "mp"), pairs)


def stage(body, outs, arrays, after, in_specs=None):
    *outs, mark = call(
        body, [shape(o) for o in outs], arrays=arrays, in_specs=in_specs, after=after, mark=True, limit=12, estimate=cost(1e3, 1e3)
    )
    return outs, (mark,)


def block_of(a, rows, at):
    return pl.BlockSpec((rows, a.shape[1]), lambda *_: (at, 0))


def sum_kernel(counts, extra, *refs):
    arrays, outs = refs[: sum(counts) + (extra and counts[0])], refs[sum(counts) + (extra and counts[0]) :]
    at = 0
    for count, out in zip(counts, outs):
        rows = arrays[at].shape[0]
        out[:rows] = sum(a[...] for a in arrays[at : at + count])
        at += count
    if extra:
        outs[0][rows:] = sum(a[...] for a in arrays[at:])


def halve(chains, after, extra=0, last=False):
    arrays, specs, outs = [], [], []
    for chain in chains:
        rows = chain[0].shape[0] - extra
        size = rows // (PIECES // 2) if last else rows >> (len(chain) - 1)
        specs += [block_of(a, size, 0 if last else 1) for a in chain]
        arrays += chain
        outs.append((size + extra, chain[0].shape[1]))
    if extra:
        specs += [block_of(a, extra, (a.shape[0] - extra) // extra) for a in chains[0]]
        arrays += chains[0]
    return stage(functools.partial(sum_kernel, [len(c) for c in chains], extra), outs, arrays, after, specs)


def quarter_kernel(many, *refs):
    arrays, (own, *parts, small) = refs[: 2 * many], refs[2 * many :]
    size = own.shape[0]
    total = lambda at: sum(a[at] for a in arrays[:many])
    own[...] = total(slice(0, size))
    sums = sum(a[...] for a in arrays[many:])
    small[...] = sums
    for j, part in enumerate(parts):
        part[:size] = total(slice((j + 1) * size, (j + 2) * size))
        part[size:] = sums


def quarters(chain, after, extra):
    rows, lanes = chain[0].shape[0] - extra, chain[0].shape[1]
    size = rows // (PIECES // 2)
    specs = [block_of(a, 4 * size, 0) for a in chain]
    specs += [block_of(a, extra, (a.shape[0] - extra) // extra) for a in chain]
    outs = [(size, lanes), *[(size + extra, lanes)] * 3, (extra, lanes)]
    return stage(functools.partial(quarter_kernel, len(chain)), outs, [*chain, *chain], after, specs)


def piece_kernel(own, a, b, c, small, out, sums):
    size = own.shape[0]
    out[...] = own[...] + a[:size] + b[:size] + c[:size]
    sums[...] = small[...] + a[size:] + b[size:] + c[size:]


def four_kernel(*refs):
    *parts, out = refs
    size = parts[0].shape[0]
    for j, part in enumerate(parts):
        out[j * size : (j + 1) * size] = part[...]


def stack_kernel(*refs):
    count = len(refs) // 3
    for low, high, out in zip(refs[:count], refs[count : 2 * count], refs[2 * count :]):
        rows = low.shape[0]
        out[:rows] = low[...]
        out[rows:] = high[...]


def stack(lows, highs, after):
    outs = [(2 * low.shape[0], low.shape[1]) for low in lows]
    return stage(stack_kernel, outs, [*lows, *highs], after)


def local(
    tokens, seq_starts, seq_lengths, attend_weight, attend_bias, output_weight, output_bias, first_gain, first_shift,
    expand_weight, expand_bias, reduce_weight, reduce_bias, second_gain, second_shift, cotangent,
):
    slots = seq_starts.shape[1]
    units, width, depth = expand_weight.shape[1], output_weight.shape[0], tokens.shape[1]
    by_pieces = lax.axis_size("dp") == PIECES
    me = lax.axis_index("mp").astype(jnp.int32)[None]
    order = order_other = order_p = jnp.arange(2 * PIECES, dtype=jnp.int32) % PIECES
    if by_pieces:
        order, order_other = piece_order((MAIN, SIDE)), piece_order((MAIN, SIDE), 1)
        order_p = piece_order((ATTEND,))
    spans = jnp.concatenate([seq_starts, seq_starts + seq_lengths])
    spans = jnp.pad(spans, ((0, 6), (0, 128 - slots)))
    eb_own = expand_bias[None, :]
    wide_rcv = swap(widen(output_weight, expand_weight, reduce_weight, eb_own))
    vectors = (output_bias, first_gain, first_shift, reduce_bias, second_gain, second_shift)
    vectors = [v[None, :] for v in vectors]

    att_other, att_own, logs, qt, kaug, seg = attend_forward(me, tokens, attend_weight, attend_bias, spans, slots)
    att_rcv = swap(att_other)
    weights = [hbm(w) for w in (output_weight, expand_weight, reduce_weight)]
    weights = (*weights, eb_own, wide_rcv, *vectors)
    (layer_own, resid, ga_own, ga_other, act, gh, nlt, grt, gbt, att, small, keep, send) = middle(
        order_other, me, att_own, att_rcv, weights, tokens, cotangent, spans
    )
    send_rcv, keep_rcv, ga_rcv = swap(send), swap(keep), swap(ga_other)
    small_rcv, layer_rcv = swap(small), swap(layer_own)
    kt, vaug, tokt, mark = prepare(me, tokens, attend_weight, attend_bias, (small,))
    send, mark = own_grads(PIECES // 2, order, grt, nlt, gbt, act, gh, att, send_rcv, (mark,))
    keep, after = own_grads(0, order, grt, nlt, gbt, act, gh, att, keep_rcv, mark)

    heads = []

    def backward(after):
        *head, mark = attend_backward(
            len(heads), qt, kt, kaug, vaug, seg, logs, att_other, att_own, ga_rcv, ga_own, after
        )
        heads.append(head)
        return (mark,)

    count = width // HD
    after = backward(after)
    small = small_rows(small, small_rcv, 3 * width, after)
    after = (small,)

    def project(after):
        parts = [head[c] for c in range(3) for head in heads]
        keep_p, send_p, mark = project_grad(order_p, tokt, small, parts, after)
        return keep_p, send_p, parts, (mark,)

    if by_pieces:

        def mid(pair, position):
            return [across(group, v, position) for group, v in zip((MAIN, SIDE), pair)]

        def mid_halve(after, last=False):
            return halve([list(chain) for chain in zip(*got)], after, last=last)

        att = functools.partial(across, ATTEND)
        got = [keep, mid(send, 8)]
        layer_out, mark = join(me, layer_own, layer_rcv, after)
        lead, after = mid_halve((mark,))
        got.append(mid(lead, 4))
        after = backward(after)
        lead, after = mid_halve(after)
        got.append(mid(lead, 2))
        after = backward(after)
        lead, after = mid_halve(after)
        got.append(mid(lead, 1))
        after = backward(after)
        own, after = mid_halve(after, last=True)
        come = mid(own, 1)
        keep_p, send_p, parts, after = project(after)
        got_p = [keep_p, att(send_p, 8)]
        rows, mark = project_rows(attend_weight, resid, parts, after)
        rows_rcv = swap(rows)
        (lead,), after = halve([got_p], (mark,), 8)
        got_p.append(att(lead, 4))
        own, after = stack(own, come, after)
        come = mid(own, 2)
        grad_tokens, mark = add_rows(me, rows, rows_rcv, after)
        (own_p, *parts_p, small), after = quarters(got_p, (mark,), 8)
        come_p = [att(part, j + 1) for j, part in enumerate(parts_p)]
        own, after = stack(own, come, after)
        come = mid(own, 4)
        outs = [own_p.shape, small.shape]
        (own_p, totals), after = stage(piece_kernel, outs, [own_p, *come_p, small], after)
        come_p = [att(own_p, j + 1) for j in range(3)]
        low, after = stack(own, come, after)
        high = mid(low, 8)
        outs = [(4 * own_p.shape[0], own_p.shape[1])]
        (own_p,), after = stage(four_kernel, outs, [own_p, *come_p], after)
        come_p = att(own_p, 4)
        (low_p,), after = stack([own_p], [come_p], after)
        high_p = att(low_p, 8)
    else:
        while len(heads) < count:
            after = backward(after)
        keep_p, send_p, parts, after = project(after)
        rows, mark = project_rows(attend_weight, resid, parts, after)
        grad_tokens, mark = add_rows(me, rows, swap(rows), (mark,))
        low, high, low_p, high_p = lax.psum((keep, send, keep_p, send_p), "dp")
        layer_out, mark = join(me, layer_own, layer_rcv, (mark,))
        totals, after = low_p[-8:], (mark,)
    grad_reduce, grad_expand, grad_output, mark = place_grads(order, *zip(low, high), units, width, after)
    grad_attend, grad_bias, grad_hidden, *vectors = place_attend(
        order_p, low_p, high_p, totals, depth, width, units, (mark,)
    )
    vectors = [v.reshape(depth) for v in vectors]
    return (
        layer_out,
        grad_tokens,
        grad_attend,
        grad_bias,
        grad_output,
        vectors[5],
        vectors[3],
        vectors[4],
        grad_expand,
        grad_hidden.reshape(units),
        grad_reduce,
        vectors[2],
        vectors[0],
        vectors[1],
    )


def solution(mesh):
    return jax.shard_map(
        local,
        mesh=mesh,
        in_specs=(
            P("dp", None),
            P("dp", None),
            P("dp", None),
            P(None, None, "mp"),
            P(None, "mp"),
            P("mp", None),
            P(),
            P(),
            P(),
            P(None, "mp"),
            P("mp"),
            P("mp", None),
            P(),
            P(),
            P(),
            P("dp", None),
        ),
        out_specs=(
            P("dp", None),
            P("dp", None),
            P(None, None, "mp"),
            P(None, "mp"),
            P("mp", None),
            P(),
            P(),
            P(),
            P(None, "mp"),
            P("mp"),
            P("mp", None),
            P(),
            P(),
            P(),
        ),
        check_vma=False,
    )
```

```python
import functools
import math

import jax
import jax.numpy as jnp
from jax import lax
from jax.experimental import pallas as pl
from jax.experimental.pallas import tpu as pltpu
from jax.sharding import PartitionSpec as P

HD = 64
EPS = 1e-05
FAR = 1e30
f32 = jnp.float32
bf16 = jnp.bfloat16
QB = 1024
QF = 256
PIECES = 16


def dot(a, b, ca=1, cb=0):
    return lax.dot_general(a, b, (((ca,), (cb,)), ((), ())), preferred_element_type=f32)


def cost(flops, size):
    return pl.CostEstimate(flops=int(flops), bytes_accessed=int(size), transcendentals=0)


def shape(dims, kind=f32):
    return jax.ShapeDtypeStruct(dims, kind)


def whole(a):
    return pl.BlockSpec(a.shape, lambda *_: (0,) * len(a.shape), pipeline_mode=pl.Buffered(1))


def call(body, outs, scalars=(), arrays=(), in_specs=None, out_specs=None, grid=(1,), scratch=(), estimate=None, after=(), limit=10, mark=False):
    n, m, k = len(scalars) + len(arrays), len(after), len(outs)
    outs = list(outs)
    out_specs = list(out_specs or [whole(o) for o in outs])
    if mark:
        outs.append(shape((8, 128)))
        out_specs.append(whole(outs[-1]))

    def kernel(*refs):
        body(*refs[:n], *refs[n + m : n + m + k], *refs[n + m + k + mark :])
        if mark:
            refs[n + m + k][...] = jnp.zeros((8, 128), f32)

    return pl.pallas_call(
        kernel,
        out_shape=outs,
        grid_spec=pltpu.PrefetchScalarGridSpec(
            num_scalar_prefetch=len(scalars),
            grid=grid,
            in_specs=[*(in_specs or [whole(a) for a in arrays]), *[pl.BlockSpec(memory_space=pl.ANY)] * m],
            out_specs=out_specs,
            scratch_shapes=list(scratch),
        ),
        compiler_params=pltpu.CompilerParams(vmem_limit_bytes=limit * 2**20),
        cost_estimate=estimate,
    )(*scalars, *arrays, *after)


def hbm(a):
    return pltpu.with_memory_space_constraint(a, pltpu.HBM)


def widen_kernel(output, expand, low, high, bias, out):
    i = pl.program_id(0)
    units, depth = expand.shape[1], output.shape[1]
    out[:, :units] = expand[...].astype(f32)
    out[:, units : units + depth] = low[...].astype(f32)
    out[:, units + depth : units + 2 * depth] = high[...].astype(f32)

    @pl.when(i < 2)
    def _():
        out[:, units + 2 * depth :] = output[...].astype(f32)

    @pl.when(i >= 2)
    def _():
        out[0:1, units + 2 * depth :] = bias[:, :depth]
        out[1:2, units + 2 * depth :] = bias[:, depth:]


def widen(output, expand, reduce, bias):
    depth, units = expand.shape
    blk = depth // 4
    rows = lambda n, at: pl.BlockSpec((blk, n), at)
    out = shape((depth, units + 3 * depth))
    return call(
        widen_kernel,
        [out],
        arrays=[hbm(a) for a in (output, expand, reduce, reduce, bias)],
        in_specs=[
            rows(depth, lambda i: (jnp.minimum(i, 1), 0)),
            rows(units, lambda i: (i, 0)),
            rows(depth, lambda i: (i, 0)),
            rows(depth, lambda i: (i + 4, 0)),
            whole(bias),
        ],
        out_specs=[rows(out.shape[1], lambda i: (i, 0))],
        grid=(4,),
        estimate=cost(0, 7e6),
        limit=14,
    )[0]


def turned_row(row):
    return jnp.broadcast_to(row, (8, row.shape[1])).T[:, 0:1]


def split3(v):
    high = v.astype(bf16)
    rest = v - high.astype(f32)
    mid = rest.astype(bf16)
    low = rest - mid.astype(f32)
    return high.astype(f32), mid.astype(f32), low


def tile_of(*given):
    row = lax.broadcasted_iota(jnp.int32, (16, given[0].shape[1]), 0)
    out = jnp.zeros(row.shape, f32)
    for j, v in enumerate(given):
        out = jnp.where(row == j, v, out)
    return out.astype(bf16)


def place_in(spans, shape_, base, axis):
    place = lax.broadcasted_iota(jnp.int32, shape_, axis) + base
    return jnp.where((place >= spans[0]) & (place < spans[1]), 1.0, 0.0)


def query_rows(spans, slots, base, count):
    cols = spans.astype(f32).T.astype(jnp.int32)
    inside = place_in((cols[:slots, 0:1], cols[:slots, 1:2]), (slots, count), base, 1)
    alone = 1.0 - jnp.sum(inside, axis=0, keepdims=True)
    return jnp.concatenate([(inside * -FAR).astype(bf16), tile_of(alone * -FAR)], axis=0)


def key_columns(spans, slots, base, count):
    inside = place_in((spans[0:1], spans[1:2]), (count, 128), base, 0)
    used = jnp.sum(inside, axis=1, keepdims=True)
    lane = lax.broadcasted_iota(jnp.int32, (count, 128), 1)
    ones = (lane > slots) & (lane < slots + 4)
    return jnp.where(
        lane < slots, 1.0 - inside, jnp.where(lane == slots, used, jnp.where(ones, 1.0, 0.0))
    )


def scaled_query(query):
    scaled = query.astype(f32) * (math.log2(math.e) / math.sqrt(HD))
    high = scaled.astype(bf16)
    return high, (scaled - high.astype(f32)).astype(bf16)


def forward_kernel(
    slots, me, tok_other, tok_own, weight, bias, spans,
    att_other, own_hbm, log_hbm, qt_hbm, kaug_hbm, seg_hbm, tokens, qhl, vt, segq, sbuf, mbuf,
    att_own, log_out, qt_out, kaug_out, sems,
):
    half = tok_other.shape[0]
    count = 2 * half
    heads = weight.shape[2] // HD
    tokens[0:half] = tok_other[...]
    tokens[half:count] = tok_own[...]
    bases = ((1 - me[0]) * half, me[0] * half)
    for part in range(2):
        at = slice(part * half, (part + 1) * half)
        segq[0 : slots + 16, at] = query_rows(spans[...], slots, bases[part], half)
    segq[slots + 16 :, :] = jnp.zeros((128 - slots - 16, count), bf16)
    bias_q, bias_v = turned_row(bias[0:1]), turned_row(bias[1:2])

    step = 512

    def project(i, carry):
        at = pl.multiple_of(i * step, step)
        rows = tokens[pl.ds(at, step), :]
        query = (dot(weight[0], rows, 0, 1) + bias_q).astype(bf16)
        qt_out[:, pl.ds(at, step)] = query
        high, low = scaled_query(query)
        value = (dot(weight[2], rows, 0, 1) + bias_v).astype(bf16)
        key = dot(rows, weight[1]).astype(bf16).astype(f32)
        base = jnp.where(at < half, bases[0], bases[1] - half) + at
        common = key_columns(spans[...], slots, base, step).astype(bf16)
        lane = lax.broadcasted_iota(jnp.int32, (step, 128), 1)
        for h in range(heads):
            qhl[h * 128 : h * 128 + HD, pl.ds(at, step)] = high[h * HD : (h + 1) * HD]
            qhl[h * 128 + HD : (h + 1) * 128, pl.ds(at, step)] = low[h * HD : (h + 1) * HD]
            vt[h * 80 : h * 80 + HD, pl.ds(at, step)] = value[h * HD : (h + 1) * HD]
            vt[h * 80 + HD : (h + 1) * 80, pl.ds(at, step)] = jnp.ones((16, step), bf16)
            if h % 2 == 0:
                pair = key[:, h * HD : h * HD + 128]
                turned = pltpu.roll(pair, HD, 1)
                twice = (jnp.where(lane < HD, pair, turned), jnp.where(lane < HD, turned, pair))
            kaug_out[h, pl.ds(at, step), 0:128] = twice[h % 2].astype(bf16)
            kaug_out[h, pl.ds(at, step), 128:256] = common
        return carry

    lax.fori_loop(0, count // step, project, 0)
    copies = [
        pltpu.make_async_copy(src, dst, sems.at[j])
        for j, (src, dst) in enumerate(
            ((kaug_out, kaug_hbm), (qt_out, qt_hbm), (segq.at[0 : slots + 16, :], seg_hbm), (log_out, log_hbm), (att_own, own_hbm))
        )
    ]
    for copy in copies[:3]:
        copy.start()

    def score(h, at, slot):
        query = jnp.concatenate([qhl[h * 128 : (h + 1) * 128, pl.ds(at, QF)], segq[:, pl.ds(at, QF)]], axis=0)
        scores = dot(kaug_out[h], query)
        sbuf[slot] = scores
        mbuf[slot] = jnp.max(scores.reshape(count // 8, 8, QF), axis=0)

    def attend(h, at, out, place, slot):
        peak = jnp.max(mbuf[slot], axis=0, keepdims=True)
        probs = jnp.exp2(sbuf[slot] - peak).astype(bf16)
        summed = dot(vt[h * 80 : (h + 1) * 80, :], probs)
        total = summed[HD : HD + 1]
        out[h * HD : (h + 1) * HD, pl.ds(place, QF)] = summed[:HD] / total
        log_out[h : h + 1, pl.ds(at, QF)] = peak + jnp.log2(total)

    score(0, 0, 0)
    for part, out in enumerate((att_other, att_own)):

        def body(i, carry, part=part, out=out):
            place = pl.multiple_of(i * QF, QF)
            at = place + part * half
            for h in range(heads):
                if h + 1 < heads:
                    score(h + 1, at, (h + 1) % 2)
                else:
                    score(0, pl.multiple_of(jnp.minimum(at + QF, count - QF), QF), 0)
                attend(h, at, out, place, h % 2)
            return carry

        lax.fori_loop(0, half // QF, body, 0)
    for copy in copies[3:]:
        copy.start()
    for copy in copies:
        copy.wait()


def halves_of(tokens):
    half, depth = tokens.shape[0] // 2, tokens.shape[1]
    return [
        pl.BlockSpec((half, depth), lambda i, me: (1 - me[0], 0)),
        pl.BlockSpec((half, depth), lambda i, me: (me[0], 0)),
    ]


def attend_forward(me, tokens, weight, bias, spans, slots):
    count, width = tokens.shape[0], weight.shape[2]
    half, heads, depth = count // 2, width // HD, tokens.shape[1]
    kept = [
        ((width, half), f32),
        ((8, count), f32),
        ((width, count), bf16),
        ((heads, count, 256), bf16),
        ((slots + 16, count), bf16),
    ]
    outs = [shape((width, half)), *[pltpu.HBM(*k) for k in kept]]
    rest = (hbm(weight), bias, spans)
    return call(
        functools.partial(forward_kernel, slots),
        outs,
        scalars=(me,),
        arrays=(hbm(tokens), hbm(tokens), *rest),
        in_specs=[*halves_of(tokens), *[whole(a) for a in rest]],
        out_specs=[whole(outs[0]), *[pl.BlockSpec(memory_space=pltpu.HBM)] * 5],
        scratch=[
            pltpu.VMEM((count, depth), bf16),
            pltpu.VMEM((heads * 128, count), bf16),
            pltpu.VMEM((heads * 80, count), bf16),
            pltpu.VMEM((128, count), bf16),
            pltpu.VMEM((2, count, QF), f32),
            pltpu.VMEM((2, 8, QF), f32),
            *[pltpu.VMEM(*k) for k in kept[:4]],
            pltpu.SemaphoreType.DMA((5,)),
        ],
        estimate=cost(20e9, 12e6),
        limit=28,
    )


def norm(v):
    center = v - jnp.mean(v, axis=-1, keepdims=True)
    rstd = lax.rsqrt(jnp.mean(center * center, axis=-1, keepdims=True) + EPS)
    return center * rstd, rstd


def norm_back(grad, n, rstd):
    first = jnp.mean(grad, axis=-1, keepdims=True)
    second = jnp.mean(grad * n, axis=-1, keepdims=True)
    return rstd * (grad - first - n * second)


def normal_parts(h):
    below = 0.5 + 0.5 * lax.erf(h * math.sqrt(0.5))
    bell = jnp.exp2(h * h * (-0.5 * math.log2(math.e)))
    return below, bell * (1.0 / math.sqrt(2.0 * math.pi))


def gather(ref, order, first, pieces):
    deep = ref.shape[0] // PIECES
    return jnp.concatenate(
        [ref[pl.ds(pl.multiple_of(order[first + r] * deep, deep), deep), :] for r in range(pieces)], axis=0
    )


def grad_lanes(order, first, grt, nlt, gbt, act, gh, att):
    pieces, half = PIECES // 2, gh.shape[1] // 2
    main = [gather(ref, order, first, pieces) for ref in (grt, nlt)]
    side = [gather(ref, order, PIECES + first, pieces) for ref in (nlt, gbt)]
    main = [dot(main[0], act[...]), dot(main[1], gh[:, :half])]
    side = [dot(side[0], gh[:, half:]), dot(side[1], att[...], 1, 1)]
    return jnp.concatenate(main, axis=1), jnp.concatenate(side, axis=1)


def middle_kernel(
    order, me, att_own, att_rcv, wo_own, we_own, wr_own, eb_own, wide,
    output_bias, gain1, shift1, reduce_bias, gain2, shift2, tok, cot, spans,
    layer_out, resid_out, ga_own, ga_other, act_out, gh_out, nlt_out, grt_out, gbt_out, att_out, small,
    keep_out, send_out, wo, we, wr, act_s, gh_s, nlt_s, grt_s, gbt_s, att_s,
):
    i = pl.program_id(0)
    steps = pl.num_programs(0) - 2
    units = we_own.shape[1]
    width = wo_own.shape[0]
    count, depth = tok.shape

    @pl.when(i == 0)
    def _():
        wo[...] = wide[:width, units + 2 * depth :].astype(bf16)
        we[...] = wide[:, :units].astype(bf16)
        for j in range(2):
            at = units + j * depth
            wr[j * depth : (j + 1) * depth] = wide[:, at : at + depth].astype(bf16)
        small[...] = jnp.zeros_like(small)

    @pl.when(i < steps)
    def _():
        base = (me[0] * steps + i) * count
        inside = place_in((spans[0:1], spans[1:2]), (count, 128), base, 0)
        valid = jnp.sum(inside, axis=1, keepdims=True)
        here = pl.ds(pl.multiple_of(i * count, count), count)

        att = jnp.concatenate([att_own[...], att_rcv[...]], axis=0).astype(bf16)
        att_out[...] = att[:width]
        att_s[:, here] = att[width:]
        resid_one = tok[...].astype(f32) + (dot(att[:width], wo_own[...], 0, 0) + dot(att[width:], wo[...], 0, 0) + output_bias[...])
        n1, rstd1 = norm(resid_one)
        normed = n1 * gain1[...] + shift1[...]
        normed_low = normed.astype(bf16)
        turned = normed_low.T
        nlt_out[...] = turned
        nlt_s[:, here] = turned
        bias = [wide[width + j : width + j + 1, units + 2 * depth :] for j in range(2)]
        bias = jnp.concatenate([eb_own[...], *bias], axis=1)
        hidden = jnp.concatenate([dot(normed_low, we_own[...]), dot(normed_low, we[...])], axis=1) + bias
        below, density = normal_parts(hidden)
        active = (hidden * below).astype(bf16)
        slope = below + hidden * density
        act_out[...] = active[:, :units]
        act_s[here, :] = active[:, units:]
        result = dot(active[:, :units], wr_own[...]) + dot(active[:, units:], wr[...])
        resid_two = normed + (result + reduce_bias[...])
        n2, rstd2 = norm(resid_two)
        layer_out[...] = ((n2 * gain2[...] + shift2[...]) * valid).astype(bf16).astype(f32)
        grad = cot[...].astype(f32) * valid
        column = lambda v: jnp.sum(v, axis=0, keepdims=True)
        small[0:1, :depth] += column(grad * n2)
        small[1:2, :depth] += column(grad)
        grad_two = norm_back(grad * gain2[...], n2, rstd2)
        grad_result = grad_two.astype(bf16)
        turned = grad_result.T
        grt_out[...] = turned
        grt_s[:, here] = turned
        small[2:3, :depth] += column(grad_result.astype(f32))
        grad_active = [dot(grad_result, w[...], 1, 1) for w in (wr_own, wr)]
        grad_hidden = (jnp.concatenate(grad_active, axis=1) * slope).astype(bf16)
        gh_out[...] = grad_hidden[:, :units]
        gh_s[here, :] = grad_hidden[:, units:]
        small[6:7] += column(grad_hidden.astype(f32))
        back = dot(grad_hidden[:, :units], we_own[...], 1, 1) + dot(grad_hidden[:, units:], we[...], 1, 1)
        grad_normed = grad_two + back
        small[3:4, :depth] += column(grad_normed * n1)
        small[4:5, :depth] += column(grad_normed)
        grad_one = norm_back(grad_normed * gain1[...], n1, rstd1)
        resid_out[...] = grad_one.T
        grad_branch = grad_one.astype(bf16)
        turned = grad_branch.T
        gbt_out[...] = turned
        gbt_s[:, here] = turned
        small[5:6, :depth] += column(grad_branch.astype(f32))
        ga_own[...] = dot(wo_own[...], grad_branch, 1, 1).astype(bf16).astype(f32)
        ga_other[...] = dot(wo[...], grad_branch, 1, 1).astype(bf16).astype(f32)

    for first, out in ((0, keep_out), (PIECES // 2, send_out)):

        @pl.when(i == steps + first // (PIECES // 2))
        def _(first=first, out=out):
            main, side = grad_lanes(order, first, grt_s, nlt_s, gbt_s, act_s, gh_s, att_s)
            out[:, : main.shape[1]] = main
            out[:, main.shape[1] :] = side


def middle(order, me, att_own, att_rcv, weights, tokens, cotangent, spans):
    half, depth = tokens.shape[0] // 2, tokens.shape[1]
    width, units = weights[0].shape[0], weights[1].shape[1]
    blk = 256
    steps = half // blk
    at = lambda i: jnp.minimum(i, steps - 1)
    by_row = lambda n: pl.BlockSpec((blk, n), lambda i, *_: (at(i), 0))
    by_col = lambda n: pl.BlockSpec((n, blk), lambda i, *_: (0, at(i)))
    mine = pl.BlockSpec((blk, depth), lambda i, order, me: (me[0] * steps + at(i), 0))
    lanes = 2 * units + width
    outs = [
        (shape((half, depth)), by_row(depth)),
        (pltpu.HBM((depth, half), f32), by_col(depth)),
        (pltpu.HBM((width, half), f32), by_col(width)),
        (pltpu.HBM((width, half), f32), by_col(width)),
        (shape((half, units), bf16), by_row(units)),
        (shape((half, units), bf16), by_row(units)),
        (shape((depth, half), bf16), by_col(depth)),
        (shape((depth, half), bf16), by_col(depth)),
        (shape((depth, half), bf16), by_col(depth)),
        (shape((width, half), bf16), by_col(width)),
        (shape((8, 2 * units)), None),
        (shape((depth // 2, lanes)), None),
        (shape((depth // 2, lanes)), None),
    ]
    return call(
        middle_kernel,
        [o for o, _ in outs],
        scalars=(order, me),
        arrays=(hbm(att_own), hbm(att_rcv), *weights, hbm(tokens), hbm(cotangent), spans),
        in_specs=[
            by_col(width),
            by_col(width),
            *[whole(a) for a in weights],
            mine,
            mine,
            whole(spans),
        ],
        out_specs=[s or whole(o) for o, s in outs],
        grid=(steps + 2,),
        scratch=[
            pltpu.VMEM((width, depth), bf16),
            pltpu.VMEM((depth, units), bf16),
            pltpu.VMEM((units, depth), bf16),
            pltpu.VMEM((half, units), bf16),
            pltpu.VMEM((half, units), bf16),
            pltpu.VMEM((depth, half), bf16),
            pltpu.VMEM((depth, half), bf16),
            pltpu.VMEM((depth, half), bf16),
            pltpu.VMEM((width, half), bf16),
        ],
        limit=36,
        estimate=cost(20e9, 40e6),
    )


def own_grads_kernel(first, order, grt, nlt, gbt, act, gh, att, got, main, side):
    a, b = grad_lanes(order, first, grt, nlt, gbt, act, gh, att)
    wide = main.shape[1]
    main[...] = a + got[:, :wide]
    side[...] = b + got[:, wide:]


def own_grads(first, order, grt, nlt, gbt, act, gh, att, got, after=()):
    units, width, rows = act.shape[1], att.shape[0], got.shape[0]
    *outs, mark = call(
        functools.partial(own_grads_kernel, first),
        [shape((rows, units + units // 2)), shape((rows, units // 2 + width))],
        scalars=(order,),
        arrays=(grt, nlt, gbt, act, gh, att, got),
        limit=24,
        estimate=cost(1e3, 1e3),
        after=after,
        mark=True,
    )
    return outs, (mark,)


def place_grads_kernel(order, low, high, low_side, high_side, reduce, expand, out, red, outt):
    deep = expand.shape[0] // PIECES
    units, width = red.shape[1], outt.shape[1]
    half = units // 2
    for r in range(PIECES):
        top, of = divmod(r, PIECES // 2)
        of = slice(of * deep, of * deep + deep)
        at = pl.ds(pl.multiple_of(order[r] * deep, deep), deep)
        red[at, :] = (low, high)[top][of, :units]
        expand[at, :half] = (low, high)[top][of, units:]
        at = pl.ds(pl.multiple_of(order[PIECES + r] * deep, deep), deep)
        expand[at, half:] = (low_side, high_side)[top][of, :half]
        outt[at, :] = (low_side, high_side)[top][of, half:]
    reduce[...] = red[...].T
    out[...] = outt[...].T


def place_grads(order, main, side, units, width, after):
    depth = 2 * main[0].shape[0]
    return call(
        place_grads_kernel,
        [pltpu.HBM(d, f32) for d in ((units, depth), (depth, units), (width, depth))],
        scalars=(order,),
        arrays=(*main, *side),
        scratch=[pltpu.VMEM((depth, units), f32), pltpu.VMEM((depth, width), f32)],
        estimate=cost(1e3, 1e3),
        after=after,
        limit=26,
        mark=True,
    )


def prepare_kernel(me, tok_other, tok_own, weight, bias, kt, vaug, tokt):
    half = tok_other.shape[0]
    heads = weight.shape[2] // HD
    lane = lax.broadcasted_iota(jnp.int32, (half, 128), 1)
    ones = jnp.where(lane < HD + 3, 1.0, 0.0)
    for part, tok in enumerate((tok_other, tok_own)):
        at = slice(part * half, (part + 1) * half)
        tokt[:, at] = tok[...].T
        kt[:, at] = dot(weight[1], tok[...], 0, 1).astype(bf16)
        value = (dot(tok[...], weight[2]) + bias[1:2]).astype(bf16).astype(f32)
        for h in range(heads):
            pair = value[:, h // 2 * 128 : h // 2 * 128 + 128]
            if h % 2:
                pair = pltpu.roll(pair, HD, 1)
            vaug[h, at, :] = jnp.where(lane < HD, pair, ones).astype(bf16)


def prepare(me, tokens, weight, bias, after):
    count, depth = tokens.shape
    width = weight.shape[2]
    return call(
        prepare_kernel,
        [shape((width, count), bf16), shape((width // HD, count, 128), bf16), shape((depth, count), bf16)],
        scalars=(me,),
        arrays=(tokens, tokens, weight, bias),
        in_specs=[*halves_of(tokens), whole(weight), whole(bias)],
        limit=10,
        mark=True,
        estimate=cost(1e3, 1e3),
        after=after,
    )


def backward_kernel(
    head, qt, kt, kaug, vaug, seg, logs, att_other, att_own, ga_other, ga_own, dq, dk, dv, dkt, dvt
):
    half = att_other.shape[1]
    slots = seg.shape[0] - 16
    scale = HD**-0.5
    dkt[...] = jnp.zeros_like(dkt)
    dvt[...] = jnp.zeros_like(dvt)
    zeros_q = jnp.zeros((256 - 2 * HD - slots - 16, QB), bf16)
    zeros_v = jnp.zeros((128 - HD - 16, QB), bf16)

    for part, (att, ga) in enumerate(((att_other, ga_other), (att_own, ga_own))):

        def body(i, carry, part=part, att=att, ga=ga):
            place = pl.multiple_of(i * QB, QB)
            at = place + part * half
            grad = ga[:, pl.ds(place, QB)]
            inner = -jnp.sum(grad * att[:, pl.ds(place, QB)], axis=0, keepdims=True)
            grad_low = grad.astype(bf16)
            upper = jnp.concatenate([grad_low, tile_of(*split3(inner)), zeros_v], axis=0)
            query = qt[:, pl.ds(at, QB)]
            logs_q = logs[head : head + 1, pl.ds(at, QB)]
            alone = seg[slots : slots + 1, pl.ds(at, QB)].astype(f32)
            tile = tile_of(alone, *split3(-logs_q))
            left = jnp.concatenate([*scaled_query(query), seg[0:slots, pl.ds(at, QB)], tile, zeros_q], axis=0)
            probs = jnp.exp2(dot(left.T, kaug[0], 1, 1))
            grad_probs = dot(upper.T, vaug[0], 1, 1)
            grad_scores = (probs * grad_probs).astype(bf16)
            dvt[...] += dot(grad_low, probs.astype(bf16))
            dkt[...] += dot(query, grad_scores)
            dq[:, pl.ds(at, QB)] = (dot(kt[...], grad_scores, 1, 1) * scale).astype(bf16)
            return carry

        lax.fori_loop(0, half // QB, body, 0)
    dk[...] = (dkt[...] * scale).astype(bf16)
    dv[...] = dvt[...].astype(bf16)


def attend_backward(head, qt, kt, kaug, vaug, seg, logs, att_other, att_own, ga_other, ga_own, after):
    count = qt.shape[1]
    by_head = lambda n: pl.BlockSpec((HD, n), lambda i: (head, 0))
    return call(
        functools.partial(backward_kernel, head),
        [shape((HD, count), bf16)] * 3,
        arrays=(qt, kt, kaug, vaug, seg, logs, att_other, att_own, ga_other, ga_own),
        in_specs=[
            by_head(count),
            by_head(count),
            pl.BlockSpec((1, count, 256), lambda i: (head, 0, 0)),
            pl.BlockSpec((1, count, 128), lambda i: (head, 0, 0)),
            whole(seg),
            whole(logs),
            *[by_head(count // 2)] * 4,
        ],
        scratch=[pltpu.VMEM((HD, count), f32), pltpu.VMEM((HD, count), f32)],
        mark=True,
        limit=26,
        estimate=cost(1e3, 1e3),
        after=after,
    )


def project_grad_kernel(order, tokt, small, *refs):
    *parts, keep, send, full = refs
    rows, lanes = keep.shape
    width = lanes // 3
    for j, part in enumerate(parts):
        full[j * HD : (j + 1) * HD] = part[...]
    column = dot(jnp.ones((8, full.shape[1]), bf16), full[...], 1, 1)
    for first, out in ((0, keep), (PIECES // 2, send)):
        out[: rows - 8] = dot(gather(tokt, order, first, PIECES // 2), full[...], 1, 1)
        out[rows - 8 :] = small[...]
        for j in range(2):
            out[rows - 4 + j : rows - 3 + j, 2 * width :] = column[0:1, 2 * j * width : (2 * j + 1) * width]


def project_grad(order, tokt, small, parts, after):
    depth, count = tokt.shape
    lanes = len(parts) * HD
    return call(
        project_grad_kernel,
        [shape((depth // 2 + 8, lanes))] * 2,
        scalars=(order,),
        arrays=(tokt, small, *parts),
        after=after,
        scratch=[pltpu.VMEM((lanes, count), bf16)],
        limit=12,
        mark=True,
        estimate=cost(1e3, 1e3),
    )


def project_rows_kernel(weight, resid, *refs):
    *parts, out, full = refs
    width, half = weight.shape[2], resid.shape[1]
    for j, part in enumerate(parts):
        full[j * HD : (j + 1) * HD] = part[...]
    total = sum(dot(weight[c], full[c * width : (c + 1) * width, :]) for c in range(weight.shape[0]))
    out[:, :half] = total[:, :half]
    out[:, half:] = total[:, half:] + resid[...]


def project_rows(weight, resid, parts, after):
    depth, count = weight.shape[1], parts[0].shape[1]
    return call(
        project_rows_kernel,
        [shape((depth, count))],
        arrays=(weight, resid, *parts),
        scratch=[pltpu.VMEM((len(parts) * HD, count), bf16)],
        limit=26,
        estimate=cost(1e3, 1e3),
        after=after,
        mark=True,
    )


def place_attend_kernel(order, low, high, small, out, bias, hidden, *vectors):
    deep = out.shape[1] // PIECES
    width = out.shape[2]
    depth = out.shape[1]
    for r in range(PIECES):
        src = (low, high)[r // (PIECES // 2)]
        of = slice(r % (PIECES // 2) * deep, r % (PIECES // 2) * deep + deep)
        at = pl.ds(pl.multiple_of(order[r] * deep, deep), deep)
        for c in range(3):
            out[c, at, :] = src[of, c * width : (c + 1) * width]
    for j in range(2):
        bias[j : j + 1] = small[4 + j : 5 + j, depth:]
    for j in range(hidden.shape[1] // width):
        hidden[:, j * width : (j + 1) * width] = small[j : j + 1, depth:]
    for j, vector in enumerate(vectors):
        vector[...] = small[j : j + 1, :depth]


def place_attend(order, low, high, small, depth, width, units, after):
    return call(
        place_attend_kernel,
        [pltpu.HBM((3, depth, width), f32), shape((2, width)), shape((1, units)), *[shape((1, depth))] * 6],
        scalars=(order,),
        arrays=(low, high, small),
        limit=8,
        after=after,
        estimate=cost(1e3, 1e3),
    )


def add_rows_kernel(me, mine, got, out):
    out[...] = (mine[...] + got[...]).T.astype(bf16)


def add_rows(me, mine, got, after):
    depth, count = mine.shape
    blk = count // 4
    last = lambda i, me: jnp.where(i // 2 == me[0], 2, 0) + i % 2
    first = lambda i, me: jnp.where(i // 2 == me[0], 0, 2) + i % 2
    turned = lambda at: pl.BlockSpec((depth, blk), lambda i, me: (0, at(i, me)))
    return call(
        add_rows_kernel,
        [pltpu.HBM((count, depth), bf16)],
        scalars=(me,),
        arrays=(mine, got),
        grid=(4,),
        in_specs=[turned(last), turned(first)],
        out_specs=[pl.BlockSpec((blk, depth), lambda i, me: (i, 0))],
        limit=12,
        after=after,
        estimate=cost(1e3, 1e3),
        mark=True,
    )


def join_kernel(me, own, other, out):
    mine = pl.program_id(0) == me[0]

    @pl.when(mine)
    def _():
        out[...] = own[...].astype(bf16)

    @pl.when(jnp.logical_not(mine))
    def _():
        out[...] = other[...].astype(bf16)


def join(me, own, other, after=()):
    half, depth = own.shape
    block = pl.BlockSpec((half, depth), lambda i, me: (0, 0))
    return call(
        join_kernel,
        [pltpu.HBM((2 * half, depth), bf16)],
        scalars=(me,),
        arrays=(own, other),
        grid=(2,),
        in_specs=[block, block],
        out_specs=[pl.BlockSpec((half, depth), lambda i, me: (i, 0))],
        estimate=cost(1e3, 1e3),
        limit=14,
        after=after,
        mark=True,
    )


def small_kernel(small, got, out):
    units, lanes = small.shape[1] // 2, out.shape[1]
    depth = lanes * 2 // 3
    wide = lanes - depth
    out[...] = jnp.zeros(out.shape, f32)
    out[0:6, :depth] = small[0:6, :depth] + got[0:6, :depth]
    hidden = small[6:7, :units] + got[6:7, units:]
    for j in range(units // wide):
        out[j : j + 1, depth:] = hidden[:, j * wide : (j + 1) * wide]


def small_rows(small, got, lanes, after):
    return call(
        small_kernel, [shape((8, lanes))], arrays=(small, got), after=after, estimate=cost(1e3, 1e3)
    )[0]


def swap(v):
    return lax.ppermute(v, "mp", [(0, 1), (1, 0)])


MAIN = ((1, 2, 4, 8), (2, 1, 8, 4))
SIDE = ((8, 4, 1, 2), (4, 8, 1, 2))
ATTEND = ((1, 2, 4, 8), (2, 1, 4, 8))


def masks(bits):
    return [sum(bits[3 - b] for b in range(4) if r >> b & 1) for r in range(PIECES)]


def piece_order(groups, which=0):
    table = jnp.array([sum((masks(group[core]) for group in groups), []) for core in (0, 1)], jnp.int32)
    core = lax.axis_index("mp")
    return lax.axis_index("dp").astype(jnp.int32) ^ table[1 - core if which else core]


def across(group, v, position):
    pairs = [
        (2 * d + core, 2 * (d ^ masks(group[core])[position]) + core)
        for d in range(PIECES)
        for core in range(2)
    ]
    return lax.ppermute(v, ("dp", "mp"), pairs)


def stage(body, outs, arrays, after, in_specs=None):
    *outs, mark = call(
        body, [shape(o) for o in outs], arrays=arrays, in_specs=in_specs, after=after, mark=True, limit=12, estimate=cost(1e3, 1e3)
    )
    return outs, (mark,)


def block_of(a, rows, at):
    return pl.BlockSpec((rows, a.shape[1]), lambda *_: (at, 0))


def sum_kernel(counts, extra, *refs):
    arrays, outs = refs[: sum(counts) + (extra and counts[0])], refs[sum(counts) + (extra and counts[0]) :]
    at = 0
    for count, out in zip(counts, outs):
        rows = arrays[at].shape[0]
        out[:rows] = sum(a[...] for a in arrays[at : at + count])
        at += count
    if extra:
        outs[0][rows:] = sum(a[...] for a in arrays[at:])


def halve(chains, after, extra=0, last=False):
    arrays, specs, outs = [], [], []
    for chain in chains:
        rows = chain[0].shape[0] - extra
        size = rows // (PIECES // 2) if last else rows >> (len(chain) - 1)
        specs += [block_of(a, size, 0 if last else 1) for a in chain]
        arrays += chain
        outs.append((size + extra, chain[0].shape[1]))
    if extra:
        specs += [block_of(a, extra, (a.shape[0] - extra) // extra) for a in chains[0]]
        arrays += chains[0]
    return stage(functools.partial(sum_kernel, [len(c) for c in chains], extra), outs, arrays, after, specs)


def quarter_kernel(many, *refs):
    arrays, (own, *parts, small) = refs[: 2 * many], refs[2 * many :]
    size = own.shape[0]
    total = lambda at: sum(a[at] for a in arrays[:many])
    own[...] = total(slice(0, size))
    sums = sum(a[...] for a in arrays[many:])
    small[...] = sums
    for j, part in enumerate(parts):
        part[:size] = total(slice((j + 1) * size, (j + 2) * size))
        part[size:] = sums


def quarters(chain, after, extra):
    rows, lanes = chain[0].shape[0] - extra, chain[0].shape[1]
    size = rows // (PIECES // 2)
    specs = [block_of(a, 4 * size, 0) for a in chain]
    specs += [block_of(a, extra, (a.shape[0] - extra) // extra) for a in chain]
    outs = [(size, lanes), *[(size + extra, lanes)] * 3, (extra, lanes)]
    return stage(functools.partial(quarter_kernel, len(chain)), outs, [*chain, *chain], after, specs)


def piece_kernel(own, a, b, c, small, out, sums):
    size = own.shape[0]
    out[...] = own[...] + a[:size] + b[:size] + c[:size]
    sums[...] = small[...] + a[size:] + b[size:] + c[size:]


def four_kernel(*refs):
    *parts, out = refs
    size = parts[0].shape[0]
    for j, part in enumerate(parts):
        out[j * size : (j + 1) * size] = part[...]


def stack_kernel(*refs):
    count = len(refs) // 3
    for low, high, out in zip(refs[:count], refs[count : 2 * count], refs[2 * count :]):
        rows = low.shape[0]
        out[:rows] = low[...]
        out[rows:] = high[...]


def stack(lows, highs, after):
    outs = [(2 * low.shape[0], low.shape[1]) for low in lows]
    return stage(stack_kernel, outs, [*lows, *highs], after)


def local(
    tokens, seq_starts, seq_lengths, attend_weight, attend_bias, output_weight, output_bias, first_gain, first_shift,
    expand_weight, expand_bias, reduce_weight, reduce_bias, second_gain, second_shift, cotangent,
):
    slots = seq_starts.shape[1]
    units, width, depth = expand_weight.shape[1], output_weight.shape[0], tokens.shape[1]
    by_pieces = lax.axis_size("dp") == PIECES
    me = lax.axis_index("mp").astype(jnp.int32)[None]
    order = order_other = order_p = jnp.arange(2 * PIECES, dtype=jnp.int32) % PIECES
    if by_pieces:
        order, order_other = piece_order((MAIN, SIDE)), piece_order((MAIN, SIDE), 1)
        order_p = piece_order((ATTEND,))
    spans = jnp.concatenate([seq_starts, seq_starts + seq_lengths])
    spans = jnp.pad(spans, ((0, 6), (0, 128 - slots)))
    eb_own = expand_bias[None, :]
    wide_rcv = swap(widen(output_weight, expand_weight, reduce_weight, eb_own))
    vectors = (output_bias, first_gain, first_shift, reduce_bias, second_gain, second_shift)
    vectors = [v[None, :] for v in vectors]

    att_other, att_own, logs, qt, kaug, seg = attend_forward(me, tokens, attend_weight, attend_bias, spans, slots)
    att_rcv = swap(att_other)
    weights = [hbm(w) for w in (output_weight, expand_weight, reduce_weight)]
    weights = (*weights, eb_own, wide_rcv, *vectors)
    (layer_own, resid, ga_own, ga_other, act, gh, nlt, grt, gbt, att, small, keep, send) = middle(
        order_other, me, att_own, att_rcv, weights, tokens, cotangent, spans
    )
    send_rcv, keep_rcv, ga_rcv = swap(send), swap(keep), swap(ga_other)
    small_rcv, layer_rcv = swap(small), swap(layer_own)
    kt, vaug, tokt, mark = prepare(me, tokens, attend_weight, attend_bias, (small,))
    send, mark = own_grads(PIECES // 2, order, grt, nlt, gbt, act, gh, att, send_rcv, (mark,))
    keep, after = own_grads(0, order, grt, nlt, gbt, act, gh, att, keep_rcv, mark)

    heads = []

    def backward(after):
        *head, mark = attend_backward(
            len(heads), qt, kt, kaug, vaug, seg, logs, att_other, att_own, ga_rcv, ga_own, after
        )
        heads.append(head)
        return (mark,)

    count = width // HD
    after = backward(after)
    small = small_rows(small, small_rcv, 3 * width, after)
    after = (small,)

    def project(after):
        parts = [head[c] for c in range(3) for head in heads]
        keep_p, send_p, mark = project_grad(order_p, tokt, small, parts, after)
        return keep_p, send_p, parts, (mark,)

    if by_pieces:

        def mid(pair, position):
            return [across(group, v, position) for group, v in zip((MAIN, SIDE), pair)]

        def mid_halve(after, last=False):
            return halve([list(chain) for chain in zip(*got)], after, last=last)

        att = functools.partial(across, ATTEND)
        got = [keep, mid(send, 8)]
        layer_out, mark = join(me, layer_own, layer_rcv, after)
        lead, after = mid_halve((mark,))
        got.append(mid(lead, 4))
        after = backward(after)
        lead, after = mid_halve(after)
        got.append(mid(lead, 2))
        after = backward(after)
        lead, after = mid_halve(after)
        got.append(mid(lead, 1))
        after = backward(after)
        own, after = mid_halve(after, last=True)
        come = mid(own, 1)
        keep_p, send_p, parts, after = project(after)
        got_p = [keep_p, att(send_p, 8)]
        rows, mark = project_rows(attend_weight, resid, parts, after)
        rows_rcv = swap(rows)
        (lead,), after = halve([got_p], (mark,), 8)
        got_p.append(att(lead, 4))
        own, after = stack(own, come, after)
        come = mid(own, 2)
        (own_p, *parts_p, small), after = quarters(got_p, after, 8)
        come_p = [att(part, j + 1) for j, part in enumerate(parts_p)]
        grad_tokens, mark = add_rows(me, rows, rows_rcv, after)
        own, after = stack(own, come, (mark,))
        come = mid(own, 4)
        outs = [own_p.shape, small.shape]
        (own_p, totals), after = stage(piece_kernel, outs, [own_p, *come_p, small], after)
        come_p = [att(own_p, j + 1) for j in range(3)]
        low, after = stack(own, come, after)
        high = mid(low, 8)
        outs = [(4 * own_p.shape[0], own_p.shape[1])]
        (own_p,), after = stage(four_kernel, outs, [own_p, *come_p], after)
        come_p = att(own_p, 4)
        (low_p,), after = stack([own_p], [come_p], after)
        high_p = att(low_p, 8)
    else:
        while len(heads) < count:
            after = backward(after)
        keep_p, send_p, parts, after = project(after)
        rows, mark = project_rows(attend_weight, resid, parts, after)
        grad_tokens, mark = add_rows(me, rows, swap(rows), (mark,))
        low, high, low_p, high_p = lax.psum((keep, send, keep_p, send_p), "dp")
        layer_out, mark = join(me, layer_own, layer_rcv, (mark,))
        totals, after = low_p[-8:], (mark,)
    grad_reduce, grad_expand, grad_output, mark = place_grads(order, *zip(low, high), units, width, after)
    grad_attend, grad_bias, grad_hidden, *vectors = place_attend(
        order_p, low_p, high_p, totals, depth, width, units, (mark,)
    )
    vectors = [v.reshape(depth) for v in vectors]
    return (
        layer_out,
        grad_tokens,
        grad_attend,
        grad_bias,
        grad_output,
        vectors[5],
        vectors[3],
        vectors[4],
        grad_expand,
        grad_hidden.reshape(units),
        grad_reduce,
        vectors[2],
        vectors[0],
        vectors[1],
    )


def solution(mesh):
    return jax.shard_map(
        local,
        mesh=mesh,
        in_specs=(
            P("dp", None),
            P("dp", None),
            P("dp", None),
            P(None, None, "mp"),
            P(None, "mp"),
            P("mp", None),
            P(),
            P(),
            P(),
            P(None, "mp"),
            P("mp"),
            P("mp", None),
            P(),
            P(),
            P(),
            P("dp", None),
        ),
        out_specs=(
            P("dp", None),
            P("dp", None),
            P(None, None, "mp"),
            P(None, "mp"),
            P("mp", None),
            P(),
            P(),
            P(),
            P(None, "mp"),
            P("mp"),
            P("mp", None),
            P(),
            P(),
            P(),
        ),
        check_vma=False,
    )
```

```python
import functools
import math

import jax
import jax.numpy as jnp
from jax import lax
from jax.experimental import pallas as pl
from jax.experimental.pallas import tpu as pltpu
from jax.sharding import PartitionSpec as P

HD = 64
EPS = 1e-05
FAR = 1e30
f32 = jnp.float32
bf16 = jnp.bfloat16
QB = 1024
QF = 256
PIECES = 16


def dot(a, b, ca=1, cb=0):
    return lax.dot_general(a, b, (((ca,), (cb,)), ((), ())), preferred_element_type=f32)


def cost(flops, size):
    return pl.CostEstimate(flops=int(flops), bytes_accessed=int(size), transcendentals=0)


def shape(dims, kind=f32):
    return jax.ShapeDtypeStruct(dims, kind)


def whole(a):
    return pl.BlockSpec(a.shape, lambda *_: (0,) * len(a.shape), pipeline_mode=pl.Buffered(1))


def call(body, outs, scalars=(), arrays=(), in_specs=None, out_specs=None, grid=(1,), scratch=(), estimate=None, after=(), limit=10, mark=False):
    n, m, k = len(scalars) + len(arrays), len(after), len(outs)
    outs = list(outs)
    out_specs = list(out_specs or [whole(o) for o in outs])
    if mark:
        outs.append(shape((8, 128)))
        out_specs.append(whole(outs[-1]))

    def kernel(*refs):
        body(*refs[:n], *refs[n + m : n + m + k], *refs[n + m + k + mark :])
        if mark:
            refs[n + m + k][...] = jnp.zeros((8, 128), f32)

    return pl.pallas_call(
        kernel,
        out_shape=outs,
        grid_spec=pltpu.PrefetchScalarGridSpec(
            num_scalar_prefetch=len(scalars),
            grid=grid,
            in_specs=[*(in_specs or [whole(a) for a in arrays]), *[pl.BlockSpec(memory_space=pl.ANY)] * m],
            out_specs=out_specs,
            scratch_shapes=list(scratch),
        ),
        compiler_params=pltpu.CompilerParams(vmem_limit_bytes=limit * 2**20),
        cost_estimate=estimate,
    )(*scalars, *arrays, *after)


def hbm(a):
    return pltpu.with_memory_space_constraint(a, pltpu.HBM)


def widen_kernel(output, expand, low, high, bias, out):
    i = pl.program_id(0)
    units, depth = expand.shape[1], output.shape[1]
    out[:, :units] = expand[...].astype(f32)
    out[:, units : units + depth] = low[...].astype(f32)
    out[:, units + depth : units + 2 * depth] = high[...].astype(f32)

    @pl.when(i == 0)
    def _():
        out[:, units + 2 * depth :] = output[...].astype(f32)

    @pl.when(i == 1)
    def _():
        out[0:1, units + 2 * depth :] = bias[:, :depth]
        out[1:2, units + 2 * depth :] = bias[:, depth:]


def widen(output, expand, reduce, bias):
    depth, units = expand.shape
    blk = depth // 2
    rows = lambda n, at: pl.BlockSpec((blk, n), at)
    out = shape((depth, units + 3 * depth))
    return call(
        widen_kernel,
        [out],
        arrays=[hbm(a) for a in (output, expand, reduce, reduce, bias)],
        in_specs=[
            rows(depth, lambda i: (0, 0)),
            rows(units, lambda i: (i, 0)),
            rows(depth, lambda i: (i, 0)),
            rows(depth, lambda i: (i + 2, 0)),
            whole(bias),
        ],
        out_specs=[rows(out.shape[1], lambda i: (i, 0))],
        grid=(2,),
        estimate=cost(0, 7e6),
        limit=24,
    )[0]


def turned_row(row):
    return jnp.broadcast_to(row, (8, row.shape[1])).T[:, 0:1]


def split3(v):
    high = v.astype(bf16)
    rest = v - high.astype(f32)
    mid = rest.astype(bf16)
    low = rest - mid.astype(f32)
    return high.astype(f32), mid.astype(f32), low


def tile_of(*given):
    row = lax.broadcasted_iota(jnp.int32, (16, given[0].shape[1]), 0)
    out = jnp.zeros(row.shape, f32)
    for j, v in enumerate(given):
        out = jnp.where(row == j, v, out)
    return out.astype(bf16)


def place_in(spans, shape_, base, axis):
    place = lax.broadcasted_iota(jnp.int32, shape_, axis) + base
    return jnp.where((place >= spans[0]) & (place < spans[1]), 1.0, 0.0)


def query_rows(spans, slots, base, count):
    cols = spans.astype(f32).T.astype(jnp.int32)
    inside = place_in((cols[:slots, 0:1], cols[:slots, 1:2]), (slots, count), base, 1)
    alone = 1.0 - jnp.sum(inside, axis=0, keepdims=True)
    return jnp.concatenate([(inside * -FAR).astype(bf16), tile_of(alone * -FAR)], axis=0)


def key_columns(spans, slots, base, count):
    inside = place_in((spans[0:1], spans[1:2]), (count, 128), base, 0)
    used = jnp.sum(inside, axis=1, keepdims=True)
    lane = lax.broadcasted_iota(jnp.int32, (count, 128), 1)
    ones = (lane > slots) & (lane < slots + 4)
    return jnp.where(
        lane < slots, 1.0 - inside, jnp.where(lane == slots, used, jnp.where(ones, 1.0, 0.0))
    )


def scaled_query(query):
    scaled = query.astype(f32) * (math.log2(math.e) / math.sqrt(HD))
    high = scaled.astype(bf16)
    return high, (scaled - high.astype(f32)).astype(bf16)


def forward_kernel(
    slots, me, tok_other, tok_own, weight, bias, spans,
    att_other, own_hbm, log_hbm, qt_hbm, kaug_hbm, seg_hbm, tokens, qhl, vt, segq, sbuf, mbuf,
    att_own, log_out, qt_out, kaug_out, sems,
):
    half = tok_other.shape[0]
    count = 2 * half
    heads = weight.shape[2] // HD
    tokens[0:half] = tok_other[...]
    tokens[half:count] = tok_own[...]
    bases = ((1 - me[0]) * half, me[0] * half)
    for part in range(2):
        at = slice(part * half, (part + 1) * half)
        segq[0 : slots + 16, at] = query_rows(spans[...], slots, bases[part], half)
    segq[slots + 16 :, :] = jnp.zeros((128 - slots - 16, count), bf16)
    bias_q, bias_v = turned_row(bias[0:1]), turned_row(bias[1:2])

    step = 512

    def project(i, carry):
        at = pl.multiple_of(i * step, step)
        rows = tokens[pl.ds(at, step), :]
        query = (dot(weight[0], rows, 0, 1) + bias_q).astype(bf16)
        qt_out[:, pl.ds(at, step)] = query
        high, low = scaled_query(query)
        value = (dot(weight[2], rows, 0, 1) + bias_v).astype(bf16)
        key = dot(rows, weight[1]).astype(bf16).astype(f32)
        base = jnp.where(at < half, bases[0], bases[1] - half) + at
        common = key_columns(spans[...], slots, base, step).astype(bf16)
        lane = lax.broadcasted_iota(jnp.int32, (step, 128), 1)
        for h in range(heads):
            qhl[h * 128 : h * 128 + HD, pl.ds(at, step)] = high[h * HD : (h + 1) * HD]
            qhl[h * 128 + HD : (h + 1) * 128, pl.ds(at, step)] = low[h * HD : (h + 1) * HD]
            vt[h * 80 : h * 80 + HD, pl.ds(at, step)] = value[h * HD : (h + 1) * HD]
            vt[h * 80 + HD : (h + 1) * 80, pl.ds(at, step)] = jnp.ones((16, step), bf16)
            if h % 2 == 0:
                pair = key[:, h * HD : h * HD + 128]
                turned = pltpu.roll(pair, HD, 1)
                twice = (jnp.where(lane < HD, pair, turned), jnp.where(lane < HD, turned, pair))
            kaug_out[h, pl.ds(at, step), 0:128] = twice[h % 2].astype(bf16)
            kaug_out[h, pl.ds(at, step), 128:256] = common
        return carry

    lax.fori_loop(0, count // step, project, 0)
    copies = [
        pltpu.make_async_copy(src, dst, sems.at[j])
        for j, (src, dst) in enumerate(
            ((kaug_out, kaug_hbm), (qt_out, qt_hbm), (segq.at[0 : slots + 16, :], seg_hbm), (log_out, log_hbm), (att_own, own_hbm))
        )
    ]
    for copy in copies[:3]:
        copy.start()

    def score(h, at, slot):
        query = jnp.concatenate([qhl[h * 128 : (h + 1) * 128, pl.ds(at, QF)], segq[:, pl.ds(at, QF)]], axis=0)
        scores = dot(kaug_out[h], query)
        sbuf[slot] = scores
        mbuf[slot] = jnp.max(scores.reshape(count // 8, 8, QF), axis=0)

    def attend(h, at, out, place, slot):
        peak = jnp.max(mbuf[slot], axis=0, keepdims=True)
        probs = jnp.exp2(sbuf[slot] - peak).astype(bf16)
        summed = dot(vt[h * 80 : (h + 1) * 80, :], probs)
        total = summed[HD : HD + 1]
        out[h * HD : (h + 1) * HD, pl.ds(place, QF)] = summed[:HD] / total
        log_out[h : h + 1, pl.ds(at, QF)] = peak + jnp.log2(total)

    score(0, 0, 0)
    for part, out in enumerate((att_other, att_own)):

        def body(i, carry, part=part, out=out):
            place = pl.multiple_of(i * QF, QF)
            at = place + part * half
            for h in range(heads):
                if h + 1 < heads:
                    score(h + 1, at, (h + 1) % 2)
                else:
                    score(0, pl.multiple_of(jnp.minimum(at + QF, count - QF), QF), 0)
                attend(h, at, out, place, h % 2)
            return carry

        lax.fori_loop(0, half // QF, body, 0)
    for copy in copies[3:]:
        copy.start()
    for copy in copies:
        copy.wait()


def halves_of(tokens):
    half, depth = tokens.shape[0] // 2, tokens.shape[1]
    return [
        pl.BlockSpec((half, depth), lambda i, me: (1 - me[0], 0)),
        pl.BlockSpec((half, depth), lambda i, me: (me[0], 0)),
    ]


def attend_forward(me, tokens, weight, bias, spans, slots):
    count, width = tokens.shape[0], weight.shape[2]
    half, heads, depth = count // 2, width // HD, tokens.shape[1]
    kept = [
        ((width, half), f32),
        ((8, count), f32),
        ((width, count), bf16),
        ((heads, count, 256), bf16),
        ((slots + 16, count), bf16),
    ]
    outs = [shape((width, half)), *[pltpu.HBM(*k) for k in kept]]
    rest = (hbm(weight), bias, spans)
    return call(
        functools.partial(forward_kernel, slots),
        outs,
        scalars=(me,),
        arrays=(hbm(tokens), hbm(tokens), *rest),
        in_specs=[*halves_of(tokens), *[whole(a) for a in rest]],
        out_specs=[whole(outs[0]), *[pl.BlockSpec(memory_space=pltpu.HBM)] * 5],
        scratch=[
            pltpu.VMEM((count, depth), bf16),
            pltpu.VMEM((heads * 128, count), bf16),
            pltpu.VMEM((heads * 80, count), bf16),
            pltpu.VMEM((128, count), bf16),
            pltpu.VMEM((2, count, QF), f32),
            pltpu.VMEM((2, 8, QF), f32),
            *[pltpu.VMEM(*k) for k in kept[:4]],
            pltpu.SemaphoreType.DMA((5,)),
        ],
        estimate=cost(20e9, 12e6),
        limit=28,
    )


def norm(v):
    center = v - jnp.mean(v, axis=-1, keepdims=True)
    rstd = lax.rsqrt(jnp.mean(center * center, axis=-1, keepdims=True) + EPS)
    return center * rstd, rstd


def norm_back(grad, n, rstd):
    first = jnp.mean(grad, axis=-1, keepdims=True)
    second = jnp.mean(grad * n, axis=-1, keepdims=True)
    return rstd * (grad - first - n * second)


def normal_parts(h):
    below = 0.5 + 0.5 * lax.erf(h * math.sqrt(0.5))
    bell = jnp.exp2(h * h * (-0.5 * math.log2(math.e)))
    return below, bell * (1.0 / math.sqrt(2.0 * math.pi))


def gather(ref, order, first, pieces):
    deep = ref.shape[0] // PIECES
    return jnp.concatenate(
        [ref[pl.ds(pl.multiple_of(order[first + r] * deep, deep), deep), :] for r in range(pieces)], axis=0
    )


def grad_lanes(order, first, grt, nlt, gbt, act, gh, att):
    pieces, half = PIECES // 2, gh.shape[1] // 2
    main = [gather(ref, order, first, pieces) for ref in (grt, nlt)]
    side = [gather(ref, order, PIECES + first, pieces) for ref in (nlt, gbt)]
    main = [dot(main[0], act[...]), dot(main[1], gh[:, :half])]
    side = [dot(side[0], gh[:, half:]), dot(side[1], att[...], 1, 1)]
    return jnp.concatenate(main, axis=1), jnp.concatenate(side, axis=1)


def middle_kernel(
    order, me, att_own, att_rcv, wo_own, we_own, wr_own, eb_own, wide,
    output_bias, gain1, shift1, reduce_bias, gain2, shift2, tok, cot, spans,
    layer_out, resid_out, ga_own, ga_other, act_out, gh_out, nlt_out, grt_out, gbt_out, att_out, small,
    keep_out, send_out, wo, we, wr, act_s, gh_s, nlt_s, grt_s, gbt_s, att_s,
):
    i = pl.program_id(0)
    steps = pl.num_programs(0) - 2
    units = we_own.shape[1]
    width = wo_own.shape[0]
    count, depth = tok.shape

    @pl.when(i == 0)
    def _():
        wo[...] = wide[:width, units + 2 * depth :].astype(bf16)
        we[...] = wide[:, :units].astype(bf16)
        for j in range(2):
            at = units + j * depth
            wr[j * depth : (j + 1) * depth] = wide[:, at : at + depth].astype(bf16)
        small[...] = jnp.zeros_like(small)

    @pl.when(i < steps)
    def _():
        base = (me[0] * steps + i) * count
        inside = place_in((spans[0:1], spans[1:2]), (count, 128), base, 0)
        valid = jnp.sum(inside, axis=1, keepdims=True)
        here = pl.ds(pl.multiple_of(i * count, count), count)

        att = jnp.concatenate([att_own[...], att_rcv[...]], axis=0).astype(bf16)
        att_out[...] = att[:width]
        att_s[:, here] = att[width:]
        resid_one = tok[...].astype(f32) + (dot(att[:width], wo_own[...], 0, 0) + dot(att[width:], wo[...], 0, 0) + output_bias[...])
        n1, rstd1 = norm(resid_one)
        normed = n1 * gain1[...] + shift1[...]
        normed_low = normed.astype(bf16)
        turned = normed_low.T
        nlt_out[...] = turned
        nlt_s[:, here] = turned
        bias = [wide[width + j : width + j + 1, units + 2 * depth :] for j in range(2)]
        bias = jnp.concatenate([eb_own[...], *bias], axis=1)
        hidden = jnp.concatenate([dot(normed_low, we_own[...]), dot(normed_low, we[...])], axis=1) + bias
        below, density = normal_parts(hidden)
        active = (hidden * below).astype(bf16)
        slope = below + hidden * density
        act_out[...] = active[:, :units]
        act_s[here, :] = active[:, units:]
        result = dot(active[:, :units], wr_own[...]) + dot(active[:, units:], wr[...])
        resid_two = normed + (result + reduce_bias[...])
        n2, rstd2 = norm(resid_two)
        layer_out[...] = ((n2 * gain2[...] + shift2[...]) * valid).astype(bf16).astype(f32)
        grad = cot[...].astype(f32) * valid
        column = lambda v: jnp.sum(v, axis=0, keepdims=True)
        small[0:1, :depth] += column(grad * n2)
        small[1:2, :depth] += column(grad)
        grad_two = norm_back(grad * gain2[...], n2, rstd2)
        grad_result = grad_two.astype(bf16)
        turned = grad_result.T
        grt_out[...] = turned
        grt_s[:, here] = turned
        small[2:3, :depth] += column(grad_result.astype(f32))
        grad_active = [dot(grad_result, w[...], 1, 1) for w in (wr_own, wr)]
        grad_hidden = (jnp.concatenate(grad_active, axis=1) * slope).astype(bf16)
        gh_out[...] = grad_hidden[:, :units]
        gh_s[here, :] = grad_hidden[:, units:]
        small[6:7] += column(grad_hidden.astype(f32))
        back = dot(grad_hidden[:, :units], we_own[...], 1, 1) + dot(grad_hidden[:, units:], we[...], 1, 1)
        grad_normed = grad_two + back
        small[3:4, :depth] += column(grad_normed * n1)
        small[4:5, :depth] += column(grad_normed)
        grad_one = norm_back(grad_normed * gain1[...], n1, rstd1)
        resid_out[...] = grad_one.T
        grad_branch = grad_one.astype(bf16)
        turned = grad_branch.T
        gbt_out[...] = turned
        gbt_s[:, here] = turned
        small[5:6, :depth] += column(grad_branch.astype(f32))
        ga_own[...] = dot(wo_own[...], grad_branch, 1, 1).astype(bf16).astype(f32)
        ga_other[...] = dot(wo[...], grad_branch, 1, 1).astype(bf16).astype(f32)

    for first, out in ((0, keep_out), (PIECES // 2, send_out)):

        @pl.when(i == steps + first // (PIECES // 2))
        def _(first=first, out=out):
            main, side = grad_lanes(order, first, grt_s, nlt_s, gbt_s, act_s, gh_s, att_s)
            out[:, : main.shape[1]] = main
            out[:, main.shape[1] :] = side


def middle(order, me, att_own, att_rcv, weights, tokens, cotangent, spans):
    half, depth = tokens.shape[0] // 2, tokens.shape[1]
    width, units = weights[0].shape[0], weights[1].shape[1]
    blk = 256
    steps = half // blk
    at = lambda i: jnp.minimum(i, steps - 1)
    by_row = lambda n: pl.BlockSpec((blk, n), lambda i, *_: (at(i), 0))
    by_col = lambda n: pl.BlockSpec((n, blk), lambda i, *_: (0, at(i)))
    mine = pl.BlockSpec((blk, depth), lambda i, order, me: (me[0] * steps + at(i), 0))
    lanes = 2 * units + width
    outs = [
        (shape((half, depth)), by_row(depth)),
        (pltpu.HBM((depth, half), f32), by_col(depth)),
        (pltpu.HBM((width, half), f32), by_col(width)),
        (pltpu.HBM((width, half), f32), by_col(width)),
        (shape((half, units), bf16), by_row(units)),
        (shape((half, units), bf16), by_row(units)),
        (shape((depth, half), bf16), by_col(depth)),
        (shape((depth, half), bf16), by_col(depth)),
        (shape((depth, half), bf16), by_col(depth)),
        (shape((width, half), bf16), by_col(width)),
        (shape((8, 2 * units)), None),
        (shape((depth // 2, lanes)), None),
        (shape((depth // 2, lanes)), None),
    ]
    return call(
        middle_kernel,
        [o for o, _ in outs],
        scalars=(order, me),
        arrays=(hbm(att_own), hbm(att_rcv), *weights, hbm(tokens), hbm(cotangent), spans),
        in_specs=[
            by_col(width),
            by_col(width),
            *[whole(a) for a in weights],
            mine,
            mine,
            whole(spans),
        ],
        out_specs=[s or whole(o) for o, s in outs],
        grid=(steps + 2,),
        scratch=[
            pltpu.VMEM((width, depth), bf16),
            pltpu.VMEM((depth, units), bf16),
            pltpu.VMEM((units, depth), bf16),
            pltpu.VMEM((half, units), bf16),
            pltpu.VMEM((half, units), bf16),
            pltpu.VMEM((depth, half), bf16),
            pltpu.VMEM((depth, half), bf16),
            pltpu.VMEM((depth, half), bf16),
            pltpu.VMEM((width, half), bf16),
        ],
        limit=36,
        estimate=cost(20e9, 40e6),
    )


def own_grads_kernel(first, order, grt, nlt, gbt, act, gh, att, got, main, side):
    a, b = grad_lanes(order, first, grt, nlt, gbt, act, gh, att)
    wide = main.shape[1]
    main[...] = a + got[:, :wide]
    side[...] = b + got[:, wide:]


def own_grads(first, order, grt, nlt, gbt, act, gh, att, got, after=()):
    units, width, rows = act.shape[1], att.shape[0], got.shape[0]
    *outs, mark = call(
        functools.partial(own_grads_kernel, first),
        [shape((rows, units + units // 2)), shape((rows, units // 2 + width))],
        scalars=(order,),
        arrays=(grt, nlt, gbt, act, gh, att, got),
        limit=24,
        estimate=cost(1e3, 1e3),
        after=after,
        mark=True,
    )
    return outs, (mark,)


def place_grads_kernel(order, low, high, low_side, high_side, reduce, expand, out, red, outt):
    deep = expand.shape[0] // PIECES
    units, width = red.shape[1], outt.shape[1]
    half = units // 2
    for r in range(PIECES):
        top, of = divmod(r, PIECES // 2)
        of = slice(of * deep, of * deep + deep)
        at = pl.ds(pl.multiple_of(order[r] * deep, deep), deep)
        red[at, :] = (low, high)[top][of, :units]
        expand[at, :half] = (low, high)[top][of, units:]
        at = pl.ds(pl.multiple_of(order[PIECES + r] * deep, deep), deep)
        expand[at, half:] = (low_side, high_side)[top][of, :half]
        outt[at, :] = (low_side, high_side)[top][of, half:]
    reduce[...] = red[...].T
    out[...] = outt[...].T


def place_grads(order, main, side, units, width, after):
    depth = 2 * main[0].shape[0]
    return call(
        place_grads_kernel,
        [pltpu.HBM(d, f32) for d in ((units, depth), (depth, units), (width, depth))],
        scalars=(order,),
        arrays=(*main, *side),
        scratch=[pltpu.VMEM((depth, units), f32), pltpu.VMEM((depth, width), f32)],
        estimate=cost(1e3, 1e3),
        after=after,
        limit=26,
        mark=True,
    )


def prepare_kernel(me, tok_other, tok_own, weight, bias, kt, vaug, tokt):
    half = tok_other.shape[0]
    heads = weight.shape[2] // HD
    lane = lax.broadcasted_iota(jnp.int32, (half, 128), 1)
    ones = jnp.where(lane < HD + 3, 1.0, 0.0)
    for part, tok in enumerate((tok_other, tok_own)):
        at = slice(part * half, (part + 1) * half)
        tokt[:, at] = tok[...].T
        kt[:, at] = dot(weight[1], tok[...], 0, 1).astype(bf16)
        value = (dot(tok[...], weight[2]) + bias[1:2]).astype(bf16).astype(f32)
        for h in range(heads):
            pair = value[:, h // 2 * 128 : h // 2 * 128 + 128]
            if h % 2:
                pair = pltpu.roll(pair, HD, 1)
            vaug[h, at, :] = jnp.where(lane < HD, pair, ones).astype(bf16)


def prepare(me, tokens, weight, bias, after):
    count, depth = tokens.shape
    width = weight.shape[2]
    return call(
        prepare_kernel,
        [shape((width, count), bf16), shape((width // HD, count, 128), bf16), shape((depth, count), bf16)],
        scalars=(me,),
        arrays=(tokens, tokens, weight, bias),
        in_specs=[*halves_of(tokens), whole(weight), whole(bias)],
        limit=10,
        mark=True,
        estimate=cost(1e3, 1e3),
        after=after,
    )


def backward_kernel(
    head, qt, kt, kaug, vaug, seg, logs, att_other, att_own, ga_other, ga_own, dq, dk, dv, dkt, dvt
):
    half = att_other.shape[1]
    slots = seg.shape[0] - 16
    scale = HD**-0.5
    dkt[...] = jnp.zeros_like(dkt)
    dvt[...] = jnp.zeros_like(dvt)
    zeros_q = jnp.zeros((256 - 2 * HD - slots - 16, QB), bf16)
    zeros_v = jnp.zeros((128 - HD - 16, QB), bf16)

    for part, (att, ga) in enumerate(((att_other, ga_other), (att_own, ga_own))):

        def body(i, carry, part=part, att=att, ga=ga):
            place = pl.multiple_of(i * QB, QB)
            at = place + part * half
            grad = ga[:, pl.ds(place, QB)]
            inner = -jnp.sum(grad * att[:, pl.ds(place, QB)], axis=0, keepdims=True)
            grad_low = grad.astype(bf16)
            upper = jnp.concatenate([grad_low, tile_of(*split3(inner)), zeros_v], axis=0)
            query = qt[:, pl.ds(at, QB)]
            logs_q = logs[head : head + 1, pl.ds(at, QB)]
            alone = seg[slots : slots + 1, pl.ds(at, QB)].astype(f32)
            tile = tile_of(alone, *split3(-logs_q))
            left = jnp.concatenate([*scaled_query(query), seg[0:slots, pl.ds(at, QB)], tile, zeros_q], axis=0)
            probs = jnp.exp2(dot(left.T, kaug[0], 1, 1))
            grad_probs = dot(upper.T, vaug[0], 1, 1)
            grad_scores = (probs * grad_probs).astype(bf16)
            dvt[...] += dot(grad_low, probs.astype(bf16))
            dkt[...] += dot(query, grad_scores)
            dq[:, pl.ds(at, QB)] = (dot(kt[...], grad_scores, 1, 1) * scale).astype(bf16)
            return carry

        lax.fori_loop(0, half // QB, body, 0)
    dk[...] = (dkt[...] * scale).astype(bf16)
    dv[...] = dvt[...].astype(bf16)


def attend_backward(head, qt, kt, kaug, vaug, seg, logs, att_other, att_own, ga_other, ga_own, after):
    count = qt.shape[1]
    by_head = lambda n: pl.BlockSpec((HD, n), lambda i: (head, 0))
    return call(
        functools.partial(backward_kernel, head),
        [shape((HD, count), bf16)] * 3,
        arrays=(qt, kt, kaug, vaug, seg, logs, att_other, att_own, ga_other, ga_own),
        in_specs=[
            by_head(count),
            by_head(count),
            pl.BlockSpec((1, count, 256), lambda i: (head, 0, 0)),
            pl.BlockSpec((1, count, 128), lambda i: (head, 0, 0)),
            whole(seg),
            whole(logs),
            *[by_head(count // 2)] * 4,
        ],
        scratch=[pltpu.VMEM((HD, count), f32), pltpu.VMEM((HD, count), f32)],
        mark=True,
        limit=26,
        estimate=cost(1e3, 1e3),
        after=after,
    )


def project_grad_kernel(order, tokt, small, *refs):
    *parts, keep, send, full = refs
    rows, lanes = keep.shape
    width = lanes // 3
    for j, part in enumerate(parts):
        full[j * HD : (j + 1) * HD] = part[...]
    column = dot(jnp.ones((8, full.shape[1]), bf16), full[...], 1, 1)
    for first, out in ((0, keep), (PIECES // 2, send)):
        out[: rows - 8] = dot(gather(tokt, order, first, PIECES // 2), full[...], 1, 1)
        out[rows - 8 :] = small[...]
        for j in range(2):
            out[rows - 4 + j : rows - 3 + j, 2 * width :] = column[0:1, 2 * j * width : (2 * j + 1) * width]


def project_grad(order, tokt, small, parts, after):
    depth, count = tokt.shape
    lanes = len(parts) * HD
    return call(
        project_grad_kernel,
        [shape((depth // 2 + 8, lanes))] * 2,
        scalars=(order,),
        arrays=(tokt, small, *parts),
        after=after,
        scratch=[pltpu.VMEM((lanes, count), bf16)],
        limit=12,
        mark=True,
        estimate=cost(1e3, 1e3),
    )


def project_rows_kernel(weight, resid, *refs):
    *parts, out, full = refs
    width, half = weight.shape[2], resid.shape[1]
    for j, part in enumerate(parts):
        full[j * HD : (j + 1) * HD] = part[...]
    total = sum(dot(weight[c], full[c * width : (c + 1) * width, :]) for c in range(weight.shape[0]))
    out[:, :half] = total[:, :half]
    out[:, half:] = total[:, half:] + resid[...]


def project_rows(weight, resid, parts, after):
    depth, count = weight.shape[1], parts[0].shape[1]
    return call(
        project_rows_kernel,
        [shape((depth, count))],
        arrays=(weight, resid, *parts),
        scratch=[pltpu.VMEM((len(parts) * HD, count), bf16)],
        limit=26,
        estimate=cost(1e3, 1e3),
        after=after,
        mark=True,
    )


def place_attend_kernel(order, low, high, small, out, bias, hidden, *vectors):
    deep = out.shape[1] // PIECES
    width = out.shape[2]
    depth = out.shape[1]
    for r in range(PIECES):
        src = (low, high)[r // (PIECES // 2)]
        of = slice(r % (PIECES // 2) * deep, r % (PIECES // 2) * deep + deep)
        at = pl.ds(pl.multiple_of(order[r] * deep, deep), deep)
        for c in range(3):
            out[c, at, :] = src[of, c * width : (c + 1) * width]
    for j in range(2):
        bias[j : j + 1] = small[4 + j : 5 + j, depth:]
    for j in range(hidden.shape[1] // width):
        hidden[:, j * width : (j + 1) * width] = small[j : j + 1, depth:]
    for j, vector in enumerate(vectors):
        vector[...] = small[j : j + 1, :depth]


def place_attend(order, low, high, small, depth, width, units, after):
    return call(
        place_attend_kernel,
        [pltpu.HBM((3, depth, width), f32), shape((2, width)), shape((1, units)), *[shape((1, depth))] * 6],
        scalars=(order,),
        arrays=(low, high, small),
        limit=8,
        after=after,
        estimate=cost(1e3, 1e3),
    )


def add_rows_kernel(me, mine, got, out):
    out[...] = (mine[...] + got[...]).T.astype(bf16)


def add_rows(me, mine, got, after):
    depth, count = mine.shape
    blk = count // 4
    last = lambda i, me: jnp.where(i // 2 == me[0], 2, 0) + i % 2
    first = lambda i, me: jnp.where(i // 2 == me[0], 0, 2) + i % 2
    turned = lambda at: pl.BlockSpec((depth, blk), lambda i, me: (0, at(i, me)))
    return call(
        add_rows_kernel,
        [pltpu.HBM((count, depth), bf16)],
        scalars=(me,),
        arrays=(mine, got),
        grid=(4,),
        in_specs=[turned(last), turned(first)],
        out_specs=[pl.BlockSpec((blk, depth), lambda i, me: (i, 0))],
        limit=12,
        after=after,
        estimate=cost(1e3, 1e3),
        mark=True,
    )


def join_kernel(me, own, other, out):
    mine = pl.program_id(0) == me[0]

    @pl.when(mine)
    def _():
        out[...] = own[...].astype(bf16)

    @pl.when(jnp.logical_not(mine))
    def _():
        out[...] = other[...].astype(bf16)


def join(me, own, other, after=()):
    half, depth = own.shape
    block = pl.BlockSpec((half, depth), lambda i, me: (0, 0))
    return call(
        join_kernel,
        [pltpu.HBM((2 * half, depth), bf16)],
        scalars=(me,),
        arrays=(own, other),
        grid=(2,),
        in_specs=[block, block],
        out_specs=[pl.BlockSpec((half, depth), lambda i, me: (i, 0))],
        estimate=cost(1e3, 1e3),
        limit=14,
        after=after,
        mark=True,
    )


def small_kernel(small, got, out):
    units, lanes = small.shape[1] // 2, out.shape[1]
    depth = lanes * 2 // 3
    wide = lanes - depth
    out[...] = jnp.zeros(out.shape, f32)
    out[0:6, :depth] = small[0:6, :depth] + got[0:6, :depth]
    hidden = small[6:7, :units] + got[6:7, units:]
    for j in range(units // wide):
        out[j : j + 1, depth:] = hidden[:, j * wide : (j + 1) * wide]


def small_rows(small, got, lanes, after):
    return call(
        small_kernel, [shape((8, lanes))], arrays=(small, got), after=after, estimate=cost(1e3, 1e3)
    )[0]


def swap(v):
    return lax.ppermute(v, "mp", [(0, 1), (1, 0)])


MAIN = ((1, 2, 4, 8), (2, 1, 8, 4))
SIDE = ((8, 4, 1, 2), (4, 8, 1, 2))
ATTEND = ((1, 2, 4, 8), (2, 1, 4, 8))


def masks(bits):
    return [sum(bits[3 - b] for b in range(4) if r >> b & 1) for r in range(PIECES)]


def piece_order(groups, which=0):
    table = jnp.array([sum((masks(group[core]) for group in groups), []) for core in (0, 1)], jnp.int32)
    core = lax.axis_index("mp")
    return lax.axis_index("dp").astype(jnp.int32) ^ table[1 - core if which else core]


def across(group, v, position):
    pairs = [
        (2 * d + core, 2 * (d ^ masks(group[core])[position]) + core)
        for d in range(PIECES)
        for core in range(2)
    ]
    return lax.ppermute(v, ("dp", "mp"), pairs)


def stage(body, outs, arrays, after, in_specs=None):
    *outs, mark = call(
        body, [shape(o) for o in outs], arrays=arrays, in_specs=in_specs, after=after, mark=True, limit=12, estimate=cost(1e3, 1e3)
    )
    return outs, (mark,)


def block_of(a, rows, at):
    return pl.BlockSpec((rows, a.shape[1]), lambda *_: (at, 0))


def sum_kernel(counts, extra, *refs):
    arrays, outs = refs[: sum(counts) + (extra and counts[0])], refs[sum(counts) + (extra and counts[0]) :]
    at = 0
    for count, out in zip(counts, outs):
        rows = arrays[at].shape[0]
        out[:rows] = sum(a[...] for a in arrays[at : at + count])
        at += count
    if extra:
        outs[0][rows:] = sum(a[...] for a in arrays[at:])


def halve(chains, after, extra=0, last=False):
    arrays, specs, outs = [], [], []
    for chain in chains:
        rows = chain[0].shape[0] - extra
        size = rows // (PIECES // 2) if last else rows >> (len(chain) - 1)
        specs += [block_of(a, size, 0 if last else 1) for a in chain]
        arrays += chain
        outs.append((size + extra, chain[0].shape[1]))
    if extra:
        specs += [block_of(a, extra, (a.shape[0] - extra) // extra) for a in chains[0]]
        arrays += chains[0]
    return stage(functools.partial(sum_kernel, [len(c) for c in chains], extra), outs, arrays, after, specs)


def quarter_kernel(many, *refs):
    arrays, (own, *parts, small) = refs[: 2 * many], refs[2 * many :]
    size = own.shape[0]
    total = lambda at: sum(a[at] for a in arrays[:many])
    own[...] = total(slice(0, size))
    sums = sum(a[...] for a in arrays[many:])
    small[...] = sums
    for j, part in enumerate(parts):
        part[:size] = total(slice((j + 1) * size, (j + 2) * size))
        part[size:] = sums


def quarters(chain, after, extra):
    rows, lanes = chain[0].shape[0] - extra, chain[0].shape[1]
    size = rows // (PIECES // 2)
    specs = [block_of(a, 4 * size, 0) for a in chain]
    specs += [block_of(a, extra, (a.shape[0] - extra) // extra) for a in chain]
    outs = [(size, lanes), *[(size + extra, lanes)] * 3, (extra, lanes)]
    return stage(functools.partial(quarter_kernel, len(chain)), outs, [*chain, *chain], after, specs)


def piece_kernel(own, a, b, c, small, out, sums):
    size = own.shape[0]
    out[...] = own[...] + a[:size] + b[:size] + c[:size]
    sums[...] = small[...] + a[size:] + b[size:] + c[size:]


def four_kernel(*refs):
    *parts, out = refs
    size = parts[0].shape[0]
    for j, part in enumerate(parts):
        out[j * size : (j + 1) * size] = part[...]


def stack_kernel(*refs):
    count = len(refs) // 3
    for low, high, out in zip(refs[:count], refs[count : 2 * count], refs[2 * count :]):
        rows = low.shape[0]
        out[:rows] = low[...]
        out[rows:] = high[...]


def stack(lows, highs, after):
    outs = [(2 * low.shape[0], low.shape[1]) for low in lows]
    return stage(stack_kernel, outs, [*lows, *highs], after)


def local(
    tokens, seq_starts, seq_lengths, attend_weight, attend_bias, output_weight, output_bias, first_gain, first_shift,
    expand_weight, expand_bias, reduce_weight, reduce_bias, second_gain, second_shift, cotangent,
):
    slots = seq_starts.shape[1]
    units, width, depth = expand_weight.shape[1], output_weight.shape[0], tokens.shape[1]
    by_pieces = lax.axis_size("dp") == PIECES
    me = lax.axis_index("mp").astype(jnp.int32)[None]
    order = order_other = order_p = jnp.arange(2 * PIECES, dtype=jnp.int32) % PIECES
    if by_pieces:
        order, order_other = piece_order((MAIN, SIDE)), piece_order((MAIN, SIDE), 1)
        order_p = piece_order((ATTEND,))
    spans = jnp.concatenate([seq_starts, seq_starts + seq_lengths])
    spans = jnp.pad(spans, ((0, 6), (0, 128 - slots)))
    eb_own = expand_bias[None, :]
    wide_rcv = swap(widen(output_weight, expand_weight, reduce_weight, eb_own))
    vectors = (output_bias, first_gain, first_shift, reduce_bias, second_gain, second_shift)
    vectors = [v[None, :] for v in vectors]

    att_other, att_own, logs, qt, kaug, seg = attend_forward(me, tokens, attend_weight, attend_bias, spans, slots)
    att_rcv = swap(att_other)
    weights = [hbm(w) for w in (output_weight, expand_weight, reduce_weight)]
    weights = (*weights, eb_own, wide_rcv, *vectors)
    (layer_own, resid, ga_own, ga_other, act, gh, nlt, grt, gbt, att, small, keep, send) = middle(
        order_other, me, att_own, att_rcv, weights, tokens, cotangent, spans
    )
    send_rcv, keep_rcv, ga_rcv = swap(send), swap(keep), swap(ga_other)
    small_rcv, layer_rcv = swap(small), swap(layer_own)
    kt, vaug, tokt, mark = prepare(me, tokens, attend_weight, attend_bias, (small,))
    send, mark = own_grads(PIECES // 2, order, grt, nlt, gbt, act, gh, att, send_rcv, (mark,))
    keep, after = own_grads(0, order, grt, nlt, gbt, act, gh, att, keep_rcv, mark)

    heads = []

    def backward(after):
        *head, mark = attend_backward(
            len(heads), qt, kt, kaug, vaug, seg, logs, att_other, att_own, ga_rcv, ga_own, after
        )
        heads.append(head)
        return (mark,)

    count = width // HD
    after = backward(after)
    small = small_rows(small, small_rcv, 3 * width, after)
    after = (small,)

    def project(after):
        parts = [head[c] for c in range(3) for head in heads]
        keep_p, send_p, mark = project_grad(order_p, tokt, small, parts, after)
        return keep_p, send_p, parts, (mark,)

    if by_pieces:

        def mid(pair, position):
            return [across(group, v, position) for group, v in zip((MAIN, SIDE), pair)]

        def mid_halve(after, last=False):
            return halve([list(chain) for chain in zip(*got)], after, last=last)

        att = functools.partial(across, ATTEND)
        got = [keep, mid(send, 8)]
        layer_out, mark = join(me, layer_own, layer_rcv, after)
        lead, after = mid_halve((mark,))
        got.append(mid(lead, 4))
        after = backward(after)
        lead, after = mid_halve(after)
        got.append(mid(lead, 2))
        after = backward(after)
        lead, after = mid_halve(after)
        got.append(mid(lead, 1))
        after = backward(after)
        own, after = mid_halve(after, last=True)
        come = mid(own, 1)
        keep_p, send_p, parts, after = project(after)
        got_p = [keep_p, att(send_p, 8)]
        rows, mark = project_rows(attend_weight, resid, parts, after)
        rows_rcv = swap(rows)
        (lead,), after = halve([got_p], (mark,), 8)
        got_p.append(att(lead, 4))
        own, after = stack(own, come, after)
        come = mid(own, 2)
        (own_p, *parts_p, small), after = quarters(got_p, after, 8)
        come_p = [att(part, j + 1) for j, part in enumerate(parts_p)]
        grad_tokens, mark = add_rows(me, rows, rows_rcv, after)
        own, after = stack(own, come, (mark,))
        come = mid(own, 4)
        outs = [own_p.shape, small.shape]
        (own_p, totals), after = stage(piece_kernel, outs, [own_p, *come_p, small], after)
        come_p = [att(own_p, j + 1) for j in range(3)]
        low, after = stack(own, come, after)
        high = mid(low, 8)
        outs = [(4 * own_p.shape[0], own_p.shape[1])]
        (own_p,), after = stage(four_kernel, outs, [own_p, *come_p], after)
        come_p = att(own_p, 4)
        (low_p,), after = stack([own_p], [come_p], after)
        high_p = att(low_p, 8)
    else:
        while len(heads) < count:
            after = backward(after)
        keep_p, send_p, parts, after = project(after)
        rows, mark = project_rows(attend_weight, resid, parts, after)
        grad_tokens, mark = add_rows(me, rows, swap(rows), (mark,))
        low, high, low_p, high_p = lax.psum((keep, send, keep_p, send_p), "dp")
        layer_out, mark = join(me, layer_own, layer_rcv, (mark,))
        totals, after = low_p[-8:], (mark,)
    grad_reduce, grad_expand, grad_output, mark = place_grads(order, *zip(low, high), units, width, after)
    grad_attend, grad_bias, grad_hidden, *vectors = place_attend(
        order_p, low_p, high_p, totals, depth, width, units, (mark,)
    )
    vectors = [v.reshape(depth) for v in vectors]
    return (
        layer_out,
        grad_tokens,
        grad_attend,
        grad_bias,
        grad_output,
        vectors[5],
        vectors[3],
        vectors[4],
        grad_expand,
        grad_hidden.reshape(units),
        grad_reduce,
        vectors[2],
        vectors[0],
        vectors[1],
    )


def solution(mesh):
    return jax.shard_map(
        local,
        mesh=mesh,
        in_specs=(
            P("dp", None),
            P("dp", None),
            P("dp", None),
            P(None, None, "mp"),
            P(None, "mp"),
            P("mp", None),
            P(),
            P(),
            P(),
            P(None, "mp"),
            P("mp"),
            P("mp", None),
            P(),
            P(),
            P(),
            P("dp", None),
        ),
        out_specs=(
            P("dp", None),
            P("dp", None),
            P(None, None, "mp"),
            P(None, "mp"),
            P("mp", None),
            P(),
            P(),
            P(),
            P(None, "mp"),
            P("mp"),
            P("mp", None),
            P(),
            P(),
            P(),
        ),
        check_vma=False,
    )
```
